32 devices in a mesh: rows: 8 (over y, x, core), labels: 4 (over z).
Axes of the slice: x: 2, y: 2, z: 4, core: 2. Of those that a mesh axis runs over, the one named last changes fastest.
Arguments:
- points: bfloat16 [4096, 1024], P('rows'), may hold values from -6 to 6
- targets: bfloat16 [4096, 21504], P('rows', 'labels'), may hold values from -6 to 6
- coeffs: float32 [4096, 21504], P('rows', 'labels'), may hold values from -6 to 6
- block_ids: int32 [2, 512], replicated, may hold values from 0 to 4095, as said below
- inverses: float32 [2, 512, 512], replicated, as said below
Outputs:
- new_coeffs: float32 [4096, 21504], P('rows', 'labels')
The draws below stay inside these ranges and needn't reach their ends.
Inputs may be any that keep to these rules, and one draw needn't show every extreme that they name: `block_ids`: the 512 ids of one block are distinct; the two blocks may share ids. Each inverses[b] is symmetric with a positive diagonal.
All inputs are finite; a program needn't handle non-finite values.
Results may differ from the reference program's by a relative error of at most 0.0029.
Values may be sent and summed in bfloat16 or wider, within the bound.
No kernel may reach another device: no remote copies, remote signals or barrier semaphores. Data moves between devices by JAX's collectives and lax.ppermute only.
A program may use at most 128 MiB of HBM per device.

```python
import jax
import jax.numpy as jnp
from jax import lax

FEAT = 1024
LABELS = 21504
BLOCK = 512
NPTS = 4096


def draw_block_ids(key, part):
    quarter = NPTS // 4
    half_block = BLOCK // 2
    blocks_out = []
    for blk in range(2):
        sub_key = jax.random.fold_in(key, 11 + blk)
        key_one, key_two, key_three = jax.random.split(sub_key, 3)
        which = jax.random.randint(key_one, (), 0, 4)
        clustered = jax.random.permutation(key_two, quarter)[:half_block] + which * quarter
        spread = (jax.random.permutation(key_three, NPTS - quarter)[:BLOCK - half_block] + (which + 1) * quarter) % NPTS
        blocks_out.append(jnp.concatenate([clustered, spread]).astype(jnp.int32))
    return jnp.stack(blocks_out).astype(jnp.int32)


def draw_inverses(key, part):
    key_one, key_two = jax.random.split(jax.random.fold_in(key, 5))
    off_scale = 0.3
    diag_vals = jax.random.uniform(key_two, (2, BLOCK), jnp.float32, 0.5, 1.0)
    base = jax.random.normal(key_one, (2, BLOCK, BLOCK), jnp.float32) * (off_scale / BLOCK ** 0.5)
    symmetric = (base + jnp.swapaxes(base, 1, 2)) * 0.7071067811865476
    eye_mat = jnp.eye(BLOCK, dtype=jnp.float32)
    return (symmetric * (1.0 - eye_mat) + eye_mat[None] * diag_vals[:, :, None]).astype(jnp.float32)


def shard_levels(rng, shape, shards, least, largest):
    loudness, own = 1.0, jax.random.fold_in(rng, 6)
    for dim, parts in shards:
        heights = jnp.exp(jax.random.uniform(jax.random.fold_in(own, dim), (parts,), jnp.float32, least / len(shards), largest / len(shards)))
        loudness = loudness * jnp.repeat(heights, shape[dim] // parts).reshape([-1 if axis == dim else 1 for axis in range(len(shape))])
    return loudness


def bell_draw(key, shape, scale, reach, cuts=(), held_as=jnp.bfloat16):
    drawn = jax.random.normal(key, shape, jnp.float32) * scale
    if len(cuts) > 0:
        drawn = shard_levels(key, shape, cuts, -0.22, 0.18) * drawn
    return jnp.clip(drawn, min=-reach, max=reach).astype(held_as)


def setup_inputs(seed: int = 0) -> dict:
    keys = jax.random.split(jax.random.key(seed), 6)
    return {
        "points": bell_draw(keys[0], (NPTS, FEAT), 1.0, 6.0, ((0, 8),)),
        "targets": bell_draw(keys[1], (NPTS, LABELS), 1.0, 6.0, ((0, 8), (1, 4))),
        "coeffs": bell_draw(keys[2], (NPTS, LABELS), 1.0, 6.0, ((0, 8), (1, 4)), jnp.float32),
        "block_ids": draw_block_ids(jax.random.fold_in(keys[5], 71), 0),
        "inverses": draw_inverses(jax.random.fold_in(keys[5], 71), 0),
    }


ridge_weight = 0.5


def kernel_tile(left, right):
    inner_prod = lax.dot_general(left, right, (((1,), (1,)), ((), ())), preferred_element_type=jnp.float32)
    left_sq = jnp.sum(jnp.square(left.astype(jnp.float32)), axis=1)
    right_sq = jnp.sum(jnp.square(right.astype(jnp.float32)), axis=1)
    sq_dist = jnp.maximum(left_sq[:, None] + right_sq[None, :] - 2.0 * inner_prod, 0.0)
    return jnp.exp(-(2.0 / left.shape[1]) * sq_dist).astype(jnp.bfloat16)


def reference(points, targets, coeffs, block_ids, inverses):
    current = coeffs
    for blk in range(2):
        point_ids = block_ids[blk].astype(jnp.int32)
        block_pts = points[point_ids]
        ktile = kernel_tile(points, block_pts)
        c_low = current.astype(jnp.bfloat16)
        product = lax.dot_general(ktile, c_low, (((0,), (0,)), ((), ())), preferred_element_type=jnp.float32)
        resid = targets[point_ids].astype(jnp.float32) - product - ridge_weight * current[point_ids]
        update = jnp.dot(inverses[blk], resid, precision=lax.Precision.HIGHEST, preferred_element_type=jnp.float32)
        current = current.at[point_ids].add(update)
    return current
```

```python
import jax
import jax.numpy as jnp
from jax import lax
from jax.sharding import PartitionSpec as P

ridge_weight = 0.5
bf16 = jnp.bfloat16
f32 = jnp.float32


def dot_nn(a, b, **kw):
    return lax.dot_general(a, b, (((1,), (0,)), ((), ())), preferred_element_type=f32, **kw)


def dot_nt(a, b, **kw):
    return lax.dot_general(a, b, (((1,), (1,)), ((), ())), preferred_element_type=f32, **kw)


def square_sums(pts):
    return jnp.sum(jnp.square(pts.astype(f32)), axis=1)


def kernel_tile(left, right):
    inner_prod = dot_nt(left, right)
    sq_dist = jnp.maximum(
        square_sums(left)[:, None] + square_sums(right)[None, :] - 2.0 * inner_prod, 0.0
    )
    return jnp.exp(-(2.0 / left.shape[1]) * sq_dist).astype(bf16)


def split_bf16(x):
    high = x.astype(bf16)
    return high, (x - high.astype(f32)).astype(bf16)


def general_path(points, targets, coeffs, block_ids, inverses):
    rows_here = points.shape[0]
    first_row = lax.axis_index("rows") * rows_here
    zero_low = jnp.zeros((), bf16)
    current = coeffs
    for blk in range(2):
        local_ids = block_ids[blk] - first_row
        inside = (local_ids >= 0) & (local_ids < rows_here)
        local_rows = jnp.clip(local_ids, 0, rows_here - 1)
        picked = jnp.where(inside[:, None], points[local_rows], zero_low)
        block_pts = lax.psum(picked, "rows").astype(f32).astype(bf16)
        ktile = kernel_tile(points, block_pts)
        c_low = current.astype(bf16)
        sel_targets = jnp.where(inside[:, None], targets[local_rows].astype(f32), 0.0)
        sel_coeffs = jnp.where(inside[:, None], current[local_rows], 0.0)
        local_side = ridge_weight * sel_coeffs - sel_targets
        product = lax.dot_general(
            ktile, c_low, (((0,), (0,)), ((), ())), preferred_element_type=f32
        )
        share = lax.psum_scatter(product + local_side, "rows", scatter_dimension=0, tiled=True)
        negated = lax.all_gather(share, "rows", axis=0, tiled=True)
        update = jnp.dot(
            inverses[blk], -negated, precision=lax.Precision.HIGHEST, preferred_element_type=f32
        )
        current = current.at[local_rows].add(jnp.where(inside[:, None], update, 0.0))
    return current


def solution(mesh):
    n = mesh.shape["rows"]
    chips = n // 2
    bits = chips.bit_length() - 1
    ring = [k ^ (k >> 1) for k in range(chips)]
    place = [ring.index(k) for k in range(chips)]

    def core_perm(chip_of):
        return [(i, 2 * chip_of(i // 2, i % 2) + i % 2) for i in range(n)]

    sib_perm = [(i, i ^ 1) for i in range(n)]
    ring_perm = core_perm(
        lambda chip, core: ring[(place[chip] + (1 if core == 0 else chips - 1)) % chips]
    )

    def stage_bit(stage, core):
        return 1 << (stage if core == 0 else bits - 1 - stage)

    def to_sib(x):
        return lax.ppermute(x, "rows", sib_perm)

    def owners(ids, rows_here):
        return ids // (2 * rows_here)

    def spread_enough(block_ids, rows_here):
        total = block_ids.size
        own = owners(block_ids.reshape(total), rows_here)
        counts = [jnp.sum((own == k).astype(jnp.int32)) for k in range(chips)]
        fits = jnp.bool_(True)
        for k in range(chips):
            fits &= counts[k] >= total // (2 * chips)
        for stage in range(bits):
            cap = stage_cap(total, stage)
            for core in range(2):
                done = sum(stage_bit(s, core) for s in range(stage))
                for base in range(chips):
                    if base & done:
                        continue
                    group = [k for k in range(chips) if k & ~done == base]
                    fits &= sum(counts[k] for k in group) <= cap
        return fits

    def stage_cap(total, stage):
        return min(total, total // 2 + ((1 << stage) - 1) * (total // chips))

    def spread_path(points, targets, coeffs, block_ids, inverses):
        rows_here, feats = points.shape
        cols = coeffs.shape[1]
        half = cols // 2
        half_f = feats // 2
        me = lax.axis_index("rows")
        chip, core = me // 2, me % 2
        blk_size = block_ids.shape[1]
        total = 2 * blk_size
        piece = total // (2 * chips)
        steps = 2 * chips - 1

        ids = block_ids.reshape(total)
        own = owners(ids, rows_here)
        ids_row = ids[None, :]
        index = jnp.arange(total, dtype=jnp.int32)
        my_first = me * rows_here
        sib_first = (me ^ 1) * rows_here
        within = jnp.arange(rows_here, dtype=jnp.int32)
        pt_ids = jnp.concatenate([my_first + within, sib_first + within])
        pick = (pt_ids[:, None] == ids_row).astype(bf16)

        pts_chip = jnp.concatenate([points, to_sib(points)], axis=0)
        pts_mine = lax.dynamic_slice(pts_chip, (0, core * half_f), (2 * rows_here, half_f))
        pts_other = lax.dynamic_slice(pts_chip, (0, (1 - core) * half_f), (2 * rows_here, half_f))
        pts_local = jnp.concatenate([pts_mine, pts_other], axis=1)

        def pack_matrix(member, cap):
            flags = member.astype(jnp.int32)
            before = (index[:, None] > index[None, :]).astype(jnp.int32)
            rank = jnp.sum(before * flags[None, :], axis=1)
            slot = jnp.where(member, rank, -1)
            return (jnp.arange(cap, dtype=jnp.int32)[:, None] == slot[None, :]).astype(bf16)

        block_half = dot_nn(pick.T, pts_mine).astype(bf16)
        for stage in range(bits):
            cap = stage_cap(total, stage)
            done0 = sum(stage_bit(s, 0) for s in range(stage))
            done1 = sum(stage_bit(s, 1) for s in range(stage))
            done = jnp.where(core == 0, done0, done1)
            bit = jnp.where(core == 0, stage_bit(stage, 0), stage_bit(stage, 1))
            mine = (own & ~done) == (chip & ~done)
            theirs = (own & ~done) == ((chip ^ bit) & ~done)
            sent = dot_nn(pack_matrix(mine, cap), block_half).astype(bf16)
            got = lax.ppermute(
                sent, "rows", core_perm(lambda k, c, s=stage: k ^ stage_bit(s, c))
            )
            unpacked = lax.dot_general(
                pack_matrix(theirs, cap), got, (((0,), (0,)), ((), ())), preferred_element_type=f32
            )
            block_half = (block_half.astype(f32) + unpacked).astype(bf16)
        block_pts = jnp.concatenate([block_half, to_sib(block_half)], axis=1)

        c_low = coeffs.astype(bf16)
        mine_at, other_at = core * half, (1 - core) * half

        def cut(x, at):
            return lax.dynamic_slice(x, (0, at), (rows_here, half))

        moved = jnp.concatenate(
            [
                cut(c_low, mine_at),
                to_sib(cut(c_low, other_at)),
                cut(targets, mine_at),
                to_sib(cut(targets, other_at)),
            ],
            axis=0,
        )

        ktile = kernel_tile(pts_local, block_pts)
        against = (ktile.astype(f32) + ridge_weight * pick.astype(f32)).astype(bf16)
        left = jnp.concatenate([-against, pick], axis=0)
        cross = kernel_tile(block_pts[blk_size:], block_pts[:blk_size]).astype(f32)
        cross += ridge_weight * (ids[blk_size:, None] == ids[None, :blk_size]).astype(f32)
        exact = dict(precision=lax.Precision.HIGHEST)
        lower = -dot_nn(inverses[1], dot_nn(cross, inverses[0], **exact), **exact)
        inv_map = jnp.concatenate(
            [
                jnp.concatenate([inverses[0], jnp.zeros_like(lower)], axis=1),
                jnp.concatenate([lower, inverses[1]], axis=1),
            ],
            axis=0,
        )

        norms = square_sums(block_pts)
        bell = jnp.exp((2.0 / feats) * (jnp.min(norms) - norms))
        along = []
        for blk in range(2):
            part = slice(blk * blk_size, (blk + 1) * blk_size)
            way = jnp.sum(inverses[blk] * bell[None, part], axis=1)
            way = way * lax.rsqrt(jnp.maximum(jnp.sum(way * way), 1e-30))
            along.append(jnp.pad(way, (blk * blk_size, (1 - blk) * blk_size)))
        rows_along = dot_nn(jnp.stack(along), inv_map, **exact)
        rest_map = inv_map - sum(along[b][:, None] * rows_along[b][None, :] for b in range(2))
        map_high, map_low = split_bf16(rest_map)
        coarse, fine = split_bf16(rows_along)
        weigh = dot_nt(jnp.concatenate([coarse, fine], axis=0), left)
        weigh = weigh[:2] + weigh[2:]
        weigh = jnp.concatenate(split_bf16(weigh), axis=0)
        amount = dot_nn(weigh, moved)
        amount = amount[:2] + amount[2:]
        for stage in range(bits):
            amount = amount + lax.ppermute(
                amount, "rows", core_perm(lambda k, c, s=stage: k ^ stage_bit(s, c))
            )
        amount_sib = to_sib(amount)

        def ring_place(which):
            return sum(jnp.where(which == k, place[k], 0) for k in range(chips))

        ahead = ring_place(own) - ring_place(chip)
        ahead = jnp.where(core == 0, -ahead, ahead)
        key = (ahead + 2 * chips - 1) % chips
        key = key * total + index
        position = jnp.sum((key[None, :] < key[:, None]).astype(jnp.int32), axis=1)
        order = (index[:, None] == position[None, :]).astype(bf16)
        row_ids = jnp.sum(jnp.where(index[:, None] == position[None, :], ids_row, 0), axis=1)
        lag = jnp.sum((key // total == 0).astype(jnp.int32))

        def shares(lo, hi):
            mat = order[lo * piece : hi * piece]
            high = dot_nn(mat, map_high).astype(bf16)
            low = dot_nn(mat, map_low).astype(bf16)
            weights = (dot_nt(high, left) + dot_nt(low, left)).astype(bf16)
            return dot_nn(weights, moved)

        cuts = [0, 1, chips, 2 * chips]
        share = []
        for lo, hi in zip(cuts[:-1], cuts[1:]):
            group = shares(lo, hi)
            share += [group[k * piece : (k + 1) * piece] for k in range(hi - lo)]

        tiles = max(1, half // 128)
        first = (tiles + 1) // 2 * 128
        bands = [(0, first), (first, half)] if first < half else [(0, half)]
        arrived = [[] for _ in bands]
        final = [[None] * (steps + 1) for _ in bands]
        spot = jnp.arange(piece, dtype=jnp.int32)
        for step in range(steps + 1):
            for b, (lo, hi) in enumerate(bands):
                value = share[step][:, lo:hi]
                if step > 0:
                    source = step * piece + spot - lag
                    slots = jnp.arange(step * piece, dtype=jnp.int32)
                    shift = (source[:, None] == slots[None, :]).astype(bf16)
                    value = value + dot_nn(shift, jnp.concatenate(arrived[b], axis=0))
                final[b][step] = value
                if step < steps:
                    arrived[b].append(lax.ppermute(value.astype(bf16), "rows", ring_perm))

        start = chips - 1
        result = coeffs
        parts = []
        for step in range(start, steps + 1):
            whole = jnp.concatenate([final[b][step] for b in range(len(bands))], axis=1)
            parts.append(split_bf16(whole))
        mine = jnp.concatenate([p for part in parts for p in part], axis=0)
        theirs = jnp.concatenate([to_sib(p) for part in parts for p in part], axis=0)
        spots = jnp.concatenate(
            [row_ids[s * piece : (s + 1) * piece] for s in range(start, steps + 1) for _ in range(2)]
        )
        place_rows = ((my_first + within)[:, None] == spots[None, :]).astype(bf16)
        mine_new = dot_nn(place_rows, mine)
        theirs_new = dot_nn(place_rows, theirs)
        here = (my_first + within)[:, None] == ids_row
        for b in range(2):
            scale = jnp.sum(jnp.where(here, along[b][None, :], 0.0), axis=1)[:, None]
            mine_new = mine_new + scale * amount[b][None, :]
            theirs_new = theirs_new + scale * amount_sib[b][None, :]
        low_half = jnp.where(core == 0, mine_new, theirs_new)
        high_half = jnp.where(core == 0, theirs_new, mine_new)
        return result + jnp.concatenate([low_half, high_half], axis=1)

    def per_device(points, targets, coeffs, block_ids, inverses):
        return lax.cond(
            spread_enough(block_ids, points.shape[0]),
            spread_path,
            general_path,
            points,
            targets,
            coeffs,
            block_ids,
            inverses,
        )

    return jax.shard_map(
        per_device,
        mesh=mesh,
        in_specs=(P("rows", None), P("rows", "labels"), P("rows", "labels"), P(), P()),
        out_specs=P("rows", "labels"),
        check_vma=False,
    )
```

```python
import jax
import jax.numpy as jnp
from jax import lax
from jax.experimental import pallas as pl
from jax.experimental.pallas import tpu as pltpu
from jax.sharding import PartitionSpec as P

ridge_weight = 0.5
bf16 = jnp.bfloat16
f32 = jnp.float32
i32 = jnp.int32
whole = pl.BlockSpec(memory_space=pltpu.VMEM)


def dot_nn(a, b):
    return lax.dot_general(a, b, (((1,), (0,)), ((), ())), preferred_element_type=f32)


def dot_nt(a, b):
    return lax.dot_general(a, b, (((1,), (1,)), ((), ())), preferred_element_type=f32)


def square_sums(pts):
    return jnp.sum(jnp.square(pts.astype(f32)), axis=1, keepdims=True)


def kernel_tile(left, right):
    inner_prod = dot_nt(left, right)
    sq_dist = jnp.maximum(square_sums(left) + square_sums(right).T - 2.0 * inner_prod, 0.0)
    return jnp.exp(-(2.0 / left.shape[1]) * sq_dist).astype(bf16)


def split_bf16(x):
    high = x.astype(bf16)
    return high, (x - high.astype(f32)).astype(bf16)


def as_row(column):
    n = column.shape[0]
    return jnp.transpose(jnp.broadcast_to(column, (n, 128)))[0:1, :]


def iota(shape, dim):
    return lax.broadcasted_iota(i32, shape, dim)


def one_hot(cond):
    return jnp.where(cond, 1.0, 0.0).astype(bf16)


def params(megabytes):
    return pltpu.CompilerParams(vmem_limit_bytes=megabytes << 20)


def cost(macs, bytes_accessed):
    return pl.CostEstimate(flops=2 * macs, bytes_accessed=bytes_accessed, transcendentals=0)


def general_path(points, targets, coeffs, block_ids, inverses):
    rows_here = points.shape[0]
    first_row = lax.axis_index("rows") * rows_here
    zero_low = jnp.zeros((), bf16)
    current = coeffs
    for blk in range(2):
        local_ids = block_ids[blk] - first_row
        inside = (local_ids >= 0) & (local_ids < rows_here)
        local_rows = jnp.clip(local_ids, 0, rows_here - 1)
        picked = jnp.where(inside[:, None], points[local_rows], zero_low)
        block_pts = lax.psum(picked, "rows").astype(f32).astype(bf16)
        ktile = kernel_tile(points, block_pts)
        c_low = current.astype(bf16)
        sel_targets = jnp.where(inside[:, None], targets[local_rows].astype(f32), 0.0)
        sel_coeffs = jnp.where(inside[:, None], current[local_rows], 0.0)
        local_side = ridge_weight * sel_coeffs - sel_targets
        product = lax.dot_general(
            ktile, c_low, (((0,), (0,)), ((), ())), preferred_element_type=f32
        )
        share = lax.psum_scatter(product + local_side, "rows", scatter_dimension=0, tiled=True)
        negated = lax.all_gather(share, "rows", axis=0, tiled=True)
        update = jnp.dot(
            inverses[blk], -negated, precision=lax.Precision.HIGHEST, preferred_element_type=f32
        )
        where_to = (jnp.arange(rows_here, dtype=i32)[:, None] == local_ids[None, :]).astype(f32)
        current = current + jnp.dot(
            where_to, update, precision=lax.Precision.HIGHEST, preferred_element_type=f32
        )
    return current


def plan(me, ids_row, ids_col, rows, ring, stage_bits, caps):
    total = ids_row.shape[1]
    chips = len(ring)
    place = [ring.index(k) for k in range(chips)]
    piece = total // (2 * chips)
    bits = len(caps)
    n_final = total - (chips - 1) * piece
    step = min(256, total)
    groups = []
    for core in range(2):
        done = 0
        for stage in range(bits):
            members = {}
            for k in range(chips):
                members.setdefault(k & ~done, []).append(k)
            groups += [(m, caps[stage]) for m in members.values()]
            done |= stage_bits[core][stage]

    def body(me_ref, idr_ref, idc_ref, flag_ref, slots_ref, their_ref, spots_ref, lag_ref):
        chip, core = me_ref[0] // 2, me_ref[0] % 2
        ids = idr_ref[...].astype(f32) + 0.5
        own = jnp.floor(ids * (0.5 / rows))
        index = iota((1, total), 1)
        rank = jnp.zeros((1, total), f32)
        for r in range(0, total, step):
            own_col = jnp.floor((idc_ref[r : r + step, :].astype(f32) + 0.5) * (0.5 / rows))
            ahead = (own_col == own) & (r + iota((step, total), 0) < index)
            rank += jnp.sum(jnp.where(ahead, 1.0, 0.0), axis=0, keepdims=True)

        def count(which):
            return jnp.sum(jnp.where(own == which, 1.0, 0.0), axis=1, keepdims=True)

        def slots(listed):
            slot = jnp.full((1, total), -1.0, f32)
            before = jnp.zeros((1, 1), f32)
            for which in listed:
                which = which.astype(f32)
                slot = jnp.where(own == which, before + rank, slot)
                before = before + count(which)
            return slot

        counts = [count(float(k)) for k in range(chips)]
        slack = counts[0] - piece
        for k in range(1, chips):
            slack = jnp.minimum(slack, counts[k] - piece)
        for members, cap in groups:
            slack = jnp.minimum(slack, cap - sum(counts[k] for k in members))
        flag_ref[0] = (jnp.max(slack) >= 0.0).astype(i32)

        slots_ref[...] = jnp.zeros(slots_ref.shape, i32)
        group = [0]
        theirs = []
        for stage in range(bits):
            bit = jnp.where(core == 0, stage_bits[0][stage], stage_bits[1][stage])
            slots_ref[stage : stage + 1, :] = slots([chip ^ g for g in group]).astype(i32)
            theirs.append(slots([chip ^ bit ^ g for g in group]))
            group = group + [g ^ bit for g in group]
        fill = jnp.zeros((128 - bits, total), f32)
        their_ref[...] = jnp.transpose(jnp.concatenate(theirs + [fill], axis=0)).astype(i32)

        def lookup(which, table):
            out = jnp.int32(table[0])
            for k in range(1, chips):
                out = jnp.where(which == k, table[k], out)
            return out

        here = lookup(chip, place)
        way = jnp.where(core == 0, chips - 1, 1)
        listed = [lookup((here + way * (k + 1)) % chips, ring) for k in range(chips)]
        position = slots(listed)
        slots_ref[bits : bits + 1, :] = position.astype(i32)
        lag_ref[...] = jnp.broadcast_to(count(listed[0].astype(f32)), (8, 128)).astype(i32)
        pos_col = jnp.transpose(jnp.broadcast_to(position, (128, total)))[:, 0:1]
        line = ((chips - 1) * piece + iota((1, n_final), 1)).astype(f32)
        spots = jnp.sum(
            jnp.where(pos_col == line, idc_ref[...].astype(f32), 0.0), axis=0, keepdims=True
        )
        spots_ref[...] = spots.astype(i32)

    smem = pl.BlockSpec(memory_space=pltpu.SMEM)
    return pl.pallas_call(
        body,
        out_shape=[
            jax.ShapeDtypeStruct((1,), i32),
            jax.ShapeDtypeStruct((8, total), i32),
            jax.ShapeDtypeStruct((total, 128), i32),
            jax.ShapeDtypeStruct((1, n_final), i32),
            jax.ShapeDtypeStruct((8, 128), i32),
        ],
        in_specs=[smem, whole, whole],
        out_specs=[smem, whole, whole, whole, whole],
        compiler_params=params(32),
        cost_estimate=cost(1 << 20, 1 << 20),
    )(me, ids_row, ids_col)


def pick_points(me, ids_row, ids_col, slots, points, sib_points, half_f, cap):
    total, rows = ids_row.shape[1], points.shape[0]

    def body(me_ref, idc_ref, slots_ref, own_ref, sib_ref, block_ref, sent_ref):
        cols = pl.ds(pl.multiple_of(me_ref[0] % 2 * half_f, 128), half_f)
        local = iota((total, rows), 1)
        own = one_hot(idc_ref[...] == local + me_ref[0] * rows)
        sib = one_hot(idc_ref[...] == local + (me_ref[0] ^ 1) * rows)
        block = (dot_nn(own, own_ref[:, cols]) + dot_nn(sib, sib_ref[:, cols])).astype(bf16)
        block_ref[...] = block
        pack = one_hot(iota((cap, total), 0) == slots_ref[0:1, :])
        sent_ref[...] = dot_nn(pack, block).astype(bf16)

    return pl.pallas_call(
        body,
        out_shape=[
            jax.ShapeDtypeStruct((total, half_f), bf16),
            jax.ShapeDtypeStruct((cap, half_f), bf16),
        ],
        in_specs=[pl.BlockSpec(memory_space=pltpu.SMEM)] + [whole] * 4,
        out_specs=[whole] * 2,
        compiler_params=params(32),
        cost_estimate=cost(2 * total * rows * half_f, 6 << 20),
    )(me, ids_col, slots, points, sib_points)


def merge_points(block, got, slots, theirs, stage, cap_next):
    total, half_f = block.shape
    cap = got.shape[0]

    def body(block_ref, got_ref, slots_ref, their_ref, out_ref, *sent_ref):
        unpack = one_hot(their_ref[:, stage : stage + 1] == iota((total, cap), 1))
        merged = (block_ref[...].astype(f32) + dot_nn(unpack, got_ref[...])).astype(bf16)
        out_ref[...] = merged
        if sent_ref:
            pack = one_hot(iota((cap_next, total), 0) == slots_ref[stage + 1 : stage + 2, :])
            sent_ref[0][...] = dot_nn(pack, merged).astype(bf16)

    out_shape = [jax.ShapeDtypeStruct((total, half_f), bf16)]
    if cap_next:
        out_shape.append(jax.ShapeDtypeStruct((cap_next, half_f), bf16))
    return pl.pallas_call(
        body,
        out_shape=out_shape,
        in_specs=[whole] * 4,
        out_specs=[whole] * len(out_shape),
        compiler_params=params(32),
        cost_estimate=cost(2 * total * cap * half_f, 6 << 20),
    )(block, got, slots, theirs)


def cut_columns(me, coeffs, targets, width, blk):
    rows = coeffs.shape[0]

    def body(me_ref, mine_ref, other_ref, target_ref, c_mine_ref, c_other_ref, t_other_ref):
        c_mine_ref[...] = mine_ref[...].astype(bf16)
        c_other_ref[...] = other_ref[...].astype(bf16)
        t_other_ref[...] = target_ref[...]

    mine = pl.BlockSpec((rows, blk), lambda j, me_ref: (0, me_ref[0] % 2 * (width // blk) + j))
    other = pl.BlockSpec((rows, blk), lambda j, me_ref: (0, (1 - me_ref[0] % 2) * (width // blk) + j))
    plain = pl.BlockSpec((rows, blk), lambda j, me_ref: (0, j))
    return pl.pallas_call(
        body,
        out_shape=[jax.ShapeDtypeStruct((rows, width), bf16)] * 3,
        grid_spec=pltpu.PrefetchScalarGridSpec(
            num_scalar_prefetch=1,
            grid=(width // blk,),
            in_specs=[mine, other, other],
            out_specs=[plain] * 3,
        ),
        compiler_params=params(32),
        cost_estimate=cost(0, rows * width * 16),
    )(me, coeffs, coeffs, targets)


def build_maps(me, points, sib_points, q_half, q_other, inverses, ids_row, ids_col):
    rows, feats = points.shape
    half_f = feats // 2
    total = ids_row.shape[1]
    blk = total // 2
    step = min(256, rows, blk)
    scale = -(2.0 / feats)

    def body(
        me_ref, own_ref, sib_ref, qh_ref, qo_ref, inv_ref, idr_ref, idc_ref,
        left_ref, rest_ref, rows_ref, along_ref, norm_ref,
    ):
        mine = pl.ds(pl.multiple_of(me_ref[0] % 2 * half_f, 128), half_f)
        other = pl.ds(pl.multiple_of((1 - me_ref[0] % 2) * half_f, 128), half_f)
        for r in range(0, total, step):
            part = square_sums(qh_ref[r : r + step, :]) + square_sums(qo_ref[r : r + step, :])
            norm_ref[r : r + step, :] = jnp.broadcast_to(part, (step, 128))
        norms = jnp.transpose(norm_ref[...])[0:1, :]

        def values(a, b, a_sq, b_sq, same):
            inner = dot_nt(a[0], b[0]) + dot_nt(a[1], b[1])
            sq_dist = jnp.maximum(a_sq + b_sq - 2.0 * inner, 0.0)
            k = jnp.exp(scale * sq_dist).astype(bf16).astype(f32)
            return (k + jnp.where(same, ridge_weight, 0.0)).astype(bf16)

        cross = []
        for r in range(blk, total, step):
            at = slice(r, r + step)
            cross.append(
                values(
                    (qh_ref[at, :], qo_ref[at, :]),
                    (qh_ref[:blk, :], qo_ref[:blk, :]),
                    norm_ref[at, 0:1],
                    norms[:, :blk],
                    idc_ref[at, :] == idr_ref[:, :blk],
                )
            )
        cross = jnp.concatenate(cross, axis=0)
        inv0, inv1 = inv_ref[0], inv_ref[1]
        high0, low0 = split_bf16(inv0)
        high1, low1 = split_bf16(inv1)
        high, low = split_bf16(dot_nn(cross, high0) + dot_nn(cross, low0))
        lower = -(dot_nn(high1, high) + dot_nn(high1, low) + dot_nn(low1, high))

        bell = jnp.exp(-scale * (jnp.min(norms) - norms))

        def direction(inv, weights):
            way = jnp.sum(inv * weights, axis=1, keepdims=True)
            return way * lax.rsqrt(jnp.maximum(jnp.sum(way * way), 1e-30))

        way0 = direction(inv0, bell[:, :blk])
        way1 = direction(inv1, bell[:, blk:])
        row00 = jnp.sum(way0 * inv0, axis=0, keepdims=True)
        row10 = jnp.sum(way1 * lower, axis=0, keepdims=True)
        row11 = jnp.sum(way1 * inv1, axis=0, keepdims=True)
        rest_ref[:blk, :blk] = (inv0 - way0 * row00).astype(bf16)
        rest_ref[:blk, blk:] = jnp.zeros((blk, blk), bf16)
        rest_ref[blk:, :blk] = (lower - way1 * row10).astype(bf16)
        rest_ref[blk:, blk:] = (inv1 - way1 * row11).astype(bf16)
        rows_ref[...] = jnp.zeros((8, total), f32)
        rows_ref[0:1, :blk] = row00
        rows_ref[1:2, :blk] = row10
        rows_ref[1:2, blk:] = row11
        along_ref[...] = jnp.zeros((8, total), f32)
        along_ref[0:1, :blk] = as_row(way0)
        along_ref[1:2, blk:] = as_row(way1)

        for which, ref in enumerate((own_ref, sib_ref)):
            for r in range(0, rows, step):
                at = slice(r, r + step)
                a = (ref[at, mine], ref[at, other])
                spot = (me_ref[0] ^ which) * rows + r + iota((step, total), 0)
                left_ref[which * rows + r : which * rows + r + step, :] = -values(
                    a,
                    (qh_ref[...], qo_ref[...]),
                    square_sums(a[0]) + square_sums(a[1]),
                    norms,
                    spot == idr_ref[...],
                )

    return pl.pallas_call(
        body,
        out_shape=[
            jax.ShapeDtypeStruct((2 * rows, total), bf16),
            jax.ShapeDtypeStruct((total, total), bf16),
            jax.ShapeDtypeStruct((8, total), f32),
            jax.ShapeDtypeStruct((8, total), f32),
        ],
        in_specs=[pl.BlockSpec(memory_space=pltpu.SMEM)] + [whole] * 7,
        out_specs=[whole] * 4,
        scratch_shapes=[pltpu.VMEM((total, 128), f32)],
        compiler_params=params(48),
        cost_estimate=cost(4 * rows * total * feats, 12 << 20),
    )(me, points, sib_points, q_half, q_other, inverses, ids_row, ids_col)


def map_shares(me, lo, count, extra, slots, pos_row, rest, left, ids_row, rows_along, mine, sib, targets, t_sib, blk):
    rows, width = mine.shape
    total = ids_row.shape[1]
    height = count + (32 if extra else 0)

    def body(*refs):
        me_ref, pos_ref, rest_ref, left_ref, idr_ref, along_ref = refs[:6]
        c_ref, cs_ref, t_ref, ts_ref, out_ref = refs[6:11]
        weights = refs[-1]

        @pl.when(pl.program_id(0) == 0)
        def _():
            sel = one_hot(pos_ref[pos_row : pos_row + 1, :] == lo + iota((count, total), 0))
            moved = dot_nn(sel, rest_ref[...]).astype(bf16)
            if extra:
                padded = jnp.concatenate([along_ref[...], jnp.zeros((8, total), f32)], axis=0)
                moved = jnp.concatenate([moved, *split_bf16(padded)], axis=0)
            for k in range(3):
                if k == 0:
                    at, other = slice(0, 2 * rows), left_ref[...]
                else:
                    at = slice((1 + k) * rows, (2 + k) * rows)
                    spot = (me_ref[0] ^ (k - 1)) * rows + iota((rows, total), 0)
                    other = one_hot(spot == idr_ref[...])
                mapped = dot_nt(moved, other)
                weights[:count, at] = mapped[:count].astype(bf16)
                if extra:
                    both = mapped[count : count + 16] + mapped[count + 16 :]
                    weights[count : count + 16, at], weights[count + 16 :, at] = split_bf16(both)

        out = dot_nn(weights[:, :rows], c_ref[...])
        out += dot_nn(weights[:, rows : 2 * rows], cs_ref[...])
        out += dot_nn(weights[:, 2 * rows : 3 * rows], t_ref[...])
        out += dot_nn(weights[:, 3 * rows :], ts_ref[...])
        out_ref[...] = out[:count]
        if extra:
            refs[11][...] = out[count : count + 8] + out[count + 16 : count + 24]

    def fixed(shape):
        return pl.BlockSpec(shape, lambda j, me_ref: (0, 0))

    plain = pl.BlockSpec((rows, blk), lambda j, me_ref: (0, j))
    mine_t = pl.BlockSpec((rows, blk), lambda j, me_ref: (0, me_ref[0] % 2 * (width // blk) + j))
    out_specs = [pl.BlockSpec((count, blk), lambda j, me_ref: (0, j))]
    out_shape = [jax.ShapeDtypeStruct((count, width), f32)]
    if extra:
        out_specs.append(pl.BlockSpec((8, blk), lambda j, me_ref: (0, j)))
        out_shape.append(jax.ShapeDtypeStruct((8, width), f32))
    return pl.pallas_call(
        body,
        out_shape=out_shape,
        grid_spec=pltpu.PrefetchScalarGridSpec(
            num_scalar_prefetch=1,
            grid=(width // blk,),
            in_specs=[
                whole,
                whole,
                whole,
                whole,
                whole,
                plain,
                plain,
                mine_t,
                plain,
            ],
            out_specs=out_specs,
            scratch_shapes=[pltpu.VMEM((height, 4 * rows), bf16)],
        ),
        compiler_params=params(48),
        cost_estimate=cost(count * 4 * rows * (width + total), rows * width * 8 + (6 << 20)),
    )(me, slots, rest, left, ids_row, rows_along, mine, sib, targets, t_sib)


def add_updates(me, coeffs, spots, ids_row, along, amount, amount_sib, mine, sib, width, blk):
    rows, cols = coeffs.shape
    total = ids_row.shape[1]
    n = len(mine)
    piece = mine[0].shape[0]

    def body(me_ref, c_ref, spots_ref, idr_ref, along_ref, am_ref, as_ref, *refs):
        mine_refs, sib_refs = refs[:n], refs[n : 2 * n]
        out_ref, sel, scale = refs[2 * n :]
        j = pl.program_id(0)

        @pl.when(j == 0)
        def _():
            here = me_ref[0] * rows + iota((rows, n * piece), 0)
            sel[...] = one_hot(here == spots_ref[...])
            at = me_ref[0] * rows + iota((rows, total), 0) == idr_ref[...]
            for b in range(2):
                scale[:, b : b + 1] = jnp.sum(
                    jnp.where(at, along_ref[b : b + 1, :], 0.0), axis=1, keepdims=True
                )

        def finish(amount_ref, parts):
            out = dot_nn(sel[...], jnp.concatenate([ref[...] for ref in parts], axis=0))
            for b in range(2):
                out += scale[:, b : b + 1] * amount_ref[b : b + 1, :]
            out_ref[...] = c_ref[...] + out

        first = me_ref[0] % 2 * (width // blk)
        inside = (j >= first) & (j < first + width // blk)
        pl.when(inside)(lambda: finish(am_ref, mine_refs))
        pl.when(jnp.logical_not(inside))(lambda: finish(as_ref, sib_refs))

    def fixed(shape):
        return pl.BlockSpec(shape, lambda j, me_ref: (0, 0))

    def side(height, k):
        def place(j, me_ref):
            first = (me_ref[0] ^ k) % 2 * (width // blk)
            return 0, jnp.clip(j - first, 0, width // blk - 1)

        return pl.BlockSpec((height, blk), place)

    plain = pl.BlockSpec((rows, blk), lambda j, me_ref: (0, j))
    return pl.pallas_call(
        body,
        out_shape=jax.ShapeDtypeStruct((rows, cols), f32),
        grid_spec=pltpu.PrefetchScalarGridSpec(
            num_scalar_prefetch=1,
            grid=(cols // blk,),
            in_specs=[
                plain,
                fixed((1, n * piece)),
                fixed((1, total)),
                fixed((8, total)),
                side(8, 0),
                side(8, 1),
                *[side(piece, 0)] * n,
                *[side(piece, 1)] * n,
            ],
            out_specs=plain,
            scratch_shapes=[pltpu.VMEM((rows, n * piece), bf16), pltpu.VMEM((rows, 128), f32)],
        ),
        compiler_params=params(48),
        cost_estimate=cost(rows * n * piece * cols, rows * cols * 12),
    )(me, coeffs, spots, ids_row, along, amount, amount_sib, *mine, *sib)


def solution(mesh):
    n = mesh.shape["rows"]
    chips = n // 2
    bits = chips.bit_length() - 1
    ring = [k ^ (k >> 1) for k in range(chips)]
    place = [ring.index(k) for k in range(chips)]

    def core_perm(chip_of):
        return [(i, 2 * chip_of(i // 2, i % 2) + i % 2) for i in range(n)]

    sib_perm = [(i, i ^ 1) for i in range(n)]
    ring_perm = core_perm(
        lambda chip, core: ring[(place[chip] + (1 if core == 0 else chips - 1)) % chips]
    )

    group_cuts = [0, 2, chips + 1, 2 * chips]

    def stage_bit(stage, core):
        return 1 << (stage if core == 0 else bits - 1 - stage)

    def to_sib(x):
        return lax.ppermute(x, "rows", sib_perm)

    def stage_cap(total, stage):
        return min(total, total // 2 + ((1 << stage) - 1) * (total // chips))

    def spread_path(points, targets, coeffs, block_ids, inverses, pts_sib, me, slots, theirs, spots, lag):
        rows_here, feats = points.shape
        cols = coeffs.shape[1]
        half_f = feats // 2
        extra_cols = -cols % 256
        if extra_cols:
            targets = jnp.pad(targets, ((0, 0), (0, extra_cols)))
            coeffs = jnp.pad(coeffs, ((0, 0), (0, extra_cols)))
        width = (cols + extra_cols) // 2
        narrow = 128 * max(d for d in (1, 2, 3, 4) if width // 128 % d == 0)
        wide = 128 * max(d for d in range(1, 9) if width // 128 % d == 0)
        total = block_ids.size
        piece = total // (2 * chips)
        steps = 2 * chips - 1
        ids_row, ids_col = block_ids.reshape(1, total), block_ids.reshape(total, 1)

        caps = [stage_cap(total, stage) for stage in range(bits)] + [0]
        block_half, sent = pick_points(
            me, ids_row, ids_col, slots, points, pts_sib, half_f, caps[0]
        )
        for stage in range(bits):
            got = lax.ppermute(
                sent, "rows", core_perm(lambda k, c, s=stage: k ^ stage_bit(s, c))
            )
            if stage == 0:
                me_later = lax.optimization_barrier((me, sent))[0]
                c_mine, c_other, t_other = cut_columns(me_later, coeffs, targets, width, narrow)
                c_sib, t_sib = to_sib(c_other), to_sib(t_other)
            block_half, *sent = merge_points(
                block_half, got, slots, theirs, stage, caps[stage + 1]
            )
            sent = sent[0] if sent else None
        block_other = to_sib(block_half)

        left, rest, rows_along, along = build_maps(
            me, points, pts_sib, block_half, block_other, inverses, ids_row, ids_col
        )

        def shares(lo, hi, rest):
            out = map_shares(
                me, lo * piece, (hi - lo) * piece, lo == 0, slots, bits, rest, left,
                ids_row, rows_along, c_mine, c_sib, targets, t_sib, wide,
            )
            return [out[0][k * piece : (k + 1) * piece] for k in range(hi - lo)], out[1:]

        first = (width // 128 + 1) // 2 * 128
        bands = [(0, first), (first, width)] if first < width else [(0, width)]
        arrived = [[] for _ in bands]
        final = []
        line = jnp.arange(piece, dtype=i32)[:, None]
        share, (amount,) = shares(group_cuts[0], group_cuts[1], rest)
        coming = list(zip(group_cuts[1:-1], group_cuts[2:]))
        for step in range(steps + 1):
            sent = []
            for b, (lo, hi) in enumerate(bands):
                value = share[step][:, lo:hi]
                if step > 0:
                    places = jnp.arange(step * piece, dtype=i32)[None, :]
                    shift = (step * piece + line - lag[0:1, 0:1] == places).astype(bf16)
                    value = value + dot_nn(shift, jnp.concatenate(arrived[b], axis=0))
                sent.append(value.astype(bf16))
                if step < steps:
                    arrived[b].append(lax.ppermute(sent[b], "rows", ring_perm))
            if step >= chips - 1:
                final.append(jnp.concatenate(sent, axis=1))
            if coming:
                after = sent if step == 0 else [arrived[0][step - 1]]
                rest = lax.optimization_barrier((rest, *after))[0]
                share += shares(*coming.pop(0), rest)[0]

        for stage in range(bits):
            amount = amount + lax.ppermute(
                amount, "rows", core_perm(lambda k, c, s=stage: k ^ stage_bit(s, c))
            )
        amount_sib = to_sib(amount)

        final_sib = [to_sib(part) for part in final]
        out = add_updates(
            me, coeffs, spots, ids_row, along, amount, amount_sib, final, final_sib, width, narrow
        )
        return out[:, :cols] if extra_cols else out

    def per_device(points, targets, coeffs, block_ids, inverses):
        rows_here = points.shape[0]
        total = block_ids.size
        me = lax.axis_index("rows").astype(i32).reshape(1)
        pts_sib = to_sib(points)
        stage_bits = [[stage_bit(s, core) for s in range(bits)] for core in range(2)]
        caps = [stage_cap(total, s) for s in range(bits)]
        flag, *plans = plan(
            me, block_ids.reshape(1, total), block_ids.reshape(total, 1), rows_here, ring, stage_bits, caps
        )
        args = (points, targets, coeffs, block_ids, inverses)
        return lax.cond(
            flag[0] > 0,
            spread_path,
            lambda *given: general_path(*given[:5]),
            *args, pts_sib, me, *plans,
        )

    return jax.shard_map(
        per_device,
        mesh=mesh,
        in_specs=(P("rows", None), P("rows", "labels"), P("rows", "labels"), P(), P()),
        out_specs=P("rows", "labels"),
        check_vma=False,
    )
```

```python
import jax
import jax.numpy as jnp
from jax import lax
from jax.experimental import pallas as pl
from jax.experimental.pallas import tpu as pltpu
from jax.sharding import PartitionSpec as P

ridge_weight = 0.5
bf16 = jnp.bfloat16
f32 = jnp.float32
i32 = jnp.int32
whole = pl.BlockSpec(memory_space=pltpu.VMEM)


def dot_nn(a, b):
    return lax.dot_general(a, b, (((1,), (0,)), ((), ())), preferred_element_type=f32)


def dot_nt(a, b):
    return lax.dot_general(a, b, (((1,), (1,)), ((), ())), preferred_element_type=f32)


def square_sums(pts):
    return jnp.sum(jnp.square(pts.astype(f32)), axis=1, keepdims=True)


def kernel_tile(left, right):
    inner_prod = dot_nt(left, right)
    sq_dist = jnp.maximum(square_sums(left) + square_sums(right).T - 2.0 * inner_prod, 0.0)
    return jnp.exp(-(2.0 / left.shape[1]) * sq_dist).astype(bf16)


def split_bf16(x):
    high = x.astype(bf16)
    return high, (x - high.astype(f32)).astype(bf16)


def as_row(column):
    n = column.shape[0]
    return jnp.transpose(jnp.broadcast_to(column, (n, 128)))[0:1, :]


def iota(shape, dim):
    return lax.broadcasted_iota(i32, shape, dim)


def one_hot(cond):
    return jnp.where(cond, 1.0, 0.0).astype(bf16)


def after(x, *others):
    return lax.optimization_barrier((x, *others))[0]


def params(megabytes):
    return pltpu.CompilerParams(vmem_limit_bytes=megabytes << 20)


def cost(macs, bytes_accessed):
    return pl.CostEstimate(flops=2 * macs, bytes_accessed=bytes_accessed, transcendentals=0)


def general_path(points, targets, coeffs, block_ids, inverses):
    rows_here = points.shape[0]
    first_row = lax.axis_index("rows") * rows_here
    zero_low = jnp.zeros((), bf16)
    current = coeffs
    for blk in range(2):
        local_ids = block_ids[blk] - first_row
        inside = (local_ids >= 0) & (local_ids < rows_here)
        local_rows = jnp.clip(local_ids, 0, rows_here - 1)
        picked = jnp.where(inside[:, None], points[local_rows], zero_low)
        block_pts = lax.psum(picked, "rows").astype(f32).astype(bf16)
        ktile = kernel_tile(points, block_pts)
        c_low = current.astype(bf16)
        sel_targets = jnp.where(inside[:, None], targets[local_rows].astype(f32), 0.0)
        sel_coeffs = jnp.where(inside[:, None], current[local_rows], 0.0)
        local_side = ridge_weight * sel_coeffs - sel_targets
        product = lax.dot_general(
            ktile, c_low, (((0,), (0,)), ((), ())), preferred_element_type=f32
        )
        share = lax.psum_scatter(product + local_side, "rows", scatter_dimension=0, tiled=True)
        negated = lax.all_gather(share, "rows", axis=0, tiled=True)
        update = jnp.dot(
            inverses[blk], -negated, precision=lax.Precision.HIGHEST, preferred_element_type=f32
        )
        where_to = (jnp.arange(rows_here, dtype=i32)[:, None] == local_ids[None, :]).astype(f32)
        current = current + jnp.dot(
            where_to, update, precision=lax.Precision.HIGHEST, preferred_element_type=f32
        )
    return current


def plan(me, block_ids, rows, ring, stage_bits, caps):
    total = block_ids.size
    blk = block_ids.shape[1]
    chips = len(ring)
    place = [ring.index(k) for k in range(chips)]
    piece = total // (2 * chips)
    bits = len(caps)
    n_final = total - (chips - 1) * piece
    step = min(256, total)
    groups = []
    for core in range(2):
        done = 0
        for stage in range(bits):
            members = {}
            for k in range(chips):
                members.setdefault(k & ~done, []).append(k)
            groups += [(m, caps[stage]) for m in members.values()]
            done |= stage_bits[core][stage]

    def body(me_ref, ids_ref, flag_ref, slots_ref, their_ref, spots_ref, lag_ref):
        chip, core = me_ref[0] // 2, me_ref[0] % 2
        ids = jnp.concatenate([ids_ref[0:1, :], ids_ref[1:2, :]], axis=1).astype(f32)
        ids_col = jnp.transpose(jnp.broadcast_to(ids, (128, total)))
        own = jnp.floor((ids + 0.5) * (0.5 / rows))
        index = iota((1, total), 1)
        rank = jnp.zeros((1, total), f32)
        for r in range(0, total, step):
            own_col = jnp.floor((ids_col[r : r + step, 0:1] + 0.5) * (0.5 / rows))
            ahead = (own_col == own) & (r + iota((step, total), 0) < index)
            rank += jnp.sum(jnp.where(ahead, 1.0, 0.0), axis=0, keepdims=True)

        def count(which):
            return jnp.sum(jnp.where(own == which, 1.0, 0.0), axis=1, keepdims=True)

        def slots(listed):
            slot = jnp.full((1, total), -1.0, f32)
            before = jnp.zeros((1, 1), f32)
            for which in listed:
                which = which.astype(f32)
                slot = jnp.where(own == which, before + rank, slot)
                before = before + count(which)
            return slot

        counts = [count(float(k)) for k in range(chips)]
        slack = counts[0] - piece
        for k in range(1, chips):
            slack = jnp.minimum(slack, counts[k] - piece)
        for members, cap in groups:
            slack = jnp.minimum(slack, cap - sum(counts[k] for k in members))
        flag_ref[0] = (jnp.max(slack) >= 0.0).astype(i32)

        slots_ref[...] = jnp.zeros(slots_ref.shape, i32)
        group = [0]
        theirs = []
        for stage in range(bits):
            bit = jnp.where(core == 0, stage_bits[0][stage], stage_bits[1][stage])
            slots_ref[stage : stage + 1, :] = slots([chip ^ g for g in group]).astype(i32)
            theirs.append(slots([chip ^ bit ^ g for g in group]))
            group = group + [g ^ bit for g in group]
        slots_ref[7:8, :] = ids.astype(i32)
        fill = jnp.zeros((127 - bits, total), f32)
        columns = jnp.concatenate(theirs + [fill, ids], axis=0)
        their_ref[...] = jnp.transpose(columns).astype(i32)

        def lookup(which, table):
            out = jnp.int32(table[0])
            for k in range(1, chips):
                out = jnp.where(which == k, table[k], out)
            return out

        here = lookup(chip, place)
        way = jnp.where(core == 0, chips - 1, 1)
        listed = [lookup((here + way * (k + 1)) % chips, ring) for k in range(chips)]
        position = slots(listed)
        slots_ref[bits : bits + 1, :] = position.astype(i32)
        lag_ref[...] = jnp.broadcast_to(count(listed[0].astype(f32)), (8, 128)).astype(i32)
        pos_col = jnp.transpose(jnp.broadcast_to(position, (128, total)))[:, 0:1]
        line = ((chips - 1) * piece + iota((1, n_final), 1)).astype(f32)
        spots = jnp.sum(
            jnp.where(pos_col == line, ids_col[:, 0:1], 0.0), axis=0, keepdims=True
        )
        spots_ref[...] = spots.astype(i32)

    smem = pl.BlockSpec(memory_space=pltpu.SMEM)
    return pl.pallas_call(
        body,
        out_shape=[
            jax.ShapeDtypeStruct((1,), i32),
            jax.ShapeDtypeStruct((8, total), i32),
            jax.ShapeDtypeStruct((total, 128), i32),
            jax.ShapeDtypeStruct((1, n_final), i32),
            jax.ShapeDtypeStruct((8, 128), i32),
        ],
        in_specs=[smem, whole],
        out_specs=[smem, whole, whole, whole, whole],
        compiler_params=params(16),
        cost_estimate=cost(1 << 20, 1 << 20),
    )(me, block_ids)


def pick_points(me, slots, theirs, points, sib_points, half_f, cap):
    total, rows = slots.shape[1], points.shape[0]

    def body(me_ref, their_ref, slots_ref, own_ref, sib_ref, block_ref, sent_ref):
        cols = pl.ds(pl.multiple_of(me_ref[0] % 2 * half_f, 128), half_f)
        local = iota((total, rows), 1)
        ids = their_ref[:, 127:128]
        own = one_hot(ids == local + me_ref[0] * rows)
        sib = one_hot(ids == local + (me_ref[0] ^ 1) * rows)
        block = (dot_nn(own, own_ref[:, cols]) + dot_nn(sib, sib_ref[:, cols])).astype(bf16)
        block_ref[...] = block
        pack = one_hot(iota((cap, total), 0) == slots_ref[0:1, :])
        sent_ref[...] = dot_nn(pack, block).astype(bf16)

    return pl.pallas_call(
        body,
        out_shape=[
            jax.ShapeDtypeStruct((total, half_f), bf16),
            jax.ShapeDtypeStruct((cap, half_f), bf16),
        ],
        in_specs=[pl.BlockSpec(memory_space=pltpu.SMEM)] + [whole] * 4,
        out_specs=[whole] * 2,
        compiler_params=params(16),
        cost_estimate=cost(2 * total * rows * half_f, 6 << 20),
    )(me, theirs, slots, points, sib_points)


def merge_points(block, got, slots, theirs, stage, cap_next):
    total, half_f = block.shape
    cap = got.shape[0]

    def body(block_ref, got_ref, slots_ref, their_ref, out_ref, *sent_ref):
        unpack = one_hot(their_ref[:, stage : stage + 1] == iota((total, cap), 1))
        merged = (block_ref[...].astype(f32) + dot_nn(unpack, got_ref[...])).astype(bf16)
        out_ref[...] = merged
        if sent_ref:
            pack = one_hot(iota((cap_next, total), 0) == slots_ref[stage + 1 : stage + 2, :])
            sent_ref[0][...] = dot_nn(pack, merged).astype(bf16)

    out_shape = [jax.ShapeDtypeStruct((total, half_f), bf16)]
    if cap_next:
        out_shape.append(jax.ShapeDtypeStruct((cap_next, half_f), bf16))
    return pl.pallas_call(
        body,
        out_shape=out_shape,
        in_specs=[whole] * 4,
        out_specs=[whole] * len(out_shape),
        compiler_params=params(16),
        cost_estimate=cost(2 * total * cap * half_f, 6 << 20),
    )(block, got, slots, theirs)


def cut_columns(me, x, width, blk):
    rows = x.shape[0]

    def body(me_ref, mine_ref, other_ref, mine_out, other_out):
        mine_out[...] = mine_ref[...].astype(bf16)
        other_out[...] = other_ref[...].astype(bf16)

    def half(k):
        return pl.BlockSpec(
            (rows, blk), lambda j, me_ref: (0, (me_ref[0] ^ k) % 2 * (width // blk) + j)
        )

    plain = pl.BlockSpec((rows, blk), lambda j, me_ref: (0, j))
    return pl.pallas_call(
        body,
        out_shape=[jax.ShapeDtypeStruct((rows, width), bf16)] * 2,
        grid_spec=pltpu.PrefetchScalarGridSpec(
            num_scalar_prefetch=1,
            grid=(width // blk,),
            in_specs=[half(0), half(1)],
            out_specs=[plain] * 2,
        ),
        compiler_params=params(16),
        cost_estimate=cost(0, rows * width * 8),
    )(me, x, x)


def pack_targets(slots, theirs, me, mine, sib, cap):
    rows, width = mine.shape
    total = slots.shape[1]

    def body(me_ref, slots_ref, mine_ref, sib_ref, out_ref):
        here = iota((cap, total), 0) == slots_ref[0:1, :]
        ids = slots_ref[7:8, :].astype(f32)
        wanted = jnp.sum(jnp.where(here, ids + 1.0, 0.0), axis=1, keepdims=True) - 1.0
        local = iota((cap, rows), 1)
        picks = [one_hot(wanted == (local + (me_ref[0] ^ k) * rows).astype(f32)) for k in range(2)]
        pick = jnp.concatenate(picks, axis=1)
        for at in range(0, width, 512):
            end = min(at + 512, width)
            strip = jnp.concatenate([mine_ref[:, at:end], sib_ref[:, at:end]], axis=0)
            out_ref[:, at:end] = dot_nn(pick, strip).astype(bf16)

    return pl.pallas_call(
        body,
        out_shape=jax.ShapeDtypeStruct((cap, width), bf16),
        in_specs=[pl.BlockSpec(memory_space=pltpu.SMEM)] + [whole] * 3,
        out_specs=whole,
        compiler_params=params(16),
        cost_estimate=cost(4 * cap * rows * width, 3 * rows * width * 2),
    )(me, slots, mine, sib)


def build_maps(me, points, sib_points, q_half, q_other, inverses, slots, theirs):
    rows, feats = points.shape
    half_f = feats // 2
    total = slots.shape[1]
    blk = total // 2
    step = min(256, rows, blk)
    scale = -(2.0 / feats)

    def body(
        me_ref, own_ref, sib_ref, qh_ref, qo_ref, inv_ref, idr_ref, idc_ref,
        left_ref, rest_ref, rows_ref, along_ref, norm_ref,
    ):
        mine = pl.ds(pl.multiple_of(me_ref[0] % 2 * half_f, 128), half_f)
        other = pl.ds(pl.multiple_of((1 - me_ref[0] % 2) * half_f, 128), half_f)
        for r in range(0, total, step):
            part = square_sums(qh_ref[r : r + step, :]) + square_sums(qo_ref[r : r + step, :])
            norm_ref[r : r + step, :] = jnp.broadcast_to(part, (step, 128))
        norms = jnp.transpose(norm_ref[...])[0:1, :]

        def values(a, b, a_sq, b_sq, same):
            inner = dot_nt(a[0], b[0]) + dot_nt(a[1], b[1])
            sq_dist = jnp.maximum(a_sq + b_sq - 2.0 * inner, 0.0)
            k = jnp.exp(scale * sq_dist).astype(bf16).astype(f32)
            return (k + jnp.where(same, ridge_weight, 0.0)).astype(bf16)

        cross = []
        for r in range(blk, total, step):
            at = slice(r, r + step)
            cross.append(
                values(
                    (qh_ref[at, :], qo_ref[at, :]),
                    (qh_ref[:blk, :], qo_ref[:blk, :]),
                    norm_ref[at, 0:1],
                    norms[:, :blk],
                    idc_ref[at, 127:128] == idr_ref[7:8, :blk],
                )
            )
        cross = jnp.concatenate(cross, axis=0)
        inv0, inv1 = inv_ref[0], inv_ref[1]
        high0, low0 = split_bf16(inv0)
        high1, low1 = split_bf16(inv1)
        high, low = split_bf16(dot_nn(cross, high0) + dot_nn(cross, low0))
        lower = -(dot_nn(high1, high) + dot_nn(high1, low) + dot_nn(low1, high))

        bell = jnp.exp(-scale * (jnp.min(norms) - norms))

        def direction(inv, weights):
            way = jnp.sum(inv * weights, axis=1, keepdims=True)
            return way * lax.rsqrt(jnp.maximum(jnp.sum(way * way), 1e-30))

        way0 = direction(inv0, bell[:, :blk])
        way1 = direction(inv1, bell[:, blk:])
        row00 = jnp.sum(way0 * inv0, axis=0, keepdims=True)
        row10 = jnp.sum(way1 * lower, axis=0, keepdims=True)
        row11 = jnp.sum(way1 * inv1, axis=0, keepdims=True)
        rest_ref[:blk, :blk] = (inv0 - way0 * row00).astype(bf16)
        rest_ref[:blk, blk:] = jnp.zeros((blk, blk), bf16)
        rest_ref[blk:, :blk] = (lower - way1 * row10).astype(bf16)
        rest_ref[blk:, blk:] = (inv1 - way1 * row11).astype(bf16)
        rows_ref[...] = jnp.zeros((8, total), f32)
        rows_ref[0:1, :blk] = row00
        rows_ref[1:2, :blk] = row10
        rows_ref[1:2, blk:] = row11
        along_ref[...] = jnp.zeros((8, total), f32)
        along_ref[0:1, :blk] = as_row(way0)
        along_ref[1:2, blk:] = as_row(way1)

        for which, ref in enumerate((own_ref, sib_ref)):
            for r in range(0, rows, step):
                at = slice(r, r + step)
                a = (ref[at, mine], ref[at, other])
                spot = (me_ref[0] ^ which) * rows + r + iota((step, total), 0)
                left_ref[which * rows + r : which * rows + r + step, :] = -values(
                    a,
                    (qh_ref[...], qo_ref[...]),
                    square_sums(a[0]) + square_sums(a[1]),
                    norms,
                    spot == idr_ref[7:8, :],
                )

    return pl.pallas_call(
        body,
        out_shape=[
            jax.ShapeDtypeStruct((2 * rows, total), bf16),
            jax.ShapeDtypeStruct((total, total), bf16),
            jax.ShapeDtypeStruct((8, total), f32),
            jax.ShapeDtypeStruct((8, total), f32),
        ],
        in_specs=[pl.BlockSpec(memory_space=pltpu.SMEM)] + [whole] * 7,
        out_specs=[whole] * 4,
        scratch_shapes=[pltpu.VMEM((total, 128), f32)],
        compiler_params=params(24),
        cost_estimate=cost(4 * rows * total * feats, 12 << 20),
    )(me, points, sib_points, q_half, q_other, inverses, slots, theirs)


def map_weights(lo, count, extra, slots, pos_row, rest, left, rows_along, cap):
    points, total = left.shape

    def fill(slots_ref, rest_ref, left_ref, along_ref, weights):
        sel = one_hot(slots_ref[pos_row : pos_row + 1, :] == lo + iota((count, total), 0))
        moved = dot_nn(sel, rest_ref[...]).astype(bf16)
        if extra:
            padded = jnp.concatenate([along_ref[...], jnp.zeros((8, total), f32)], axis=0)
            moved = jnp.concatenate([moved, *split_bf16(padded)], axis=0)
        pack = one_hot(iota((cap, total), 0) == slots_ref[0:1, :])
        for at, other in ((slice(0, points), left_ref[...]), (slice(points, points + cap), pack)):
            mapped = dot_nt(moved, other)
            weights[:count, at] = mapped[:count].astype(bf16)
            if extra:
                both = mapped[count : count + 16] + mapped[count + 16 :]
                weights[count : count + 16, at], weights[count + 16 :, at] = split_bf16(both)

    if extra:
        return fill

    def body(slots_ref, rest_ref, left_ref, out_ref):
        fill(slots_ref, rest_ref, left_ref, None, out_ref)

    return pl.pallas_call(
        body,
        out_shape=jax.ShapeDtypeStruct((count, points + cap), bf16),
        in_specs=[whole] * 3,
        out_specs=whole,
        compiler_params=params(20),
        cost_estimate=cost(count * (2 * points + cap) * total, 6 << 20),
    )(slots, rest, left)


def strips_of(bands):
    return [(k, min(k + 512, end)) for at, end in bands for k in range(at, end, 512)]


def first_shares(count, piece, bands, slots, pos_row, rest, left, rows_along, parts):
    width, cap = parts[0].shape[1], parts[-1].shape[0]
    height, depth = count + 32, left.shape[0] + cap
    fill = map_weights(0, count, True, slots, pos_row, rest, left, rows_along, cap)

    def body(slots_ref, rest_ref, left_ref, along_ref, *refs):
        part_refs, out_ref, amount_ref = refs[:3], refs[3], refs[4]
        band_refs, weights = refs[5:-1], refs[-1]
        fill(slots_ref, rest_ref, left_ref, along_ref, weights)
        for at, end in strips_of(bands):
            strip = jnp.concatenate([ref[:, at:end] for ref in part_refs], axis=0)
            out = dot_nn(weights[...], strip)
            out_ref[:, at:end] = out[piece:count]
            amount_ref[:, at:end] = out[count : count + 8] + out[count + 16 : count + 24]
            for band, ref in zip(bands, band_refs):
                if band[0] <= at < band[1]:
                    ref[:, at - band[0] : end - band[0]] = out[:piece].astype(bf16)

    out_shape = [
        jax.ShapeDtypeStruct((count - piece, width), f32),
        jax.ShapeDtypeStruct((8, width), f32),
    ]
    out_shape += [jax.ShapeDtypeStruct((piece, end - at), bf16) for at, end in bands]
    return pl.pallas_call(
        body,
        out_shape=out_shape,
        in_specs=[whole] * 7,
        out_specs=[whole] * len(out_shape),
        scratch_shapes=[pltpu.VMEM((height, depth), bf16)],
        compiler_params=params(20),
        cost_estimate=cost(count * depth * (width + 1024), 12 << 20),
    )(slots, rest, left, rows_along, *parts)


def more_shares(me, weights, lo, count, parts):
    depth, width = weights.shape[1], parts[0].shape[1]

    def body(me_ref, weights_ref, *refs):
        for at, end in strips_of([(0, width)]):
            strip = jnp.concatenate([ref[:, at:end] for ref in refs[:3]], axis=0)
            refs[3][:, at:end] = dot_nn(weights_ref[lo : lo + count, :], strip)

    return pl.pallas_call(
        body,
        out_shape=jax.ShapeDtypeStruct((count, width), f32),
        in_specs=[pl.BlockSpec(memory_space=pltpu.SMEM)] + [whole] * 4,
        out_specs=whole,
        compiler_params=params(16),
        cost_estimate=cost(count * depth * width, 10 << 20),
    )(me, weights, *parts)


def final_maps(me, slots, along, spots, rows):
    total, n = slots.shape[1], spots.shape[1]

    def body(me_ref, slots_ref, along_ref, spots_ref, sel_ref, scale_ref):
        first = me_ref[0] * rows
        sel_ref[...] = one_hot(first + iota((rows, n), 0) == spots_ref[...])
        same = first + iota((rows, total), 0) == slots_ref[7:8, :]
        scale_ref[...] = jnp.zeros((rows, 128), f32)
        for b in range(2):
            weight = jnp.where(same, along_ref[b : b + 1, :], 0.0)
            scale_ref[:, b : b + 1] = jnp.sum(weight, axis=1, keepdims=True)

    return pl.pallas_call(
        body,
        out_shape=[jax.ShapeDtypeStruct((rows, n), bf16), jax.ShapeDtypeStruct((rows, 128), f32)],
        in_specs=[pl.BlockSpec(memory_space=pltpu.SMEM)] + [whole] * 3,
        out_specs=[whole] * 2,
        compiler_params=params(16),
        cost_estimate=cost(1 << 20, 3 << 20),
    )(me, slots, along, spots)


def add_band(me, coeffs, buffer, sel, scale, amount, amount_sib, mine, sib, width, band, blk):
    rows, cols = coeffs.shape
    n = len(mine)
    piece = mine[0].shape[0]
    per_half, at, count = width // blk, band[0] // blk, (band[1] - band[0]) // blk

    def body(me_ref, c_ref, sel_ref, scale_ref, am_ref, as_ref, *refs):
        mine_refs, sib_refs, out_ref = refs[:n], refs[n : 2 * n], refs[-1]

        def finish(amount_ref, parts):
            out = dot_nn(sel_ref[...], jnp.concatenate([ref[...] for ref in parts], axis=0))
            for b in range(2):
                out += scale_ref[:, b : b + 1] * amount_ref[b : b + 1, :]
            out_ref[...] = c_ref[...] + out

        inside = pl.program_id(0) // count == me_ref[0] % 2
        pl.when(inside)(lambda: finish(am_ref, mine_refs))
        pl.when(jnp.logical_not(inside))(lambda: finish(as_ref, sib_refs))

    def side(height, k, offset):
        def place(j, me_ref):
            first = (me_ref[0] ^ k) % 2 * count
            return 0, offset + jnp.clip(j - first, 0, count - 1)

        return pl.BlockSpec((height, blk), place)

    plain = pl.BlockSpec((rows, blk), lambda j, me_ref: (0, j // count * per_half + at + j % count))
    operands = [coeffs, sel, scale, amount, amount_sib, *mine, *sib]
    in_specs = [plain, whole, whole, side(8, 0, at), side(8, 1, at)]
    in_specs += [side(piece, 0, 0)] * n + [side(piece, 1, 0)] * n
    aliases = {}
    if buffer is not None:
        aliases = {1 + len(operands): 0}
        operands.append(buffer)
        in_specs.append(pl.BlockSpec(memory_space=pl.ANY))
    return pl.pallas_call(
        body,
        out_shape=jax.ShapeDtypeStruct((rows, cols), f32),
        grid_spec=pltpu.PrefetchScalarGridSpec(
            num_scalar_prefetch=1, grid=(2 * count,), in_specs=in_specs, out_specs=plain
        ),
        input_output_aliases=aliases,
        compiler_params=params(16),
        cost_estimate=cost(rows * n * piece * cols // 2, rows * cols * 4),
    )(me, *operands)


def solution(mesh):
    n = mesh.shape["rows"]
    chips = n // 2
    bits = chips.bit_length() - 1
    ring = [k ^ (k >> 1) for k in range(chips)]
    place = [ring.index(k) for k in range(chips)]

    def core_perm(chip_of):
        return [(i, 2 * chip_of(i // 2, i % 2) + i % 2) for i in range(n)]

    sib_perm = [(i, i ^ 1) for i in range(n)]
    ring_perm = core_perm(
        lambda chip, core: ring[(place[chip] + (1 if core == 0 else chips - 1)) % chips]
    )

    def stage_bit(stage, core):
        return 1 << (stage if core == 0 else bits - 1 - stage)

    def to_sib(x):
        return lax.ppermute(x, "rows", sib_perm)

    def stage_cap(total, stage):
        return min(total, total // 2 + ((1 << stage) - 1) * (total // chips))

    def spread_path(points, targets, coeffs, inverses, pts_sib, me, slots, theirs, spots, lag):
        rows_here, feats = points.shape
        cols = coeffs.shape[1]
        half_f = feats // 2
        extra_cols = -cols % 256
        if extra_cols:
            targets = jnp.pad(targets, ((0, 0), (0, extra_cols)))
            coeffs = jnp.pad(coeffs, ((0, 0), (0, extra_cols)))
        width = (cols + extra_cols) // 2
        blk = 128 * max(d for d in (1, 2, 3, 4) if width // 128 % d == 0)
        total = slots.shape[1]
        piece = total // (2 * chips)
        steps = 2 * chips - 1

        caps = [stage_cap(total, stage) for stage in range(bits)] + [0]
        block_half, sent = pick_points(me, slots, theirs, points, pts_sib, half_f, caps[0])
        for stage in range(bits):
            got = lax.ppermute(
                sent, "rows", core_perm(lambda k, c, s=stage: k ^ stage_bit(s, c))
            )
            if stage == 0:
                t_mine, t_other = cut_columns(after(me, sent), targets, width, blk)
                t_sib = to_sib(t_other)
            if stage == min(1, bits - 1):
                c_mine, c_other = cut_columns(after(me, sent), coeffs, width, blk)
                c_sib = to_sib(c_other)
                t_packed = pack_targets(
                    slots, theirs, after(me, c_other), t_mine, t_sib, caps[0]
                )
            block_half, *sent = merge_points(
                block_half, got, slots, theirs, stage, caps[stage + 1]
            )
            sent = sent[0] if sent else None
        block_other = to_sib(block_half)
        parts = [c_mine, c_sib, t_packed]

        left, rest, rows_along, along = build_maps(
            me, points, pts_sib, block_half, block_other, inverses, slots, theirs
        )

        blocks = width // blk
        first = (blocks + 1) // 2 * blk
        bands = [(0, first), (first, width)] if first < width else [(0, width)]
        lead = 2
        share, amount, *first_sent = first_shares(
            lead * piece, piece, bands, slots, bits, rest, left, rows_along, parts
        )
        share = {1: share}
        arrived = [[] for _ in bands]
        final = [[] for _ in bands]
        final_sib = [[] for _ in bands]
        line = jnp.arange(piece, dtype=i32)[:, None]
        places = jnp.arange(steps * piece, dtype=i32)[None, :]
        fillers = []
        latest = None
        for step in range(steps + 1):
            for b, (lo, hi) in enumerate(bands):
                if step == 0:
                    sent = first_sent[b]
                else:
                    arrived[b][-1] = after(arrived[b][-1], latest, *fillers)
                    fillers = []
                    source = step * piece + line - lag[0:1, 0:1]
                    shift = (source == places[:, : step * piece]).astype(bf16)
                    carried = dot_nn(shift, jnp.concatenate(arrived[b], axis=0))
                    sent = (share[step][:, lo:hi] + carried).astype(bf16)
                latest = sent
                if step < steps:
                    arrived[b].append(lax.ppermute(sent, "rows", ring_perm))
                if step >= chips - 1:
                    final[b].append(sent)
                    final_sib[b].append(to_sib(sent))
            if step == 0:
                weights = map_weights(
                    lead * piece, total - lead * piece, False, after(slots, latest), bits,
                    rest, left, None, caps[0],
                )
                fillers.append(weights)
            elif 2 * step < 2 * chips:
                rows = (2 * step - lead) * piece
                pair = more_shares(after(me, latest), weights, rows, 2 * piece, parts)
                share[2 * step], share[2 * step + 1] = pair[:piece], pair[piece:]
                fillers.append(pair)
            elif step == chips:
                sel, scale = final_maps(after(me, latest), slots, along, spots, rows_here)
                fillers.append(scale)
            if 3 <= step < 3 + bits:
                amount = amount + after(coming, latest)
            if 2 <= step < 2 + bits:
                coming = lax.ppermute(
                    after(amount, latest), "rows",
                    core_perm(lambda k, c, s=step - 2: k ^ stage_bit(s, c)),
                )
        amount_sib = to_sib(amount)

        out = None
        for b, band in enumerate(bands):
            out = add_band(
                me, coeffs, out, sel, scale, amount, amount_sib, final[b], final_sib[b],
                width, band, blk,
            )
        return out[:, :cols] if extra_cols else out

    def per_device(points, targets, coeffs, block_ids, inverses):
        rows_here = points.shape[0]
        total = block_ids.size
        me = lax.axis_index("rows").astype(i32).reshape(1)
        pts_sib = to_sib(points)
        stage_bits = [[stage_bit(s, core) for s in range(bits)] for core in range(2)]
        caps = [stage_cap(total, s) for s in range(bits)]
        fits, *plans = plan(me, block_ids, rows_here, ring, stage_bits, caps)
        out = spread_path(points, targets, coeffs, inverses, pts_sib, me, *plans)

        def general(state):
            return jnp.ones_like(fits), general_path(points, targets, coeffs, block_ids, inverses)

        return lax.while_loop(lambda state: state[0][0] == 0, general, (fits, out))[1]

    return jax.shard_map(
        per_device,
        mesh=mesh,
        in_specs=(P("rows", None), P("rows", "labels"), P("rows", "labels"), P(), P()),
        out_specs=P("rows", "labels"),
        check_vma=False,
    )
```

```python
import jax
import jax.numpy as jnp
from jax import lax
from jax.experimental import pallas as pl
from jax.experimental.pallas import tpu as pltpu
from jax.sharding import PartitionSpec as P

ridge_weight = 0.5
bf16 = jnp.bfloat16
f32 = jnp.float32
i32 = jnp.int32
whole = pl.BlockSpec(memory_space=pltpu.VMEM)


def dot_nn(a, b):
    return lax.dot_general(a, b, (((1,), (0,)), ((), ())), preferred_element_type=f32)


def dot_nt(a, b):
    return lax.dot_general(a, b, (((1,), (1,)), ((), ())), preferred_element_type=f32)


def square_sums(pts):
    return jnp.sum(jnp.square(pts.astype(f32)), axis=1, keepdims=True)


def kernel_tile(left, right):
    inner_prod = dot_nt(left, right)
    sq_dist = jnp.maximum(square_sums(left) + square_sums(right).T - 2.0 * inner_prod, 0.0)
    return jnp.exp(-(2.0 / left.shape[1]) * sq_dist).astype(bf16)


def split_bf16(x):
    high = x.astype(bf16)
    return high, (x - high.astype(f32)).astype(bf16)


def both_parts(x):
    high, low = split_bf16(x)
    return jnp.concatenate([high.astype(f32), low.astype(f32)], axis=0).astype(bf16)


def as_row(column):
    n = column.shape[0]
    return jnp.transpose(jnp.broadcast_to(column, (n, 128)))[0:1, :]


def iota(shape, dim):
    return lax.broadcasted_iota(i32, shape, dim)


def one_hot(cond):
    return jnp.where(cond, 1.0, 0.0).astype(bf16)


def after(x, *others):
    return lax.optimization_barrier((x, *others))[0]


def params(megabytes):
    return pltpu.CompilerParams(vmem_limit_bytes=megabytes << 20)


def cost(macs, bytes_accessed):
    return pl.CostEstimate(flops=2 * macs, bytes_accessed=bytes_accessed, transcendentals=0)


def general_path(points, targets, coeffs, block_ids, inverses):
    rows_here = points.shape[0]
    first_row = lax.axis_index("rows") * rows_here
    zero_low = jnp.zeros((), bf16)
    current = coeffs
    for blk in range(2):
        local_ids = block_ids[blk] - first_row
        inside = (local_ids >= 0) & (local_ids < rows_here)
        local_rows = jnp.clip(local_ids, 0, rows_here - 1)
        picked = jnp.where(inside[:, None], points[local_rows], zero_low)
        block_pts = lax.psum(picked, "rows").astype(f32).astype(bf16)
        ktile = kernel_tile(points, block_pts)
        c_low = current.astype(bf16)
        sel_targets = jnp.where(inside[:, None], targets[local_rows].astype(f32), 0.0)
        sel_coeffs = jnp.where(inside[:, None], current[local_rows], 0.0)
        local_side = ridge_weight * sel_coeffs - sel_targets
        product = lax.dot_general(
            ktile, c_low, (((0,), (0,)), ((), ())), preferred_element_type=f32
        )
        share = lax.psum_scatter(product + local_side, "rows", scatter_dimension=0, tiled=True)
        negated = lax.all_gather(share, "rows", axis=0, tiled=True)
        update = jnp.dot(
            inverses[blk], -negated, precision=lax.Precision.HIGHEST, preferred_element_type=f32
        )
        where_to = (jnp.arange(rows_here, dtype=i32)[:, None] == local_ids[None, :]).astype(f32)
        current = current + jnp.dot(
            where_to, update, precision=lax.Precision.HIGHEST, preferred_element_type=f32
        )
    return current


def plan(me, block_ids, rows, ring, stage_bits, caps):
    total = block_ids.size
    blk = block_ids.shape[1]
    chips = len(ring)
    place = [ring.index(k) for k in range(chips)]
    piece = total // (2 * chips)
    bits = len(caps)
    n_final = total - (chips - 1) * piece
    step = min(256, total)
    groups = []
    for core in range(2):
        done = 0
        for stage in range(bits):
            members = {}
            for k in range(chips):
                members.setdefault(k & ~done, []).append(k)
            groups += [(m, caps[stage]) for m in members.values()]
            done |= stage_bits[core][stage]

    def body(me_ref, ids_ref, flag_ref, slots_ref, their_ref, spots_ref, shift_ref):
        chip, core = me_ref[0] // 2, me_ref[0] % 2
        ids = jnp.concatenate([ids_ref[0:1, :], ids_ref[1:2, :]], axis=1).astype(f32)
        ids_col = jnp.transpose(jnp.broadcast_to(ids, (128, total)))
        own = jnp.floor((ids + 0.5) * (0.5 / rows))
        index = iota((1, total), 1)
        rank = jnp.zeros((1, total), f32)
        for r in range(0, total, step):
            own_col = jnp.floor((ids_col[r : r + step, 0:1] + 0.5) * (0.5 / rows))
            ahead = (own_col == own) & (r + iota((step, total), 0) < index)
            rank += jnp.sum(jnp.where(ahead, 1.0, 0.0), axis=0, keepdims=True)

        def count(which):
            return jnp.sum(jnp.where(own == which, 1.0, 0.0), axis=1, keepdims=True)

        def slots(listed):
            slot = jnp.full((1, total), -1.0, f32)
            before = jnp.zeros((1, 1), f32)
            for which in listed:
                which = which.astype(f32)
                slot = jnp.where(own == which, before + rank, slot)
                before = before + count(which)
            return slot

        counts = [count(float(k)) for k in range(chips)]
        slack = counts[0] - piece
        for k in range(1, chips):
            slack = jnp.minimum(slack, counts[k] - piece)
        for members, cap in groups:
            slack = jnp.minimum(slack, cap - sum(counts[k] for k in members))
        flag_ref[0] = (jnp.max(slack) >= 0.0).astype(i32)

        slots_ref[...] = jnp.zeros(slots_ref.shape, i32)
        group = [0]
        columns = []
        for stage in range(bits):
            bit = jnp.where(core == 0, stage_bits[0][stage], stage_bits[1][stage])
            mine = slots([chip ^ g for g in group])
            if stage == 0:
                slots_ref[0:1, :] = mine.astype(i32)
                line = iota((caps[0], total), 0).astype(f32)
                wanted = jnp.where(mine == line, ids + 1.0, 0.0)
                wanted = jnp.sum(wanted, axis=1, keepdims=True) - 1.0
            if stage == bits - 1:
                columns += [mine, slots([chip ^ bit ^ g for g in group])]
            else:
                held = sum(count((chip ^ g).astype(f32)) for g in group)
                columns.append(jnp.broadcast_to(held, (1, total)))
            group = group + [g ^ bit for g in group]
        slots_ref[7:8, :] = ids.astype(i32)
        fill = jnp.zeros((127 - len(columns), total), f32)
        columns = jnp.concatenate(columns + [fill, ids], axis=0)
        their_ref[...] = jnp.transpose(columns).astype(i32)
        their_ref[: caps[0], 126:127] = wanted.astype(i32)

        def lookup(which, table):
            out = jnp.int32(table[0])
            for k in range(1, chips):
                out = jnp.where(which == k, table[k], out)
            return out

        here = lookup(chip, place)
        way = jnp.where(core == 0, chips - 1, 1)
        listed = [lookup((here + way * (k + 1)) % chips, ring) for k in range(chips)]
        position = slots(listed)
        slots_ref[bits : bits + 1, :] = position.astype(i32)
        lag = count(listed[0].astype(f32)).astype(i32)
        length = (2 * chips - 1) * piece
        source = iota((piece, length), 0) - lag + length
        shift_ref[...] = one_hot(source == iota((piece, length), 1))
        pos_col = jnp.transpose(jnp.broadcast_to(position, (128, total)))[:, 0:1]
        line = ((chips - 1) * piece + iota((1, n_final), 1)).astype(f32)
        spots = jnp.sum(
            jnp.where(pos_col == line, ids_col[:, 0:1], 0.0), axis=0, keepdims=True
        )
        spots_ref[...] = spots.astype(i32)

    smem = pl.BlockSpec(memory_space=pltpu.SMEM)
    return pl.pallas_call(
        body,
        out_shape=[
            jax.ShapeDtypeStruct((1,), i32),
            jax.ShapeDtypeStruct((8, total), i32),
            jax.ShapeDtypeStruct((total, 128), i32),
            jax.ShapeDtypeStruct((1, n_final), i32),
            jax.ShapeDtypeStruct((piece, total - piece), bf16),
        ],
        in_specs=[smem, whole],
        out_specs=[smem, whole, whole, whole, whole],
        compiler_params=params(16),
        cost_estimate=cost(1 << 20, 1 << 20),
    )(me, block_ids)


def pick_points(me, theirs, points, sib_points, half_f, cap):
    rows = points.shape[0]

    def body(me_ref, their_ref, own_ref, sib_ref, sent_ref):
        cols = pl.ds(pl.multiple_of(me_ref[0] % 2 * half_f, 128), half_f)
        wanted = their_ref[:cap, 126:127]
        local = iota((cap, rows), 1)
        own = one_hot(wanted == local + me_ref[0] * rows)
        sib = one_hot(wanted == local + (me_ref[0] ^ 1) * rows)
        out = dot_nn(own, own_ref[:, cols]) + dot_nn(sib, sib_ref[:, cols])
        sent_ref[...] = out.astype(bf16)

    return pl.pallas_call(
        body,
        out_shape=jax.ShapeDtypeStruct((cap, half_f), bf16),
        in_specs=[pl.BlockSpec(memory_space=pltpu.SMEM)] + [whole] * 3,
        out_specs=whole,
        compiler_params=params(16),
        cost_estimate=cost(2 * cap * rows * half_f, 4 << 20),
    )(me, theirs, points, sib_points)


def append_rows(sent, got, theirs, stage, cap_next):
    cap, half_f = sent.shape

    def body(sent_ref, got_ref, their_ref, out_ref):
        held = their_ref[:cap_next, stage : stage + 1]
        behind = one_hot(iota((cap_next, cap), 0) - held == iota((cap_next, cap), 1))
        out = dot_nn(behind, got_ref[...])
        out_ref[:cap, :] = (out[:cap] + sent_ref[...].astype(f32)).astype(bf16)
        if cap_next > cap:
            out_ref[cap:, :] = out[cap:].astype(bf16)

    return pl.pallas_call(
        body,
        out_shape=jax.ShapeDtypeStruct((cap_next, half_f), bf16),
        in_specs=[whole] * 3,
        out_specs=whole,
        compiler_params=params(16),
        cost_estimate=cost(cap * cap_next * half_f, 4 << 20),
    )(sent, got, theirs)


def place_rows(packed, theirs, column, block=None):
    cap, half_f = packed.shape
    total = theirs.shape[0]

    def body(packed_ref, their_ref, *refs):
        spots = one_hot(their_ref[:, column : column + 1] == iota((total, cap), 1))
        out = dot_nn(spots, packed_ref[...])
        if block is not None:
            out += refs[0][...].astype(f32)
        refs[-1][...] = out.astype(bf16)

    return pl.pallas_call(
        body,
        out_shape=jax.ShapeDtypeStruct((total, half_f), bf16),
        in_specs=[whole] * (2 if block is None else 3),
        out_specs=whole,
        compiler_params=params(16),
        cost_estimate=cost(total * cap * half_f, 4 << 20),
    )(packed, theirs, *([] if block is None else [block]))


def point_norms(points, sib_points):
    rows = points.shape[0]

    def body(own_ref, sib_ref, out_ref):
        for k, ref in enumerate((own_ref, sib_ref)):
            norm = square_sums(ref[...])
            out_ref[k * rows : (k + 1) * rows, :] = jnp.broadcast_to(norm, (rows, 128))

    return pl.pallas_call(
        body,
        out_shape=jax.ShapeDtypeStruct((2 * rows, 128), f32),
        in_specs=[whole] * 2,
        out_specs=whole,
        compiler_params=params(16),
        cost_estimate=cost(4 << 20, 3 << 20),
    )(points, sib_points)


def cut_columns(me, x, width, blk):
    rows = x.shape[0]

    def body(me_ref, mine_ref, other_ref, mine_out, other_out):
        mine_out[...] = mine_ref[...].astype(bf16)
        other_out[...] = other_ref[...].astype(bf16)

    def half(k):
        return pl.BlockSpec(
            (rows, blk), lambda j, me_ref: (0, (me_ref[0] ^ k) % 2 * (width // blk) + j)
        )

    plain = pl.BlockSpec((rows, blk), lambda j, me_ref: (0, j))
    return pl.pallas_call(
        body,
        out_shape=[jax.ShapeDtypeStruct((rows, width), bf16)] * 2,
        grid_spec=pltpu.PrefetchScalarGridSpec(
            num_scalar_prefetch=1,
            grid=(width // blk,),
            in_specs=[half(0), half(1)],
            out_specs=[plain] * 2,
        ),
        compiler_params=params(16),
        cost_estimate=cost(0, rows * width * 8),
    )(me, x, x)


def pack_targets(me, theirs, targets, cap, width, blk):
    rows = targets.shape[0]

    def body(me_ref, their_ref, mine_ref, other_ref, mine_out, other_out):
        local = iota((cap, rows), 1) + me_ref[0] * rows
        pick = one_hot(their_ref[:cap, 126:127] == local)
        mine_out[...] = dot_nn(pick, mine_ref[...]).astype(bf16)
        other_out[...] = dot_nn(pick, other_ref[...]).astype(bf16)

    def half(k):
        return pl.BlockSpec(
            (rows, blk), lambda j, me_ref: (0, (me_ref[0] ^ k) % 2 * (width // blk) + j)
        )

    plain = pl.BlockSpec((cap, blk), lambda j, me_ref: (0, j))
    return pl.pallas_call(
        body,
        out_shape=[jax.ShapeDtypeStruct((cap, width), bf16)] * 2,
        grid_spec=pltpu.PrefetchScalarGridSpec(
            num_scalar_prefetch=1,
            grid=(width // blk,),
            in_specs=[whole, half(0), half(1)],
            out_specs=[plain] * 2,
        ),
        compiler_params=params(16),
        cost_estimate=cost(2 * cap * rows * width, rows * width * 8),
    )(me, theirs, targets, targets)


def build_maps(me, points, sib_points, norms_in, q_half, q_other, inverses, slots, theirs):
    rows, feats = points.shape
    half_f = feats // 2
    total = slots.shape[1]
    blk = total // 2
    step = min(256, rows, blk)
    scale = -(2.0 / feats)

    def body(
        me_ref, own_ref, sib_ref, pn_ref, qh_ref, qo_ref, inv_ref, idr_ref, idc_ref,
        left_ref, rest_ref, rows_ref, along_ref, norm_ref,
    ):
        mine = pl.ds(pl.multiple_of(me_ref[0] % 2 * half_f, 128), half_f)
        other = pl.ds(pl.multiple_of((1 - me_ref[0] % 2) * half_f, 128), half_f)
        for r in range(0, total, step):
            part = square_sums(qh_ref[r : r + step, :]) + square_sums(qo_ref[r : r + step, :])
            norm_ref[r : r + step, :] = jnp.broadcast_to(part, (step, 128))
        norms = jnp.transpose(norm_ref[...])[0:1, :]

        def values(a, b, a_sq, b_sq, same):
            inner = dot_nt(a[0], b[0]) + dot_nt(a[1], b[1])
            sq_dist = jnp.maximum(a_sq + b_sq - 2.0 * inner, 0.0)
            k = jnp.exp(scale * sq_dist).astype(bf16).astype(f32)
            return (k + jnp.where(same, ridge_weight, 0.0)).astype(bf16)

        cross = []
        for r in range(blk, total, step):
            at = slice(r, r + step)
            cross.append(
                values(
                    (qh_ref[at, :], qo_ref[at, :]),
                    (qh_ref[:blk, :], qo_ref[:blk, :]),
                    norm_ref[at, 0:1],
                    norms[:, :blk],
                    idc_ref[at, 127:128] == idr_ref[7:8, :blk],
                )
            )
        cross = jnp.concatenate(cross, axis=0)
        inv0, inv1 = inv_ref[0], inv_ref[1]
        high0, low0 = split_bf16(inv0)
        high1, low1 = split_bf16(inv1)
        high, low = split_bf16(dot_nn(cross, high0) + dot_nn(cross, low0))
        lower = -(dot_nn(high1, high) + dot_nn(high1, low) + dot_nn(low1, high))

        bell = jnp.exp(-scale * (jnp.min(norms) - norms))

        def direction(inv, weights):
            way = jnp.sum(inv * weights, axis=1, keepdims=True)
            return way * lax.rsqrt(jnp.maximum(jnp.sum(way * way), 1e-30))

        way0 = direction(inv0, bell[:, :blk])
        way1 = direction(inv1, bell[:, blk:])
        row00 = jnp.sum(way0 * inv0, axis=0, keepdims=True)
        row10 = jnp.sum(way1 * lower, axis=0, keepdims=True)
        row11 = jnp.sum(way1 * inv1, axis=0, keepdims=True)
        rest_ref[:blk, :blk] = (inv0 - way0 * row00).astype(bf16)
        rest_ref[:blk, blk:] = jnp.zeros((blk, blk), bf16)
        rest_ref[blk:, :blk] = (lower - way1 * row10).astype(bf16)
        rest_ref[blk:, blk:] = (inv1 - way1 * row11).astype(bf16)
        rows_ref[...] = jnp.zeros((8, total), f32)
        rows_ref[0:1, :blk] = row00
        rows_ref[1:2, :blk] = row10
        rows_ref[1:2, blk:] = row11
        along_ref[...] = jnp.zeros((8, total), f32)
        along_ref[0:1, :blk] = as_row(way0)
        along_ref[1:2, blk:] = as_row(way1)

        for which, ref in enumerate((own_ref, sib_ref)):
            for r in range(0, rows, step):
                at = slice(r, r + step)
                a = (ref[at, mine], ref[at, other])
                spot = (me_ref[0] ^ which) * rows + r + iota((step, total), 0)
                left_ref[which * rows + r : which * rows + r + step, :] = -values(
                    a,
                    (qh_ref[...], qo_ref[...]),
                    pn_ref[which * rows + r : which * rows + r + step, 0:1],
                    norms,
                    spot == idr_ref[7:8, :],
                )

    return pl.pallas_call(
        body,
        out_shape=[
            jax.ShapeDtypeStruct((2 * rows, total), bf16),
            jax.ShapeDtypeStruct((total, total), bf16),
            jax.ShapeDtypeStruct((8, total), f32),
            jax.ShapeDtypeStruct((8, total), f32),
        ],
        in_specs=[pl.BlockSpec(memory_space=pltpu.SMEM)] + [whole] * 8,
        out_specs=[whole] * 4,
        scratch_shapes=[pltpu.VMEM((total, 128), f32)],
        compiler_params=params(24),
        cost_estimate=cost(4 * rows * total * feats, 12 << 20),
    )(me, points, sib_points, norms_in, q_half, q_other, inverses, slots, theirs)


def map_weights(lo, count, extra, slots, pos_row, rest, left, rows_along, cap):
    points, total = left.shape

    def fill(slots_ref, rest_ref, left_ref, along_ref, weights):
        sel = one_hot(slots_ref[pos_row : pos_row + 1, :] == lo + iota((count, total), 0))
        moved = dot_nn(sel, rest_ref[...]).astype(bf16)
        if extra:
            moved = jnp.concatenate([moved, both_parts(along_ref[...])], axis=0)
        pack = one_hot(iota((cap, total), 0) == slots_ref[0:1, :])
        for at, other in ((slice(0, points), left_ref[...]), (slice(points, points + cap), pack)):
            mapped = dot_nt(moved, other)
            weights[:count, at] = mapped[:count].astype(bf16)
            if extra:
                both = mapped[count : count + 8] + mapped[count + 8 :]
                weights[count:, at] = both_parts(both)

    if extra:
        return fill

    def body(slots_ref, rest_ref, left_ref, out_ref):
        fill(slots_ref, rest_ref, left_ref, None, out_ref)

    return pl.pallas_call(
        body,
        out_shape=jax.ShapeDtypeStruct((count, points + cap), bf16),
        in_specs=[whole] * 3,
        out_specs=whole,
        compiler_params=params(20),
        cost_estimate=cost(count * (2 * points + cap) * total, 6 << 20),
    )(slots, rest, left)


def strips_of(bands):
    return [(k, min(k + 512, end)) for at, end in bands for k in range(at, end, 512)]


def strip_of(refs, at, end):
    targets = refs[2][:, at:end] + refs[3][:, at:end]
    return jnp.concatenate([refs[0][:, at:end], refs[1][:, at:end], targets], axis=0)


def first_shares(piece, bands, slots, pos_row, rest, left, rows_along, parts):
    width, cap = parts[0].shape[1], parts[-1].shape[0]
    height, depth = piece + 16, left.shape[0] + cap
    fill = map_weights(0, piece, True, slots, pos_row, rest, left, rows_along, cap)

    def body(slots_ref, rest_ref, left_ref, along_ref, *refs):
        part_refs, refs = refs[: len(parts)], refs[len(parts) :]
        amount_ref, band_refs, weights = refs[0], refs[1:-1], refs[-1]
        fill(slots_ref, rest_ref, left_ref, along_ref, weights)
        for at, end in strips_of(bands):
            out = dot_nn(weights[...], strip_of(part_refs, at, end))
            amount_ref[:, at:end] = out[piece : piece + 8] + out[piece + 8 :]
            for band, ref in zip(bands, band_refs):
                if band[0] <= at < band[1]:
                    strip = slice(at - band[0], end - band[0])
                    ref[:piece, strip] = out[:piece].astype(bf16)
                    ref[piece:, strip] = both_parts(out[piece : piece + 8] + out[piece + 8 :])

    out_shape = [jax.ShapeDtypeStruct((8, width), f32)]
    out_shape += [jax.ShapeDtypeStruct((piece + 16, end - at), bf16) for at, end in bands]
    return pl.pallas_call(
        body,
        out_shape=out_shape,
        in_specs=[whole] * (4 + len(parts)),
        out_specs=[whole] * len(out_shape),
        scratch_shapes=[pltpu.VMEM((height, depth), bf16)],
        compiler_params=params(20),
        cost_estimate=cost(height * depth * (width + 1024), 12 << 20),
    )(slots, rest, left, rows_along, *parts)


def more_shares(me, weights, lo, count, bands, parts):
    depth, width = weights.shape[1], parts[0].shape[1]

    def body(me_ref, weights_ref, *refs):
        for at, end in strips_of(bands):
            strip = strip_of(refs, at, end)
            refs[-1][:, at:end] = dot_nn(weights_ref[lo : lo + count, :], strip)

    return pl.pallas_call(
        body,
        out_shape=jax.ShapeDtypeStruct((count, width), f32),
        in_specs=[pl.BlockSpec(memory_space=pltpu.SMEM)] + [whole] * (1 + len(parts)),
        out_specs=whole,
        compiler_params=params(16),
        cost_estimate=cost(count * depth * width, 10 << 20),
    )(me, weights, *parts)


def add_arrived(me, share, row, band, shift, arrived, carry):
    piece, length = shift.shape
    n = len(arrived)

    def body(me_ref, share_ref, shift_ref, *refs):
        out = share_ref[row : row + piece, band[0] : band[1]]
        for k, ref in enumerate(refs[:-1]):
            at = length - (n - k) * piece
            out += dot_nn(shift_ref[:, at : at + piece], ref[:piece, :])
        refs[-1][:piece, :] = out.astype(bf16)
        if carry:
            refs[-1][piece:, :] = refs[-2][piece:, :]

    height = piece + (16 if carry else 0)
    return pl.pallas_call(
        body,
        out_shape=jax.ShapeDtypeStruct((height, band[1] - band[0]), bf16),
        in_specs=[pl.BlockSpec(memory_space=pltpu.SMEM)] + [whole] * (2 + n),
        out_specs=whole,
        compiler_params=params(12),
        cost_estimate=cost(n * piece * piece * (band[1] - band[0]), 6 << 20),
    )(me, share, shift, *arrived)


def sum_amounts(me, amount, bands, arrived):
    piece = arrived[0][0].shape[0] - 16

    def body(me_ref, amount_ref, *refs):
        out_ref, refs = refs[-1], list(refs[:-1])
        for (at, end), pieces in zip(bands, arrived):
            out = amount_ref[:, at:end]
            for _ in pieces:
                both = refs.pop(0)[piece:, :].astype(f32)
                out += both[:8] + both[8:]
            out_ref[:, at:end] = out

    return pl.pallas_call(
        body,
        out_shape=jax.ShapeDtypeStruct(amount.shape, f32),
        in_specs=[pl.BlockSpec(memory_space=pltpu.SMEM)] + [whole] * (1 + sum(map(len, arrived))),
        out_specs=whole,
        compiler_params=params(12),
        cost_estimate=cost(0, 2 << 20),
    )(me, amount, *[ref for pieces in arrived for ref in pieces])


def final_maps(me, slots, along, spots, rows):
    total, n = slots.shape[1], spots.shape[1]

    def body(me_ref, slots_ref, along_ref, spots_ref, sel_ref, scale_ref):
        first = me_ref[0] * rows
        sel_ref[...] = one_hot(first + iota((rows, n), 0) == spots_ref[...])
        same = first + iota((rows, total), 0) == slots_ref[7:8, :]
        scale_ref[...] = jnp.zeros((rows, 128), f32)
        for b in range(2):
            weight = jnp.where(same, along_ref[b : b + 1, :], 0.0)
            scale_ref[:, b : b + 1] = jnp.sum(weight, axis=1, keepdims=True)

    return pl.pallas_call(
        body,
        out_shape=[jax.ShapeDtypeStruct((rows, n), bf16), jax.ShapeDtypeStruct((rows, 128), f32)],
        in_specs=[pl.BlockSpec(memory_space=pltpu.SMEM)] + [whole] * 3,
        out_specs=[whole] * 2,
        compiler_params=params(16),
        cost_estimate=cost(1 << 20, 3 << 20),
    )(me, slots, along, spots)


def add_early(me, other, coeffs, sel, scale, amount, pieces, width, band, blk):
    rows = coeffs.shape[0]
    n, piece = len(pieces), pieces[0].shape[0]
    per_half, at, count = width // blk, band[0] // blk, (band[1] - band[0]) // blk

    def body(me_ref, src_ref, sel_ref, scale_ref, amount_ref, *refs):
        strip = jnp.concatenate([ref[...] for ref in refs[:-1]], axis=0)
        out = src_ref[...] + dot_nn(sel_ref[:, : n * piece], strip)
        for b in range(2):
            out += scale_ref[:, b : b + 1] * amount_ref[b : b + 1, :]
        refs[-1][...] = out

    def source(j, me_ref):
        return 0, (me_ref[0] ^ other) % 2 * per_half + at + j

    plain = pl.BlockSpec((piece, blk), lambda j, me_ref: (0, j))
    return pl.pallas_call(
        body,
        out_shape=jax.ShapeDtypeStruct((rows, count * blk), f32),
        grid_spec=pltpu.PrefetchScalarGridSpec(
            num_scalar_prefetch=1,
            grid=(count,),
            in_specs=[
                pl.BlockSpec((rows, blk), source),
                whole,
                whole,
                pl.BlockSpec((8, blk), lambda j, me_ref: (0, at + j)),
                *[plain] * n,
            ],
            out_specs=pl.BlockSpec((rows, blk), lambda j, me_ref: (0, j)),
        ),
        compiler_params=params(12),
        cost_estimate=cost(rows * n * piece * count * blk, rows * count * blk * 8),
    )(me, coeffs, sel, scale, amount, *pieces)


def add_last(me, early, cols, buffer, sel, mine, sib, width, band, blk):
    rows = sel.shape[0]
    n, piece = len(mine), mine[0].shape[0]
    per_half, at, count = width // blk, band[0] // blk, (band[1] - band[0]) // blk

    def body(me_ref, sel_ref, early_mine, early_sib, *refs):
        j = pl.program_id(0)
        cut = pl.ds(pl.multiple_of(j % count * blk, 128), blk)

        def finish(early_ref, parts):
            strip = jnp.concatenate([ref[:, cut] for ref in parts], axis=0)
            chosen = sel_ref[:, sel_ref.shape[1] - n * piece :]
            refs[-1][...] = early_ref[:, cut] + dot_nn(chosen, strip)

        inside = j // count == me_ref[0] % 2
        pl.when(inside)(lambda: finish(early_mine, refs[:n]))
        pl.when(jnp.logical_not(inside))(lambda: finish(early_sib, refs[n : 2 * n]))

    spread = pl.BlockSpec((rows, blk), lambda j, me_ref: (0, j // count * per_half + at + j % count))
    operands = [sel, *early, *mine, *sib]
    in_specs = [whole] * len(operands)
    aliases = {}
    if buffer is not None:
        aliases = {1 + len(operands): 0}
        operands.append(buffer)
        in_specs.append(pl.BlockSpec(memory_space=pl.ANY))
    return pl.pallas_call(
        body,
        out_shape=pltpu.HBM((rows, cols), f32),
        grid_spec=pltpu.PrefetchScalarGridSpec(
            num_scalar_prefetch=1, grid=(2 * count,), in_specs=in_specs, out_specs=spread
        ),
        input_output_aliases=aliases,
        compiler_params=params(12),
        cost_estimate=cost(rows * n * piece * 2 * count * blk, rows * 2 * count * blk * 8),
    )(me, *operands)


def solution(mesh):
    n = mesh.shape["rows"]
    chips = n // 2
    bits = chips.bit_length() - 1
    ring = [k ^ (k >> 1) for k in range(chips)]
    place = [ring.index(k) for k in range(chips)]

    def core_perm(chip_of):
        return [(i, 2 * chip_of(i // 2, i % 2) + i % 2) for i in range(n)]

    sib_perm = [(i, i ^ 1) for i in range(n)]
    ring_perm = core_perm(
        lambda chip, core: ring[(place[chip] + (1 if core == 0 else chips - 1)) % chips]
    )

    def stage_bit(stage, core):
        return 1 << (stage if core == 0 else bits - 1 - stage)

    def to_sib(x):
        return lax.ppermute(x, "rows", sib_perm)

    def stage_cap(total, stage):
        return min(total, total // 2 + ((1 << stage) - 1) * (total // chips))

    def spread_path(points, targets, coeffs, inverses, pts_sib, me, slots, theirs, spots, shift):
        rows_here, feats = points.shape
        cols = coeffs.shape[1]
        half_f = feats // 2
        extra_cols = -cols % 256
        if extra_cols:
            targets = jnp.pad(targets, ((0, 0), (0, extra_cols)))
            coeffs = jnp.pad(coeffs, ((0, 0), (0, extra_cols)))
        width = (cols + extra_cols) // 2
        blk = 128 * max(d for d in (1, 2, 3, 4) if width // 128 % d == 0)
        total = slots.shape[1]
        piece = total // (2 * chips)
        steps = 2 * chips - 1

        blocks = width // blk
        first = (blocks + 1) // 2 * blk
        bands = [(0, first), (first, width)] if first < width else [(0, width)]

        caps = [stage_cap(total, stage) for stage in range(bits)]
        sent = pick_points(me, theirs, points, pts_sib, half_f, caps[0])
        for stage in range(bits):
            got = lax.ppermute(
                sent, "rows", core_perm(lambda k, c, s=stage: k ^ stage_bit(s, c))
            )
            if stage == 0:
                wide = 128 * max(d for d in range(1, 9) if width // 128 % d == 0)
                t_mine, t_other = pack_targets(
                    after(me, sent), theirs, targets, caps[0], width, wide
                )
                t_sib = to_sib(t_other)
            if stage < bits - 1:
                sent = append_rows(sent, got, theirs, stage, caps[stage + 1])
        placed = place_rows(sent, theirs, bits - 1)
        norms = point_norms(after(points, placed), pts_sib)
        block_half = place_rows(after(got, norms), theirs, bits, placed)
        block_other = to_sib(block_half)
        c_mine, c_other = cut_columns(after(me, block_half), coeffs, width, blk)
        c_sib = to_sib(after(c_other, block_other))
        parts = [c_mine, c_sib, t_mine, t_sib]

        left, rest, rows_along, along = build_maps(
            me, points, pts_sib, norms, block_half, block_other, inverses, slots,
            theirs,
        )

        amount, *first_sent = first_shares(
            piece, bands, slots, bits, rest, left, rows_along, parts
        )
        share = {}
        arrived = [[] for _ in bands]
        final = [[] for _ in bands]
        final_sib = [[] for _ in bands]
        early_mine, early_sib = [], []
        early = steps - 1 - chips
        fillers = []
        latest = None

        def exchange(b, latest):
            for part in final[b][len(final_sib[b]) :]:
                final_sib[b].append(to_sib(after(part, latest)))

        def early_of(other, b, amounts, pieces, me_then):
            return add_early(
                me_then, other, coeffs, sel, scale, amounts, pieces[b][:early], width, bands[b], blk
            )

        for step in range(steps + 1):
            for b, band in enumerate(bands):
                if step == 0:
                    sent = first_sent[b]
                else:
                    arrived[b][-1] = after(arrived[b][-1], latest, *fillers)
                    fillers = []
                    sent = add_arrived(
                        me, *share[step], band, shift, arrived[b][-chips:], step < chips - 1
                    )
                latest = sent
                if step < steps:
                    arrived[b].append(lax.ppermute(sent, "rows", ring_perm))
                if step >= chips - 1:
                    final[b].append(sent)
                if step == steps:
                    exchange(b, latest)
                    if b + 1 < len(bands):
                        early_sib.append(
                            early_of(1, b + 1, amount_sib, final_sib, after(me, latest))
                        )
                        fillers.append(early_sib[-1])
            row = 2 * step + 1
            if row < 2 * chips:
                count = min(2, 2 * chips - row)
                weights = map_weights(
                    row * piece, count * piece, False, after(slots, latest), bits, rest, left,
                    None, caps[0],
                )
                more = more_shares(after(me, latest), weights, 0, count * piece, bands, parts)
                for k in range(count):
                    share[row + k] = (more, k * piece)
                fillers.append(more)
            if step == chips - 1:
                carried = [pieces[: chips - 1] for pieces in arrived]
                amount = sum_amounts(after(me, latest), amount, bands, carried)
                sel, scale = final_maps(after(me, latest), slots, along, spots, rows_here)
                fillers += [amount, scale]
            b = step - (steps - 1 - len(bands))
            if 0 <= b < len(bands):
                early_mine.append(early_of(0, b, amount, final, after(me, latest)))
                fillers.append(early_mine[-1])
            if step == steps - 1:
                amount_sib = to_sib(after(amount, latest))
                for b in range(len(bands)):
                    exchange(b, latest)
                early_sib.append(early_of(1, 0, amount_sib, final_sib, me))
                fillers.append(early_sib[-1])

        out = None
        for b, band in enumerate(bands):
            out = add_last(
                me, (early_mine[b], early_sib[b]), cols + extra_cols, out, sel,
                final[b][early:], final_sib[b][early:], width, band, blk,
            )
        return out[:, :cols] if extra_cols else out

    def per_device(points, targets, coeffs, block_ids, inverses):
        rows_here = points.shape[0]
        total = block_ids.size
        me = lax.axis_index("rows").astype(i32).reshape(1)
        pts_sib = to_sib(points)
        stage_bits = [[stage_bit(s, core) for s in range(bits)] for core in range(2)]
        caps = [stage_cap(total, s) for s in range(bits)]
        fits, *plans = plan(me, block_ids, rows_here, ring, stage_bits, caps)
        out = spread_path(points, targets, coeffs, inverses, pts_sib, me, *plans)

        def general(state):
            return jnp.ones_like(fits), general_path(points, targets, coeffs, block_ids, inverses)

        return lax.while_loop(lambda state: state[0][0] == 0, general, (fits, out))[1]

    return jax.shard_map(
        per_device,
        mesh=mesh,
        in_specs=(P("rows", None), P("rows", "labels"), P("rows", "labels"), P(), P()),
        out_specs=P("rows", "labels"),
        check_vma=False,
    )
```

```python
import jax
import jax.numpy as jnp
from jax import lax
from jax.experimental import pallas as pl
from jax.experimental.pallas import tpu as pltpu
from jax.sharding import PartitionSpec as P

ridge_weight = 0.5
bf16 = jnp.bfloat16
f32 = jnp.float32
i32 = jnp.int32
whole = pl.BlockSpec(memory_space=pltpu.VMEM)


def dot_nn(a, b):
    return lax.dot_general(a, b, (((1,), (0,)), ((), ())), preferred_element_type=f32)


def dot_nt(a, b):
    return lax.dot_general(a, b, (((1,), (1,)), ((), ())), preferred_element_type=f32)


def square_sums(pts):
    return jnp.sum(jnp.square(pts.astype(f32)), axis=1, keepdims=True)


def kernel_tile(left, right):
    inner_prod = dot_nt(left, right)
    sq_dist = jnp.maximum(square_sums(left) + square_sums(right).T - 2.0 * inner_prod, 0.0)
    return jnp.exp(-(2.0 / left.shape[1]) * sq_dist).astype(bf16)


def split_bf16(x):
    high = x.astype(bf16)
    return high, (x - high.astype(f32)).astype(bf16)


def both_parts(x):
    high, low = split_bf16(x)
    return jnp.concatenate([high.astype(f32), low.astype(f32)], axis=0).astype(bf16)


def as_row(column):
    n = column.shape[0]
    return jnp.transpose(jnp.broadcast_to(column, (n, 128)))[0:1, :]


def iota(shape, dim):
    return lax.broadcasted_iota(i32, shape, dim)


def one_hot(cond):
    return jnp.where(cond, 1.0, 0.0).astype(bf16)


def after(x, *others):
    return lax.optimization_barrier((x, *others))[0]


def params(megabytes):
    return pltpu.CompilerParams(vmem_limit_bytes=megabytes << 20)


def cost(macs, bytes_accessed):
    return pl.CostEstimate(flops=2 * macs, bytes_accessed=bytes_accessed, transcendentals=0)


def general_path(points, targets, coeffs, block_ids, inverses):
    rows_here = points.shape[0]
    first_row = lax.axis_index("rows") * rows_here
    zero_low = jnp.zeros((), bf16)
    current = coeffs
    for blk in range(2):
        local_ids = block_ids[blk] - first_row
        inside = (local_ids >= 0) & (local_ids < rows_here)
        local_rows = jnp.clip(local_ids, 0, rows_here - 1)
        picked = jnp.where(inside[:, None], points[local_rows], zero_low)
        block_pts = lax.psum(picked, "rows").astype(f32).astype(bf16)
        ktile = kernel_tile(points, block_pts)
        c_low = current.astype(bf16)
        sel_targets = jnp.where(inside[:, None], targets[local_rows].astype(f32), 0.0)
        sel_coeffs = jnp.where(inside[:, None], current[local_rows], 0.0)
        local_side = ridge_weight * sel_coeffs - sel_targets
        product = lax.dot_general(
            ktile, c_low, (((0,), (0,)), ((), ())), preferred_element_type=f32
        )
        share = lax.psum_scatter(product + local_side, "rows", scatter_dimension=0, tiled=True)
        negated = lax.all_gather(share, "rows", axis=0, tiled=True)
        update = jnp.dot(
            inverses[blk], -negated, precision=lax.Precision.HIGHEST, preferred_element_type=f32
        )
        where_to = (jnp.arange(rows_here, dtype=i32)[:, None] == local_ids[None, :]).astype(f32)
        current = current + jnp.dot(
            where_to, update, precision=lax.Precision.HIGHEST, preferred_element_type=f32
        )
    return current


def plan(me, block_ids, rows, ring, stage_bits, caps):
    total = block_ids.size
    blk = block_ids.shape[1]
    chips = len(ring)
    place = [ring.index(k) for k in range(chips)]
    piece = total // (2 * chips)
    bits = len(caps)
    n_final = total - (chips - 1) * piece
    step = min(256, total)
    groups = []
    for core in range(2):
        done = 0
        for stage in range(bits):
            members = {}
            for k in range(chips):
                members.setdefault(k & ~done, []).append(k)
            groups += [(m, caps[stage]) for m in members.values()]
            done |= stage_bits[core][stage]

    def body(me_ref, ids_ref, flag_ref, slots_ref, their_ref, spots_ref, shift_ref):
        chip, core = me_ref[0] // 2, me_ref[0] % 2
        ids = jnp.concatenate([ids_ref[0:1, :], ids_ref[1:2, :]], axis=1).astype(f32)
        ids_col = jnp.transpose(jnp.broadcast_to(ids, (128, total)))
        own = jnp.floor((ids + 0.5) * (0.5 / rows))
        index = iota((1, total), 1)
        rank = jnp.zeros((1, total), f32)
        for r in range(0, total, step):
            own_col = jnp.floor((ids_col[r : r + step, 0:1] + 0.5) * (0.5 / rows))
            ahead = (own_col == own) & (r + iota((step, total), 0) < index)
            rank += jnp.sum(jnp.where(ahead, 1.0, 0.0), axis=0, keepdims=True)

        def count(which):
            return jnp.sum(jnp.where(own == which, 1.0, 0.0), axis=1, keepdims=True)

        def slots(listed):
            slot = jnp.full((1, total), -1.0, f32)
            before = jnp.zeros((1, 1), f32)
            for which in listed:
                which = which.astype(f32)
                slot = jnp.where(own == which, before + rank, slot)
                before = before + count(which)
            return slot

        counts = [count(float(k)) for k in range(chips)]
        slack = counts[0] - piece
        for k in range(1, chips):
            slack = jnp.minimum(slack, counts[k] - piece)
        for members, cap in groups:
            slack = jnp.minimum(slack, cap - sum(counts[k] for k in members))
        flag_ref[0] = (jnp.max(slack) >= 0.0).astype(i32)

        slots_ref[...] = jnp.zeros(slots_ref.shape, i32)
        group = [0]
        columns = []
        for stage in range(bits):
            bit = jnp.where(core == 0, stage_bits[0][stage], stage_bits[1][stage])
            mine = slots([chip ^ g for g in group])
            if stage == 0:
                slots_ref[0:1, :] = mine.astype(i32)
                line = iota((caps[0], total), 0).astype(f32)
                wanted = jnp.where(mine == line, ids + 1.0, 0.0)
                wanted = jnp.sum(wanted, axis=1, keepdims=True) - 1.0
            if stage == bits - 1:
                columns += [mine, slots([chip ^ bit ^ g for g in group])]
            else:
                held = sum(count((chip ^ g).astype(f32)) for g in group)
                columns.append(jnp.broadcast_to(held, (1, total)))
            group = group + [g ^ bit for g in group]
        slots_ref[7:8, :] = ids.astype(i32)
        fill = jnp.zeros((127 - len(columns), total), f32)
        columns = jnp.concatenate(columns + [fill, ids], axis=0)
        their_ref[...] = jnp.transpose(columns).astype(i32)
        their_ref[: caps[0], 126:127] = wanted.astype(i32)

        def lookup(which, table):
            out = jnp.int32(table[0])
            for k in range(1, chips):
                out = jnp.where(which == k, table[k], out)
            return out

        here = lookup(chip, place)
        way = jnp.where(core == 0, chips - 1, 1)
        listed = [lookup((here + way * (k + 1)) % chips, ring) for k in range(chips)]
        position = slots(listed)
        slots_ref[bits : bits + 1, :] = position.astype(i32)
        lag = count(listed[0].astype(f32)).astype(i32)
        length = (2 * chips - 1) * piece
        source = iota((piece, length), 0) - lag + length
        shift_ref[...] = one_hot(source == iota((piece, length), 1))
        pos_col = jnp.transpose(jnp.broadcast_to(position, (128, total)))[:, 0:1]
        line = ((chips - 1) * piece + iota((1, n_final), 1)).astype(f32)
        spots = jnp.sum(
            jnp.where(pos_col == line, ids_col[:, 0:1], 0.0), axis=0, keepdims=True
        )
        spots_ref[...] = spots.astype(i32)

    smem = pl.BlockSpec(memory_space=pltpu.SMEM)
    return pl.pallas_call(
        body,
        out_shape=[
            jax.ShapeDtypeStruct((1,), i32),
            jax.ShapeDtypeStruct((8, total), i32),
            jax.ShapeDtypeStruct((total, 128), i32),
            jax.ShapeDtypeStruct((1, n_final), i32),
            jax.ShapeDtypeStruct((piece, total - piece), bf16),
        ],
        in_specs=[smem, whole],
        out_specs=[smem, whole, whole, whole, whole],
        compiler_params=params(16),
        cost_estimate=cost(1 << 20, 1 << 20),
    )(me, block_ids)


def pick_points(me, theirs, points, sib_points, half_f, cap):
    rows = points.shape[0]

    def body(me_ref, their_ref, own_ref, sib_ref, sent_ref):
        cols = pl.ds(pl.multiple_of(me_ref[0] % 2 * half_f, 128), half_f)
        wanted = their_ref[:cap, 126:127]
        local = iota((cap, rows), 1)
        own = one_hot(wanted == local + me_ref[0] * rows)
        sib = one_hot(wanted == local + (me_ref[0] ^ 1) * rows)
        out = dot_nn(own, own_ref[:, cols]) + dot_nn(sib, sib_ref[:, cols])
        sent_ref[...] = out.astype(bf16)

    return pl.pallas_call(
        body,
        out_shape=jax.ShapeDtypeStruct((cap, half_f), bf16),
        in_specs=[pl.BlockSpec(memory_space=pltpu.SMEM)] + [whole] * 3,
        out_specs=whole,
        compiler_params=params(16),
        cost_estimate=cost(2 * cap * rows * half_f, 4 << 20),
    )(me, theirs, points, sib_points)


def append_rows(sent, got, theirs, stage, cap_next):
    cap, half_f = sent.shape

    def body(sent_ref, got_ref, their_ref, out_ref):
        held = their_ref[:cap_next, stage : stage + 1]
        behind = one_hot(iota((cap_next, cap), 0) - held == iota((cap_next, cap), 1))
        out = dot_nn(behind, got_ref[...])
        out_ref[:cap, :] = (out[:cap] + sent_ref[...].astype(f32)).astype(bf16)
        if cap_next > cap:
            out_ref[cap:, :] = out[cap:].astype(bf16)

    return pl.pallas_call(
        body,
        out_shape=jax.ShapeDtypeStruct((cap_next, half_f), bf16),
        in_specs=[whole] * 3,
        out_specs=whole,
        compiler_params=params(16),
        cost_estimate=cost(cap * cap_next * half_f, 4 << 20),
    )(sent, got, theirs)


def place_rows(packed, theirs, column, block=None):
    cap, half_f = packed.shape
    total = theirs.shape[0]

    def body(packed_ref, their_ref, *refs):
        spots = one_hot(their_ref[:, column : column + 1] == iota((total, cap), 1))
        out = dot_nn(spots, packed_ref[...])
        if block is not None:
            out += refs[0][...].astype(f32)
        refs[-1][...] = out.astype(bf16)

    return pl.pallas_call(
        body,
        out_shape=jax.ShapeDtypeStruct((total, half_f), bf16),
        in_specs=[whole] * (2 if block is None else 3),
        out_specs=whole,
        compiler_params=params(16),
        cost_estimate=cost(total * cap * half_f, 4 << 20),
    )(packed, theirs, *([] if block is None else [block]))


def point_norms(points, sib_points):
    rows = points.shape[0]

    def body(own_ref, sib_ref, out_ref):
        for k, ref in enumerate((own_ref, sib_ref)):
            norm = square_sums(ref[...])
            out_ref[k * rows : (k + 1) * rows, :] = jnp.broadcast_to(norm, (rows, 128))

    return pl.pallas_call(
        body,
        out_shape=jax.ShapeDtypeStruct((2 * rows, 128), f32),
        in_specs=[whole] * 2,
        out_specs=whole,
        compiler_params=params(16),
        cost_estimate=cost(4 << 20, 3 << 20),
    )(points, sib_points)


def cut_columns(me, x, width, blk):
    rows = x.shape[0]

    def body(me_ref, mine_ref, other_ref, mine_out, other_out):
        mine_out[...] = mine_ref[...].astype(bf16)
        other_out[...] = other_ref[...].astype(bf16)

    def half(k):
        return pl.BlockSpec(
            (rows, blk), lambda j, me_ref: (0, (me_ref[0] ^ k) % 2 * (width // blk) + j)
        )

    plain = pl.BlockSpec((rows, blk), lambda j, me_ref: (0, j))
    return pl.pallas_call(
        body,
        out_shape=[jax.ShapeDtypeStruct((rows, width), bf16)] * 2,
        grid_spec=pltpu.PrefetchScalarGridSpec(
            num_scalar_prefetch=1,
            grid=(width // blk,),
            in_specs=[half(0), half(1)],
            out_specs=[plain] * 2,
        ),
        compiler_params=params(16),
        cost_estimate=cost(0, rows * width * 8),
    )(me, x, x)


def pack_targets(me, theirs, targets, cap, width, blk):
    rows = targets.shape[0]

    def body(me_ref, their_ref, mine_ref, other_ref, mine_out, other_out):
        local = iota((cap, rows), 1) + me_ref[0] * rows
        pick = one_hot(their_ref[:cap, 126:127] == local)
        mine_out[...] = dot_nn(pick, mine_ref[...]).astype(bf16)
        other_out[...] = dot_nn(pick, other_ref[...]).astype(bf16)

    def half(k):
        return pl.BlockSpec(
            (rows, blk), lambda j, me_ref: (0, (me_ref[0] ^ k) % 2 * (width // blk) + j)
        )

    plain = pl.BlockSpec((cap, blk), lambda j, me_ref: (0, j))
    return pl.pallas_call(
        body,
        out_shape=[jax.ShapeDtypeStruct((cap, width), bf16)] * 2,
        grid_spec=pltpu.PrefetchScalarGridSpec(
            num_scalar_prefetch=1,
            grid=(width // blk,),
            in_specs=[whole, half(0), half(1)],
            out_specs=[plain] * 2,
        ),
        compiler_params=params(16),
        cost_estimate=cost(2 * cap * rows * width, rows * width * 8),
    )(me, theirs, targets, targets)


def build_maps(me, points, sib_points, norms_in, q_half, q_other, inverses, slots, theirs):
    rows, feats = points.shape
    half_f = feats // 2
    total = slots.shape[1]
    blk = total // 2
    step = min(256, rows, blk)
    scale = -(2.0 / feats)

    def body(
        me_ref, own_ref, sib_ref, pn_ref, qh_ref, qo_ref, inv_ref, idr_ref, idc_ref,
        left_ref, rest_ref, rows_ref, along_ref, norm_ref,
    ):
        mine = pl.ds(pl.multiple_of(me_ref[0] % 2 * half_f, 128), half_f)
        other = pl.ds(pl.multiple_of((1 - me_ref[0] % 2) * half_f, 128), half_f)
        for r in range(0, total, step):
            part = square_sums(qh_ref[r : r + step, :]) + square_sums(qo_ref[r : r + step, :])
            norm_ref[r : r + step, :] = jnp.broadcast_to(part, (step, 128))
        norms = jnp.transpose(norm_ref[...])[0:1, :]

        def values(a, b, a_sq, b_sq, same):
            inner = dot_nt(a[0], b[0]) + dot_nt(a[1], b[1])
            sq_dist = jnp.maximum(a_sq + b_sq - 2.0 * inner, 0.0)
            k = jnp.exp(scale * sq_dist).astype(bf16).astype(f32)
            return (k + jnp.where(same, ridge_weight, 0.0)).astype(bf16)

        cross = []
        for r in range(blk, total, step):
            at = slice(r, r + step)
            cross.append(
                values(
                    (qh_ref[at, :], qo_ref[at, :]),
                    (qh_ref[:blk, :], qo_ref[:blk, :]),
                    norm_ref[at, 0:1],
                    norms[:, :blk],
                    idc_ref[at, 127:128] == idr_ref[7:8, :blk],
                )
            )
        cross = jnp.concatenate(cross, axis=0)
        inv0, inv1 = inv_ref[0], inv_ref[1]
        high0, low0 = split_bf16(inv0)
        high1, low1 = split_bf16(inv1)
        high, low = split_bf16(dot_nn(cross, high0) + dot_nn(cross, low0))
        lower = -(dot_nn(high1, high) + dot_nn(high1, low) + dot_nn(low1, high))

        bell = jnp.exp(-scale * (jnp.min(norms) - norms))

        def direction(inv, weights):
            way = jnp.sum(inv * weights, axis=1, keepdims=True)
            return way * lax.rsqrt(jnp.maximum(jnp.sum(way * way), 1e-30))

        way0 = direction(inv0, bell[:, :blk])
        way1 = direction(inv1, bell[:, blk:])
        row00 = jnp.sum(way0 * inv0, axis=0, keepdims=True)
        row10 = jnp.sum(way1 * lower, axis=0, keepdims=True)
        row11 = jnp.sum(way1 * inv1, axis=0, keepdims=True)
        rest_ref[:blk, :blk] = (inv0 - way0 * row00).astype(bf16)
        rest_ref[:blk, blk:] = jnp.zeros((blk, blk), bf16)
        rest_ref[blk:, :blk] = (lower - way1 * row10).astype(bf16)
        rest_ref[blk:, blk:] = (inv1 - way1 * row11).astype(bf16)
        rows_ref[...] = jnp.zeros((8, total), f32)
        rows_ref[0:1, :blk] = row00
        rows_ref[1:2, :blk] = row10
        rows_ref[1:2, blk:] = row11
        along_ref[...] = jnp.zeros((8, total), f32)
        along_ref[0:1, :blk] = as_row(way0)
        along_ref[1:2, blk:] = as_row(way1)

        for which, ref in enumerate((own_ref, sib_ref)):
            for r in range(0, rows, step):
                at = slice(r, r + step)
                a = (ref[at, mine], ref[at, other])
                spot = (me_ref[0] ^ which) * rows + r + iota((step, total), 0)
                left_ref[which * rows + r : which * rows + r + step, :] = -values(
                    a,
                    (qh_ref[...], qo_ref[...]),
                    pn_ref[which * rows + r : which * rows + r + step, 0:1],
                    norms,
                    spot == idr_ref[7:8, :],
                )

    return pl.pallas_call(
        body,
        out_shape=[
            jax.ShapeDtypeStruct((2 * rows, total), bf16),
            jax.ShapeDtypeStruct((total, total), bf16),
            jax.ShapeDtypeStruct((8, total), f32),
            jax.ShapeDtypeStruct((8, total), f32),
        ],
        in_specs=[pl.BlockSpec(memory_space=pltpu.SMEM)] + [whole] * 8,
        out_specs=[whole] * 4,
        scratch_shapes=[pltpu.VMEM((total, 128), f32)],
        compiler_params=params(24),
        cost_estimate=cost(4 * rows * total * feats, 12 << 20),
    )(me, points, sib_points, norms_in, q_half, q_other, inverses, slots, theirs)


def map_weights(lo, count, extra, slots, pos_row, rest, left, rows_along, cap):
    points, total = left.shape

    def fill(slots_ref, rest_ref, left_ref, along_ref, weights):
        sel = one_hot(slots_ref[pos_row : pos_row + 1, :] == lo + iota((count, total), 0))
        moved = dot_nn(sel, rest_ref[...]).astype(bf16)
        if extra:
            moved = jnp.concatenate([moved, both_parts(along_ref[...])], axis=0)
        pack = one_hot(iota((cap, total), 0) == slots_ref[0:1, :])
        for at, other in ((slice(0, points), left_ref[...]), (slice(points, points + cap), pack)):
            mapped = dot_nt(moved, other)
            weights[:count, at] = mapped[:count].astype(bf16)
            if extra:
                both = mapped[count : count + 8] + mapped[count + 8 :]
                weights[count:, at] = both_parts(both)

    if extra:
        return fill

    def body(slots_ref, rest_ref, left_ref, out_ref):
        fill(slots_ref, rest_ref, left_ref, None, out_ref)

    return pl.pallas_call(
        body,
        out_shape=jax.ShapeDtypeStruct((count, points + cap), bf16),
        in_specs=[whole] * 3,
        out_specs=whole,
        compiler_params=params(20),
        cost_estimate=cost(count * (2 * points + cap) * total, 6 << 20),
    )(slots, rest, left)


def strips_of(bands):
    return [(k, min(k + 512, end)) for at, end in bands for k in range(at, end, 512)]


def strip_of(refs, at, end):
    targets = refs[2][:, at:end] + refs[3][:, at:end]
    return jnp.concatenate([refs[0][:, at:end], refs[1][:, at:end], targets], axis=0)


def first_shares(piece, bands, slots, pos_row, rest, left, rows_along, parts):
    width, cap = parts[0].shape[1], parts[-1].shape[0]
    height, depth = piece + 16, left.shape[0] + cap
    fill = map_weights(0, piece, True, slots, pos_row, rest, left, rows_along, cap)

    def body(slots_ref, rest_ref, left_ref, along_ref, *refs):
        part_refs, refs = refs[: len(parts)], refs[len(parts) :]
        amount_ref, band_refs, weights = refs[0], refs[1:-1], refs[-1]
        fill(slots_ref, rest_ref, left_ref, along_ref, weights)
        for at, end in strips_of(bands):
            out = dot_nn(weights[...], strip_of(part_refs, at, end))
            amount_ref[:, at:end] = out[piece : piece + 8] + out[piece + 8 :]
            for band, ref in zip(bands, band_refs):
                if band[0] <= at < band[1]:
                    strip = slice(at - band[0], end - band[0])
                    ref[:piece, strip] = out[:piece].astype(bf16)
                    ref[piece:, strip] = both_parts(out[piece : piece + 8] + out[piece + 8 :])

    out_shape = [jax.ShapeDtypeStruct((8, width), f32)]
    out_shape += [jax.ShapeDtypeStruct((piece + 16, end - at), bf16) for at, end in bands]
    return pl.pallas_call(
        body,
        out_shape=out_shape,
        in_specs=[whole] * (4 + len(parts)),
        out_specs=[whole] * len(out_shape),
        scratch_shapes=[pltpu.VMEM((height, depth), bf16)],
        compiler_params=params(20),
        cost_estimate=cost(height * depth * (width + 1024), 12 << 20),
    )(slots, rest, left, rows_along, *parts)


def more_shares(me, weights, lo, count, bands, parts):
    depth, width = weights.shape[1], parts[0].shape[1]

    def body(me_ref, weights_ref, *refs):
        for at, end in strips_of(bands):
            strip = strip_of(refs, at, end)
            refs[-1][:, at:end] = dot_nn(weights_ref[lo : lo + count, :], strip)

    return pl.pallas_call(
        body,
        out_shape=jax.ShapeDtypeStruct((count, width), f32),
        in_specs=[pl.BlockSpec(memory_space=pltpu.SMEM)] + [whole] * (1 + len(parts)),
        out_specs=whole,
        compiler_params=params(16),
        cost_estimate=cost(count * depth * width, 10 << 20),
    )(me, weights, *parts)


def add_arrived(me, share, row, band, shift, arrived, carry):
    piece, length = shift.shape
    n = len(arrived)

    def body(me_ref, share_ref, shift_ref, *refs):
        out = share_ref[row : row + piece, band[0] : band[1]]
        for k, ref in enumerate(refs[:-1]):
            at = length - (n - k) * piece
            out += dot_nn(shift_ref[:, at : at + piece], ref[:piece, :])
        refs[-1][:piece, :] = out.astype(bf16)
        if carry:
            refs[-1][piece:, :] = refs[-2][piece:, :]

    height = piece + (16 if carry else 0)
    return pl.pallas_call(
        body,
        out_shape=jax.ShapeDtypeStruct((height, band[1] - band[0]), bf16),
        in_specs=[pl.BlockSpec(memory_space=pltpu.SMEM)] + [whole] * (2 + n),
        out_specs=whole,
        compiler_params=params(12),
        cost_estimate=cost(n * piece * piece * (band[1] - band[0]), 6 << 20),
    )(me, share, shift, *arrived)


def sum_amounts(me, amount, bands, arrived):
    piece = arrived[0][0].shape[0] - 16

    def body(me_ref, amount_ref, *refs):
        out_ref, refs = refs[-1], list(refs[:-1])
        for (at, end), pieces in zip(bands, arrived):
            out = amount_ref[:, at:end]
            for _ in pieces:
                both = refs.pop(0)[piece:, :].astype(f32)
                out += both[:8] + both[8:]
            out_ref[:, at:end] = out

    return pl.pallas_call(
        body,
        out_shape=jax.ShapeDtypeStruct(amount.shape, f32),
        in_specs=[pl.BlockSpec(memory_space=pltpu.SMEM)] + [whole] * (1 + sum(map(len, arrived))),
        out_specs=whole,
        compiler_params=params(12),
        cost_estimate=cost(0, 2 << 20),
    )(me, amount, *[ref for pieces in arrived for ref in pieces])


def final_maps(me, slots, along, spots, rows):
    total, n = slots.shape[1], spots.shape[1]

    def body(me_ref, slots_ref, along_ref, spots_ref, sel_ref, scale_ref):
        first = me_ref[0] * rows
        sel_ref[...] = one_hot(first + iota((rows, n), 0) == spots_ref[...])
        same = first + iota((rows, total), 0) == slots_ref[7:8, :]
        scale_ref[...] = jnp.zeros((rows, 128), f32)
        for b in range(2):
            weight = jnp.where(same, along_ref[b : b + 1, :], 0.0)
            scale_ref[:, b : b + 1] = jnp.sum(weight, axis=1, keepdims=True)

    return pl.pallas_call(
        body,
        out_shape=[jax.ShapeDtypeStruct((rows, n), bf16), jax.ShapeDtypeStruct((rows, 128), f32)],
        in_specs=[pl.BlockSpec(memory_space=pltpu.SMEM)] + [whole] * 3,
        out_specs=[whole] * 2,
        compiler_params=params(16),
        cost_estimate=cost(1 << 20, 3 << 20),
    )(me, slots, along, spots)


def add_early(me, other, coeffs, sel, scale, amount, pieces, width, band, blk):
    rows = coeffs.shape[0]
    n, piece = len(pieces), pieces[0].shape[0]
    per_half, at, count = width // blk, band[0] // blk, (band[1] - band[0]) // blk

    def body(me_ref, src_ref, sel_ref, scale_ref, amount_ref, *refs):
        strip = jnp.concatenate([ref[...] for ref in refs[:-1]], axis=0)
        out = src_ref[...] + dot_nn(sel_ref[:, : n * piece], strip)
        for b in range(2):
            out += scale_ref[:, b : b + 1] * amount_ref[b : b + 1, :]
        refs[-1][...] = out

    def source(j, me_ref):
        return 0, (me_ref[0] ^ other) % 2 * per_half + at + j

    plain = pl.BlockSpec((piece, blk), lambda j, me_ref: (0, j))
    return pl.pallas_call(
        body,
        out_shape=jax.ShapeDtypeStruct((rows, count * blk), f32),
        grid_spec=pltpu.PrefetchScalarGridSpec(
            num_scalar_prefetch=1,
            grid=(count,),
            in_specs=[
                pl.BlockSpec((rows, blk), source),
                whole,
                whole,
                pl.BlockSpec((8, blk), lambda j, me_ref: (0, at + j)),
                *[plain] * n,
            ],
            out_specs=pl.BlockSpec((rows, blk), lambda j, me_ref: (0, j)),
        ),
        compiler_params=params(12),
        cost_estimate=cost(rows * n * piece * count * blk, rows * count * blk * 8),
    )(me, coeffs, sel, scale, amount, *pieces)


def add_last(me, early, cols, buffer, sel, mine, sib, width, band, blk):
    rows = sel.shape[0]
    n, piece = len(mine), mine[0].shape[0]
    per_half, at, count = width // blk, band[0] // blk, (band[1] - band[0]) // blk

    def body(me_ref, sel_ref, early_mine, early_sib, *refs):
        j = pl.program_id(0)
        cut = pl.ds(pl.multiple_of(j % count * blk, 128), blk)

        def finish(early_ref, parts):
            strip = jnp.concatenate([ref[:, cut] for ref in parts], axis=0)
            chosen = sel_ref[:, sel_ref.shape[1] - n * piece :]
            refs[-1][...] = early_ref[:, cut] + dot_nn(chosen, strip)

        inside = j // count == me_ref[0] % 2
        pl.when(inside)(lambda: finish(early_mine, refs[:n]))
        pl.when(jnp.logical_not(inside))(lambda: finish(early_sib, refs[n : 2 * n]))

    spread = pl.BlockSpec((rows, blk), lambda j, me_ref: (0, j // count * per_half + at + j % count))
    operands = [sel, *early, *mine, *sib]
    in_specs = [whole] * len(operands)
    aliases = {}
    if buffer is not None:
        aliases = {1 + len(operands): 0}
        operands.append(buffer)
        in_specs.append(pl.BlockSpec(memory_space=pl.ANY))
    return pl.pallas_call(
        body,
        out_shape=pltpu.HBM((rows, cols), f32),
        grid_spec=pltpu.PrefetchScalarGridSpec(
            num_scalar_prefetch=1, grid=(2 * count,), in_specs=in_specs, out_specs=spread
        ),
        input_output_aliases=aliases,
        compiler_params=params(12),
        cost_estimate=cost(rows * n * piece * 2 * count * blk, rows * 2 * count * blk * 8),
    )(me, *operands)


def solution(mesh):
    n = mesh.shape["rows"]
    chips = n // 2
    bits = chips.bit_length() - 1
    ring = [k ^ (k >> 1) for k in range(chips)]
    place = [ring.index(k) for k in range(chips)]

    def core_perm(chip_of):
        return [(i, 2 * chip_of(i // 2, i % 2) + i % 2) for i in range(n)]

    sib_perm = [(i, i ^ 1) for i in range(n)]
    ring_perm = core_perm(
        lambda chip, core: ring[(place[chip] + (1 if core == 0 else chips - 1)) % chips]
    )

    def stage_bit(stage, core):
        return 1 << (stage if core == 0 else bits - 1 - stage)

    def to_sib(x):
        return lax.ppermute(x, "rows", sib_perm)

    def stage_cap(total, stage):
        return min(total, total // 2 + ((1 << stage) - 1) * (total // chips))

    def spread_path(points, targets, coeffs, inverses, pts_sib, me, slots, theirs, spots, shift):
        rows_here, feats = points.shape
        cols = coeffs.shape[1]
        half_f = feats // 2
        extra_cols = -cols % 256
        if extra_cols:
            targets = jnp.pad(targets, ((0, 0), (0, extra_cols)))
            coeffs = jnp.pad(coeffs, ((0, 0), (0, extra_cols)))
        width = (cols + extra_cols) // 2
        blk = 128 * max(d for d in (1, 2, 3, 4) if width // 128 % d == 0)
        total = slots.shape[1]
        piece = total // (2 * chips)
        steps = 2 * chips - 1

        blocks = width // blk
        first = (blocks + 1) // 2 * blk
        bands = [(0, first), (first, width)] if first < width else [(0, width)]

        caps = [stage_cap(total, stage) for stage in range(bits)]
        sent = pick_points(me, theirs, points, pts_sib, half_f, caps[0])
        for stage in range(bits):
            got = lax.ppermute(
                sent, "rows", core_perm(lambda k, c, s=stage: k ^ stage_bit(s, c))
            )
            if stage == 0:
                wide = 128 * max(d for d in range(1, 9) if width // 128 % d == 0)
                t_mine, t_other = pack_targets(
                    after(me, sent), theirs, targets, caps[0], width, wide
                )
                t_sib = to_sib(t_other)
                got = after(got, t_other)
            if stage < bits - 1:
                sent = append_rows(sent, got, theirs, stage, caps[stage + 1])
        c_mine, c_other = cut_columns(after(me, sent), coeffs, width, blk)
        placed = place_rows(sent, theirs, bits - 1)
        norms = point_norms(after(points, placed), pts_sib)
        block_half = place_rows(after(got, norms, c_other), theirs, bits, placed)
        block_other = to_sib(block_half)
        c_sib = to_sib(after(c_other, block_other))
        parts = [c_mine, c_sib, t_mine, t_sib]

        left, rest, rows_along, along = build_maps(
            me, points, pts_sib, norms, block_half, block_other, inverses, slots,
            theirs,
        )

        amount, *first_sent = first_shares(
            piece, bands, slots, bits, rest, left, rows_along, parts
        )
        share = {}
        arrived = [[] for _ in bands]
        final = [[] for _ in bands]
        final_sib = [[] for _ in bands]
        early_mine, early_sib = [], []
        early = steps - chips
        fillers = []
        latest = None

        def exchange(b, latest):
            for part in final[b][len(final_sib[b]) :]:
                final_sib[b].append(to_sib(after(part, latest)))

        def early_of(other, b, amounts, pieces, me_then):
            return add_early(
                me_then, other, coeffs, sel, scale, amounts, pieces[b][:early], width, bands[b], blk
            )

        for step in range(steps + 1):
            for b, band in enumerate(bands):
                if step == 0:
                    sent = first_sent[b]
                else:
                    arrived[b][-1] = after(arrived[b][-1], latest, *fillers)
                    fillers = []
                    sent = add_arrived(
                        me, *share[step], band, shift, arrived[b][-chips:], step < chips - 1
                    )
                latest = sent
                if step < steps:
                    arrived[b].append(lax.ppermute(sent, "rows", ring_perm))
                if step >= chips - 1:
                    final[b].append(sent)
                if step == steps:
                    exchange(b, latest)
                    if b == 0:
                        fillers += early_sib[1:]
            row = 2 * step + 1
            if row < 2 * chips:
                count = min(2, 2 * chips - row)
                weights = map_weights(
                    row * piece, count * piece, False, after(slots, latest), bits, rest, left,
                    None, caps[0],
                )
                more = more_shares(after(me, latest), weights, 0, count * piece, bands, parts)
                for k in range(count):
                    share[row + k] = (more, k * piece)
                fillers.append(more)
            if step == chips - 1:
                carried = [pieces[: chips - 1] for pieces in arrived]
                amount = sum_amounts(after(me, latest), amount, bands, carried)
                sel, scale = final_maps(after(me, latest), slots, along, spots, rows_here)
                fillers += [amount, scale]
            b = step - (steps - 2)
            if 0 <= b < len(bands):
                early_mine.append(early_of(0, b, amount, final, after(me, latest)))
                fillers.append(early_mine[-1])
            if step == steps - 1:
                amount_sib = to_sib(after(amount, early_mine[-1]))
                for b in range(len(bands)):
                    exchange(b, early_mine[-1])
                for b in range(len(bands)):
                    early_sib.append(early_of(1, b, amount_sib, final_sib, me))
                fillers.append(early_sib[0])

        out = None
        for b, band in enumerate(bands):
            out = add_last(
                me, (early_mine[b], early_sib[b]), cols + extra_cols, out, sel,
                final[b][early:], final_sib[b][early:], width, band, blk,
            )
        return out[:, :cols] if extra_cols else out

    def per_device(points, targets, coeffs, block_ids, inverses):
        rows_here = points.shape[0]
        total = block_ids.size
        me = lax.axis_index("rows").astype(i32).reshape(1)
        pts_sib = to_sib(points)
        stage_bits = [[stage_bit(s, core) for s in range(bits)] for core in range(2)]
        caps = [stage_cap(total, s) for s in range(bits)]
        fits, *plans = plan(me, block_ids, rows_here, ring, stage_bits, caps)
        out = spread_path(points, targets, coeffs, inverses, pts_sib, me, *plans)

        def general(state):
            return jnp.ones_like(fits), general_path(points, targets, coeffs, block_ids, inverses)

        return lax.while_loop(lambda state: state[0][0] == 0, general, (fits, out))[1]

    return jax.shard_map(
        per_device,
        mesh=mesh,
        in_specs=(P("rows", None), P("rows", "labels"), P("rows", "labels"), P(), P()),
        out_specs=P("rows", "labels"),
        check_vma=False,
    )
```

```python
import jax
import jax.numpy as jnp
from jax import lax
from jax.experimental import pallas as pl
from jax.experimental.pallas import tpu as pltpu
from jax.sharding import PartitionSpec as P

ridge_weight = 0.5
bf16 = jnp.bfloat16
f32 = jnp.float32
i32 = jnp.int32
whole = pl.BlockSpec(memory_space=pltpu.VMEM)


def dot_nn(a, b):
    return lax.dot_general(a, b, (((1,), (0,)), ((), ())), preferred_element_type=f32)


def dot_nt(a, b):
    return lax.dot_general(a, b, (((1,), (1,)), ((), ())), preferred_element_type=f32)


def square_sums(pts):
    return jnp.sum(jnp.square(pts.astype(f32)), axis=1, keepdims=True)


def kernel_tile(left, right):
    inner_prod = dot_nt(left, right)
    sq_dist = jnp.maximum(square_sums(left) + square_sums(right).T - 2.0 * inner_prod, 0.0)
    return jnp.exp(-(2.0 / left.shape[1]) * sq_dist).astype(bf16)


def split_bf16(x):
    high = x.astype(bf16)
    return high, (x - high.astype(f32)).astype(bf16)


def both_parts(x):
    high, low = split_bf16(x)
    return jnp.concatenate([high.astype(f32), low.astype(f32)], axis=0).astype(bf16)


def as_row(column):
    n = column.shape[0]
    return jnp.transpose(jnp.broadcast_to(column, (n, 128)))[0:1, :]


def iota(shape, dim):
    return lax.broadcasted_iota(i32, shape, dim)


def one_hot(cond):
    return jnp.where(cond, 1.0, 0.0).astype(bf16)


def after(x, *others):
    return lax.optimization_barrier((x, *others))[0]


def params(megabytes):
    return pltpu.CompilerParams(vmem_limit_bytes=megabytes << 20)


def cost(macs, bytes_accessed):
    return pl.CostEstimate(flops=2 * macs, bytes_accessed=bytes_accessed, transcendentals=0)


def ring_sum(x, n):
    def hop(_, state):
        total, moving = state
        moving = lax.ppermute(moving, "rows", [(i, (i + 1) % n) for i in range(n)])
        return total + moving, moving

    return lax.fori_loop(0, n - 1, hop, (x, x))[0]


def general_path(n, points, targets, coeffs, block_ids, inverses):
    rows_here = points.shape[0]
    first_row = lax.axis_index("rows") * rows_here
    zero_low = jnp.zeros((), bf16)
    current = coeffs
    for blk in range(2):
        local_ids = block_ids[blk] - first_row
        inside = (local_ids >= 0) & (local_ids < rows_here)
        local_rows = jnp.clip(local_ids, 0, rows_here - 1)
        picked = jnp.where(inside[:, None], points[local_rows], zero_low)
        block_pts = ring_sum(picked, n)
        ktile = kernel_tile(points, block_pts)
        c_low = current.astype(bf16)
        sel_targets = jnp.where(inside[:, None], targets[local_rows].astype(f32), 0.0)
        sel_coeffs = jnp.where(inside[:, None], current[local_rows], 0.0)
        local_side = ridge_weight * sel_coeffs - sel_targets
        product = lax.dot_general(
            ktile, c_low, (((0,), (0,)), ((), ())), preferred_element_type=f32
        )
        negated = ring_sum(product + local_side, n)
        update = jnp.dot(
            inverses[blk], -negated, precision=lax.Precision.HIGHEST, preferred_element_type=f32
        )
        where_to = (jnp.arange(rows_here, dtype=i32)[:, None] == local_ids[None, :]).astype(f32)
        current = current + jnp.dot(
            where_to, update, precision=lax.Precision.HIGHEST, preferred_element_type=f32
        )
    return current


def plan(me, block_ids, rows, ring, stage_bits, caps):
    total = block_ids.size
    blk = block_ids.shape[1]
    chips = len(ring)
    place = [ring.index(k) for k in range(chips)]
    piece = total // (2 * chips)
    bits = len(caps)
    n_final = total - (chips - 1) * piece
    step = min(256, total)
    groups = []
    for core in range(2):
        done = 0
        for stage in range(bits):
            members = {}
            for k in range(chips):
                members.setdefault(k & ~done, []).append(k)
            groups += [(m, caps[stage]) for m in members.values()]
            done |= stage_bits[core][stage]

    def body(me_ref, ids_ref, flag_ref, slots_ref, their_ref, spots_ref, shift_ref):
        chip, core = me_ref[0] // 2, me_ref[0] % 2
        ids = jnp.concatenate([ids_ref[0:1, :], ids_ref[1:2, :]], axis=1).astype(f32)
        ids_col = jnp.transpose(jnp.broadcast_to(ids, (128, total)))
        own = jnp.floor((ids + 0.5) * (0.5 / rows))
        index = iota((1, total), 1)
        rank = jnp.zeros((1, total), f32)
        for r in range(0, total, step):
            own_col = jnp.floor((ids_col[r : r + step, 0:1] + 0.5) * (0.5 / rows))
            ahead = (own_col == own) & (r + iota((step, total), 0) < index)
            rank += jnp.sum(jnp.where(ahead, 1.0, 0.0), axis=0, keepdims=True)

        def count(which):
            return jnp.sum(jnp.where(own == which, 1.0, 0.0), axis=1, keepdims=True)

        def slots(listed):
            slot = jnp.full((1, total), -1.0, f32)
            before = jnp.zeros((1, 1), f32)
            for which in listed:
                which = which.astype(f32)
                slot = jnp.where(own == which, before + rank, slot)
                before = before + count(which)
            return slot

        counts = [count(float(k)) for k in range(chips)]
        slack = counts[0] - piece
        for k in range(1, chips):
            slack = jnp.minimum(slack, counts[k] - piece)
        for members, cap in groups:
            slack = jnp.minimum(slack, cap - sum(counts[k] for k in members))
        flag_ref[0] = (jnp.max(slack) >= 0.0).astype(i32)

        slots_ref[...] = jnp.zeros(slots_ref.shape, i32)
        group = [0]
        columns = []
        for stage in range(bits):
            bit = jnp.where(core == 0, stage_bits[0][stage], stage_bits[1][stage])
            mine = slots([chip ^ g for g in group])
            if stage == 0:
                slots_ref[0:1, :] = mine.astype(i32)
                line = iota((caps[0], total), 0).astype(f32)
                wanted = jnp.where(mine == line, ids + 1.0, 0.0)
                wanted = jnp.sum(wanted, axis=1, keepdims=True) - 1.0
            if stage == bits - 1:
                columns += [mine, slots([chip ^ bit ^ g for g in group])]
            else:
                held = sum(count((chip ^ g).astype(f32)) for g in group)
                columns.append(jnp.broadcast_to(held, (1, total)))
            group = group + [g ^ bit for g in group]
        slots_ref[7:8, :] = ids.astype(i32)
        fill = jnp.zeros((127 - len(columns), total), f32)
        columns = jnp.concatenate(columns + [fill, ids], axis=0)
        their_ref[...] = jnp.transpose(columns).astype(i32)
        their_ref[: caps[0], 126:127] = wanted.astype(i32)

        def lookup(which, table):
            out = jnp.int32(table[0])
            for k in range(1, chips):
                out = jnp.where(which == k, table[k], out)
            return out

        here = lookup(chip, place)
        way = jnp.where(core == 0, chips - 1, 1)
        listed = [lookup((here + way * (k + 1)) % chips, ring) for k in range(chips)]
        position = slots(listed)
        slots_ref[bits : bits + 1, :] = position.astype(i32)
        lag = count(listed[0].astype(f32)).astype(i32)
        length = (2 * chips - 1) * piece
        source = iota((piece, length), 0) - lag + length
        shift_ref[...] = one_hot(source == iota((piece, length), 1))
        pos_col = jnp.transpose(jnp.broadcast_to(position, (128, total)))[:, 0:1]
        line = ((chips - 1) * piece + iota((1, n_final), 1)).astype(f32)
        spots = jnp.sum(
            jnp.where(pos_col == line, ids_col[:, 0:1], 0.0), axis=0, keepdims=True
        )
        spots_ref[...] = spots.astype(i32)

    smem = pl.BlockSpec(memory_space=pltpu.SMEM)
    return pl.pallas_call(
        body,
        out_shape=[
            jax.ShapeDtypeStruct((1,), i32),
            jax.ShapeDtypeStruct((8, total), i32),
            jax.ShapeDtypeStruct((total, 128), i32),
            jax.ShapeDtypeStruct((1, n_final), i32),
            jax.ShapeDtypeStruct((piece, total - piece), bf16),
        ],
        in_specs=[smem, whole],
        out_specs=[smem, whole, whole, whole, whole],
        compiler_params=params(16),
        cost_estimate=cost(1 << 20, 1 << 20),
    )(me, block_ids)


def pick_points(me, theirs, points, sib_points, half_f, cap):
    rows = points.shape[0]

    def body(me_ref, their_ref, own_ref, sib_ref, sent_ref):
        cols = pl.ds(pl.multiple_of(me_ref[0] % 2 * half_f, 128), half_f)
        wanted = their_ref[:cap, 126:127]
        local = iota((cap, rows), 1)
        own = one_hot(wanted == local + me_ref[0] * rows)
        sib = one_hot(wanted == local + (me_ref[0] ^ 1) * rows)
        out = dot_nn(own, own_ref[:, cols]) + dot_nn(sib, sib_ref[:, cols])
        sent_ref[...] = out.astype(bf16)

    return pl.pallas_call(
        body,
        out_shape=jax.ShapeDtypeStruct((cap, half_f), bf16),
        in_specs=[pl.BlockSpec(memory_space=pltpu.SMEM)] + [whole] * 3,
        out_specs=whole,
        compiler_params=params(16),
        cost_estimate=cost(2 * cap * rows * half_f, 4 << 20),
    )(me, theirs, points, sib_points)


def append_rows(sent, got, theirs, stage, cap_next):
    cap, half_f = sent.shape

    def body(sent_ref, got_ref, their_ref, out_ref):
        held = their_ref[:cap_next, stage : stage + 1]
        behind = one_hot(iota((cap_next, cap), 0) - held == iota((cap_next, cap), 1))
        out = dot_nn(behind, got_ref[...])
        out_ref[:cap, :] = (out[:cap] + sent_ref[...].astype(f32)).astype(bf16)
        if cap_next > cap:
            out_ref[cap:, :] = out[cap:].astype(bf16)

    return pl.pallas_call(
        body,
        out_shape=jax.ShapeDtypeStruct((cap_next, half_f), bf16),
        in_specs=[whole] * 3,
        out_specs=whole,
        compiler_params=params(16),
        cost_estimate=cost(cap * cap_next * half_f, 4 << 20),
    )(sent, got, theirs)


def place_rows(packed, theirs, column, block=None):
    cap, half_f = packed.shape
    total = theirs.shape[0]

    def body(packed_ref, their_ref, *refs):
        spots = one_hot(their_ref[:, column : column + 1] == iota((total, cap), 1))
        out = dot_nn(spots, packed_ref[...])
        if block is not None:
            out += refs[0][...].astype(f32)
        refs[-1][...] = out.astype(bf16)

    return pl.pallas_call(
        body,
        out_shape=jax.ShapeDtypeStruct((total, half_f), bf16),
        in_specs=[whole] * (2 if block is None else 3),
        out_specs=whole,
        compiler_params=params(16),
        cost_estimate=cost(total * cap * half_f, 4 << 20),
    )(packed, theirs, *([] if block is None else [block]))


def point_norms(points, sib_points):
    rows = points.shape[0]

    def body(own_ref, sib_ref, out_ref):
        for k, ref in enumerate((own_ref, sib_ref)):
            norm = square_sums(ref[...])
            out_ref[k * rows : (k + 1) * rows, :] = jnp.broadcast_to(norm, (rows, 128))

    return pl.pallas_call(
        body,
        out_shape=jax.ShapeDtypeStruct((2 * rows, 128), f32),
        in_specs=[whole] * 2,
        out_specs=whole,
        compiler_params=params(16),
        cost_estimate=cost(4 << 20, 3 << 20),
    )(points, sib_points)


def cut_columns(me, x, width, blk):
    rows = x.shape[0]

    def body(me_ref, mine_ref, other_ref, mine_out, other_out):
        mine_out[...] = mine_ref[...].astype(bf16)
        other_out[...] = other_ref[...].astype(bf16)

    def half(k):
        return pl.BlockSpec(
            (rows, blk), lambda j, me_ref: (0, (me_ref[0] ^ k) % 2 * (width // blk) + j)
        )

    plain = pl.BlockSpec((rows, blk), lambda j, me_ref: (0, j))
    return pl.pallas_call(
        body,
        out_shape=[jax.ShapeDtypeStruct((rows, width), bf16)] * 2,
        grid_spec=pltpu.PrefetchScalarGridSpec(
            num_scalar_prefetch=1,
            grid=(width // blk,),
            in_specs=[half(0), half(1)],
            out_specs=[plain] * 2,
        ),
        compiler_params=params(16),
        cost_estimate=cost(0, rows * width * 8),
    )(me, x, x)


def pack_targets(me, theirs, targets, cap, width, blk):
    rows = targets.shape[0]

    def body(me_ref, their_ref, mine_ref, other_ref, mine_out, other_out):
        local = iota((cap, rows), 1) + me_ref[0] * rows
        pick = one_hot(their_ref[:cap, 126:127] == local)
        mine_out[...] = dot_nn(pick, mine_ref[...]).astype(bf16)
        other_out[...] = dot_nn(pick, other_ref[...]).astype(bf16)

    def half(k):
        return pl.BlockSpec(
            (rows, blk), lambda j, me_ref: (0, (me_ref[0] ^ k) % 2 * (width // blk) + j)
        )

    plain = pl.BlockSpec((cap, blk), lambda j, me_ref: (0, j))
    return pl.pallas_call(
        body,
        out_shape=[jax.ShapeDtypeStruct((cap, width), bf16)] * 2,
        grid_spec=pltpu.PrefetchScalarGridSpec(
            num_scalar_prefetch=1,
            grid=(width // blk,),
            in_specs=[whole, half(0), half(1)],
            out_specs=[plain] * 2,
        ),
        compiler_params=params(16),
        cost_estimate=cost(2 * cap * rows * width, rows * width * 8),
    )(me, theirs, targets, targets)


def build_maps(me, points, sib_points, norms_in, q_half, q_other, inverses, slots, theirs):
    rows, feats = points.shape
    half_f = feats // 2
    total = slots.shape[1]
    blk = total // 2
    step = min(256, rows, blk)
    scale = -(2.0 / feats)

    def body(
        me_ref, own_ref, sib_ref, pn_ref, qh_ref, qo_ref, inv_ref, idr_ref, idc_ref,
        left_ref, rest_ref, rows_ref, along_ref, norm_ref,
    ):
        mine = pl.ds(pl.multiple_of(me_ref[0] % 2 * half_f, 128), half_f)
        other = pl.ds(pl.multiple_of((1 - me_ref[0] % 2) * half_f, 128), half_f)
        for r in range(0, total, step):
            part = square_sums(qh_ref[r : r + step, :]) + square_sums(qo_ref[r : r + step, :])
            norm_ref[r : r + step, :] = jnp.broadcast_to(part, (step, 128))
        norms = jnp.transpose(norm_ref[...])[0:1, :]

        def values(a, b, a_sq, b_sq, same):
            inner = dot_nt(a[0], b[0]) + dot_nt(a[1], b[1])
            sq_dist = jnp.maximum(a_sq + b_sq - 2.0 * inner, 0.0)
            k = jnp.exp(scale * sq_dist).astype(bf16).astype(f32)
            return (k + jnp.where(same, ridge_weight, 0.0)).astype(bf16)

        cross = []
        for r in range(blk, total, step):
            at = slice(r, r + step)
            cross.append(
                values(
                    (qh_ref[at, :], qo_ref[at, :]),
                    (qh_ref[:blk, :], qo_ref[:blk, :]),
                    norm_ref[at, 0:1],
                    norms[:, :blk],
                    idc_ref[at, 127:128] == idr_ref[7:8, :blk],
                )
            )
        cross = jnp.concatenate(cross, axis=0)
        inv0, inv1 = inv_ref[0], inv_ref[1]
        high0, low0 = split_bf16(inv0)
        high1, low1 = split_bf16(inv1)
        high, low = split_bf16(dot_nn(cross, high0) + dot_nn(cross, low0))
        lower = -(dot_nn(high1, high) + dot_nn(high1, low) + dot_nn(low1, high))

        bell = jnp.exp(-scale * (jnp.min(norms) - norms))

        def direction(inv, weights):
            way = jnp.sum(inv * weights, axis=1, keepdims=True)
            return way * lax.rsqrt(jnp.maximum(jnp.sum(way * way), 1e-30))

        way0 = direction(inv0, bell[:, :blk])
        way1 = direction(inv1, bell[:, blk:])
        row00 = jnp.sum(way0 * inv0, axis=0, keepdims=True)
        row10 = jnp.sum(way1 * lower, axis=0, keepdims=True)
        row11 = jnp.sum(way1 * inv1, axis=0, keepdims=True)
        rest_ref[:blk, :blk] = (inv0 - way0 * row00).astype(bf16)
        rest_ref[:blk, blk:] = jnp.zeros((blk, blk), bf16)
        rest_ref[blk:, :blk] = (lower - way1 * row10).astype(bf16)
        rest_ref[blk:, blk:] = (inv1 - way1 * row11).astype(bf16)
        rows_ref[...] = jnp.zeros((8, total), f32)
        rows_ref[0:1, :blk] = row00
        rows_ref[1:2, :blk] = row10
        rows_ref[1:2, blk:] = row11
        along_ref[...] = jnp.zeros((8, total), f32)
        along_ref[0:1, :blk] = as_row(way0)
        along_ref[1:2, blk:] = as_row(way1)

        for which, ref in enumerate((own_ref, sib_ref)):
            for r in range(0, rows, step):
                at = slice(r, r + step)
                a = (ref[at, mine], ref[at, other])
                spot = (me_ref[0] ^ which) * rows + r + iota((step, total), 0)
                left_ref[which * rows + r : which * rows + r + step, :] = -values(
                    a,
                    (qh_ref[...], qo_ref[...]),
                    pn_ref[which * rows + r : which * rows + r + step, 0:1],
                    norms,
                    spot == idr_ref[7:8, :],
                )

    return pl.pallas_call(
        body,
        out_shape=[
            jax.ShapeDtypeStruct((2 * rows, total), bf16),
            jax.ShapeDtypeStruct((total, total), bf16),
            jax.ShapeDtypeStruct((8, total), f32),
            jax.ShapeDtypeStruct((8, total), f32),
        ],
        in_specs=[pl.BlockSpec(memory_space=pltpu.SMEM)] + [whole] * 8,
        out_specs=[whole] * 4,
        scratch_shapes=[pltpu.VMEM((total, 128), f32)],
        compiler_params=params(24),
        cost_estimate=cost(4 * rows * total * feats, 12 << 20),
    )(me, points, sib_points, norms_in, q_half, q_other, inverses, slots, theirs)


def map_weights(lo, count, extra, slots, pos_row, rest, left, rows_along, cap):
    points, total = left.shape

    def fill(slots_ref, rest_ref, left_ref, along_ref, weights):
        sel = one_hot(slots_ref[pos_row : pos_row + 1, :] == lo + iota((count, total), 0))
        moved = dot_nn(sel, rest_ref[...]).astype(bf16)
        if extra:
            moved = jnp.concatenate([moved, both_parts(along_ref[...])], axis=0)
        pack = one_hot(iota((cap, total), 0) == slots_ref[0:1, :])
        for at, other in ((slice(0, points), left_ref[...]), (slice(points, points + cap), pack)):
            mapped = dot_nt(moved, other)
            weights[:count, at] = mapped[:count].astype(bf16)
            if extra:
                both = mapped[count : count + 8] + mapped[count + 8 :]
                weights[count:, at] = both_parts(both)

    if extra:
        return fill

    def body(slots_ref, rest_ref, left_ref, out_ref):
        fill(slots_ref, rest_ref, left_ref, None, out_ref)

    return pl.pallas_call(
        body,
        out_shape=jax.ShapeDtypeStruct((count, points + cap), bf16),
        in_specs=[whole] * 3,
        out_specs=whole,
        compiler_params=params(20),
        cost_estimate=cost(count * (2 * points + cap) * total, 6 << 20),
    )(slots, rest, left)


def strips_of(bands):
    return [(k, min(k + 512, end)) for at, end in bands for k in range(at, end, 512)]


def strip_of(refs, at, end):
    targets = refs[2][:, at:end] + refs[3][:, at:end]
    return jnp.concatenate([refs[0][:, at:end], refs[1][:, at:end], targets], axis=0)


def first_shares(piece, bands, slots, pos_row, rest, left, rows_along, parts):
    width, cap = parts[0].shape[1], parts[-1].shape[0]
    height, depth = piece + 16, left.shape[0] + cap
    fill = map_weights(0, piece, True, slots, pos_row, rest, left, rows_along, cap)

    def body(slots_ref, rest_ref, left_ref, along_ref, *refs):
        part_refs, refs = refs[: len(parts)], refs[len(parts) :]
        amount_ref, band_refs, weights = refs[0], refs[1:-1], refs[-1]
        fill(slots_ref, rest_ref, left_ref, along_ref, weights)
        for at, end in strips_of(bands):
            out = dot_nn(weights[...], strip_of(part_refs, at, end))
            amount_ref[:, at:end] = out[piece : piece + 8] + out[piece + 8 :]
            for band, ref in zip(bands, band_refs):
                if band[0] <= at < band[1]:
                    strip = slice(at - band[0], end - band[0])
                    ref[:piece, strip] = out[:piece].astype(bf16)
                    ref[piece:, strip] = both_parts(out[piece : piece + 8] + out[piece + 8 :])

    out_shape = [jax.ShapeDtypeStruct((8, width), f32)]
    out_shape += [jax.ShapeDtypeStruct((piece + 16, end - at), bf16) for at, end in bands]
    return pl.pallas_call(
        body,
        out_shape=out_shape,
        in_specs=[whole] * (4 + len(parts)),
        out_specs=[whole] * len(out_shape),
        scratch_shapes=[pltpu.VMEM((height, depth), bf16)],
        compiler_params=params(20),
        cost_estimate=cost(height * depth * (width + 1024), 12 << 20),
    )(slots, rest, left, rows_along, *parts)


def more_shares(me, weights, lo, count, bands, parts):
    depth, width = weights.shape[1], parts[0].shape[1]

    def body(me_ref, weights_ref, *refs):
        for at, end in strips_of(bands):
            strip = strip_of(refs, at, end)
            refs[-1][:, at:end] = dot_nn(weights_ref[lo : lo + count, :], strip)

    return pl.pallas_call(
        body,
        out_shape=jax.ShapeDtypeStruct((count, width), f32),
        in_specs=[pl.BlockSpec(memory_space=pltpu.SMEM)] + [whole] * (1 + len(parts)),
        out_specs=whole,
        compiler_params=params(16),
        cost_estimate=cost(count * depth * width, 10 << 20),
    )(me, weights, *parts)


def add_arrived(me, share, row, band, shift, arrived, carry):
    piece, length = shift.shape
    n = len(arrived)

    def body(me_ref, share_ref, shift_ref, *refs):
        out = share_ref[row : row + piece, band[0] : band[1]]
        for k, ref in enumerate(refs[:-1]):
            at = length - (n - k) * piece
            out += dot_nn(shift_ref[:, at : at + piece], ref[:piece, :])
        refs[-1][:piece, :] = out.astype(bf16)
        if carry:
            refs[-1][piece:, :] = refs[-2][piece:, :]

    height = piece + (16 if carry else 0)
    return pl.pallas_call(
        body,
        out_shape=jax.ShapeDtypeStruct((height, band[1] - band[0]), bf16),
        in_specs=[pl.BlockSpec(memory_space=pltpu.SMEM)] + [whole] * (2 + n),
        out_specs=whole,
        compiler_params=params(12),
        cost_estimate=cost(n * piece * piece * (band[1] - band[0]), 6 << 20),
    )(me, share, shift, *arrived)


def sum_amounts(me, amount, bands, arrived):
    piece = arrived[0][0].shape[0] - 16

    def body(me_ref, amount_ref, *refs):
        out_ref, refs = refs[-1], list(refs[:-1])
        for (at, end), pieces in zip(bands, arrived):
            out = amount_ref[:, at:end]
            for _ in pieces:
                both = refs.pop(0)[piece:, :].astype(f32)
                out += both[:8] + both[8:]
            out_ref[:, at:end] = out

    return pl.pallas_call(
        body,
        out_shape=jax.ShapeDtypeStruct(amount.shape, f32),
        in_specs=[pl.BlockSpec(memory_space=pltpu.SMEM)] + [whole] * (1 + sum(map(len, arrived))),
        out_specs=whole,
        compiler_params=params(12),
        cost_estimate=cost(0, 2 << 20),
    )(me, amount, *[ref for pieces in arrived for ref in pieces])


def final_maps(me, slots, along, spots, rows):
    total, n = slots.shape[1], spots.shape[1]

    def body(me_ref, slots_ref, along_ref, spots_ref, sel_ref, scale_ref):
        first = me_ref[0] * rows
        sel_ref[...] = one_hot(first + iota((rows, n), 0) == spots_ref[...])
        same = first + iota((rows, total), 0) == slots_ref[7:8, :]
        scale_ref[...] = jnp.zeros((rows, 128), f32)
        for b in range(2):
            weight = jnp.where(same, along_ref[b : b + 1, :], 0.0)
            scale_ref[:, b : b + 1] = jnp.sum(weight, axis=1, keepdims=True)

    return pl.pallas_call(
        body,
        out_shape=[jax.ShapeDtypeStruct((rows, n), bf16), jax.ShapeDtypeStruct((rows, 128), f32)],
        in_specs=[pl.BlockSpec(memory_space=pltpu.SMEM)] + [whole] * 3,
        out_specs=[whole] * 2,
        compiler_params=params(16),
        cost_estimate=cost(1 << 20, 3 << 20),
    )(me, slots, along, spots)


def strips_in(span):
    return [(k, min(k + 512, span)) for k in range(0, span, 512)]


def add_early(me, other, coeffs, sel, scale, amount, pieces, width, band):
    rows, span = coeffs.shape[0], band[1] - band[0]
    n, piece = len(pieces), pieces[0].shape[0]
    strips = strips_in(span)

    def body(me_ref, src_ref, sel_ref, scale_ref, amount_ref, *refs):
        out_ref, arrivals = refs[-2:]
        first = (me_ref[0] ^ other) % 2 * width + band[0]
        copies = []
        for i, (at, end) in enumerate(strips):
            cols = pl.ds(pl.multiple_of(first + at, 128), end - at)
            copy = pltpu.make_async_copy(src_ref.at[:, cols], out_ref.at[:, at:end], arrivals.at[i])
            copy.start()
            copies.append(copy)
        for copy, (at, end) in zip(copies, strips):
            strip = jnp.concatenate([ref[:, at:end] for ref in refs[:n]], axis=0)
            out = dot_nn(sel_ref[:, : n * piece], strip)
            for b in range(2):
                row = amount_ref[b : b + 1, band[0] + at : band[0] + end]
                out += scale_ref[:, b : b + 1] * row
            copy.wait()
            out_ref[:, at:end] += out

    return pl.pallas_call(
        body,
        out_shape=jax.ShapeDtypeStruct((rows, span), f32),
        in_specs=[
            pl.BlockSpec(memory_space=pltpu.SMEM),
            pl.BlockSpec(memory_space=pl.ANY),
            *[whole] * (3 + n),
        ],
        out_specs=whole,
        scratch_shapes=[pltpu.SemaphoreType.DMA((len(strips),))],
        compiler_params=params(12),
        cost_estimate=cost(rows * n * piece * span, rows * span * 8),
    )(me, coeffs, sel, scale, amount, *pieces)


def add_last(me, early, cols, buffer, sel, mine, sib, width, band):
    rows, span = sel.shape[0], band[1] - band[0]
    n, piece = len(mine), mine[0].shape[0]
    strips = strips_in(span)

    def body(me_ref, sel_ref, early_mine, early_sib, *refs):
        out_ref, held, departures = refs[-3:]
        chosen = sel_ref[:, sel_ref.shape[1] - n * piece :]
        copies = []
        for k, early_ref in enumerate((early_mine, early_sib)):
            first = (me_ref[0] ^ k) % 2 * width + band[0]
            for i, (at, end) in enumerate(strips):
                strip = jnp.concatenate([ref[:, at:end] for ref in refs[k * n : k * n + n]], axis=0)
                held[k, :, at:end] = early_ref[:, at:end] + dot_nn(chosen, strip)
                cut = pl.ds(pl.multiple_of(first + at, 128), end - at)
                copy = pltpu.make_async_copy(
                    held.at[k, :, at:end], out_ref.at[:, cut], departures.at[k * len(strips) + i]
                )
                copy.start()
                copies.append(copy)
        for copy in copies:
            copy.wait()

    operands = [sel, *early, *mine, *sib]
    in_specs = [pl.BlockSpec(memory_space=pltpu.SMEM)] + [whole] * len(operands)
    aliases = {}
    if buffer is not None:
        aliases = {1 + len(operands): 0}
        operands.append(buffer)
        in_specs.append(pl.BlockSpec(memory_space=pl.ANY))
    return pl.pallas_call(
        body,
        out_shape=pltpu.HBM((rows, cols), f32),
        in_specs=in_specs,
        out_specs=pl.BlockSpec(memory_space=pltpu.HBM),
        scratch_shapes=[
            pltpu.VMEM((2, rows, span), f32),
            pltpu.SemaphoreType.DMA((2 * len(strips),)),
        ],
        input_output_aliases=aliases,
        compiler_params=params(12),
        cost_estimate=cost(rows * n * piece * 2 * span, rows * 2 * span * 8),
    )(me, *operands)


def solution(mesh):
    n = mesh.shape["rows"]
    chips = n // 2
    bits = chips.bit_length() - 1
    ring = [k ^ (k >> 1) for k in range(chips)]
    place = [ring.index(k) for k in range(chips)]

    def core_perm(chip_of):
        return [(i, 2 * chip_of(i // 2, i % 2) + i % 2) for i in range(n)]

    sib_perm = [(i, i ^ 1) for i in range(n)]
    ring_perm = core_perm(
        lambda chip, core: ring[(place[chip] + (1 if core == 0 else chips - 1)) % chips]
    )

    def stage_bit(stage, core):
        return 1 << (stage if core == 0 else bits - 1 - stage)

    def to_sib(x):
        return lax.ppermute(x, "rows", sib_perm)

    def stage_cap(total, stage):
        return min(total, total // 2 + ((1 << stage) - 1) * (total // chips))

    def spread_path(points, targets, coeffs, inverses, pts_sib, me, slots, theirs, spots, shift):
        rows_here, feats = points.shape
        cols = coeffs.shape[1]
        half_f = feats // 2
        extra_cols = -cols % 256
        if extra_cols:
            targets = jnp.pad(targets, ((0, 0), (0, extra_cols)))
            coeffs = jnp.pad(coeffs, ((0, 0), (0, extra_cols)))
        width = (cols + extra_cols) // 2
        blk = 128 * max(d for d in (1, 2, 3, 4) if width // 128 % d == 0)
        total = slots.shape[1]
        piece = total // (2 * chips)
        steps = 2 * chips - 1

        blocks = width // blk
        first = (blocks + 1) // 2 * blk
        bands = [(0, first), (first, width)] if first < width else [(0, width)]

        caps = [stage_cap(total, stage) for stage in range(bits)]
        sent = pick_points(me, theirs, points, pts_sib, half_f, caps[0])
        for stage in range(bits):
            got = lax.ppermute(
                sent, "rows", core_perm(lambda k, c, s=stage: k ^ stage_bit(s, c))
            )
            if stage == 0:
                wide = 128 * max(d for d in range(1, 9) if width // 128 % d == 0)
                t_mine, t_other = pack_targets(
                    after(me, sent), theirs, targets, caps[0], width, wide
                )
                t_sib = to_sib(t_other)
                got = after(got, t_other)
            if stage < bits - 1:
                sent = append_rows(sent, got, theirs, stage, caps[stage + 1])
        c_mine, c_other = cut_columns(after(me, sent), coeffs, width, blk)
        placed = place_rows(sent, theirs, bits - 1)
        norms = point_norms(after(points, placed), pts_sib)
        block_half = place_rows(after(got, norms, c_other), theirs, bits, placed)
        block_other = to_sib(block_half)
        c_sib = to_sib(after(c_other, block_other))
        parts = [c_mine, c_sib, t_mine, t_sib]

        left, rest, rows_along, along = build_maps(
            me, points, pts_sib, norms, block_half, block_other, inverses, slots,
            theirs,
        )

        amount, *first_sent = first_shares(
            piece, bands, slots, bits, rest, left, rows_along, parts
        )
        share = {}
        arrived = [[] for _ in bands]
        final = [[] for _ in bands]
        final_sib = [[] for _ in bands]
        early_mine, early_sib = [], []
        early = steps - chips
        fillers = []
        latest = None

        def exchange(b, latest):
            for part in final[b][len(final_sib[b]) :]:
                final_sib[b].append(to_sib(after(part, latest)))

        def early_of(other, b, amounts, pieces, me_then):
            return add_early(
                me_then, other, coeffs, sel, scale, amounts, pieces[b][:early], width, bands[b]
            )

        for step in range(steps + 1):
            for b, band in enumerate(bands):
                if step == 0:
                    sent = first_sent[b]
                else:
                    arrived[b][-1] = after(arrived[b][-1], latest, *fillers)
                    fillers = []
                    sent = add_arrived(
                        me, *share[step], band, shift, arrived[b][-chips:], step < chips - 1
                    )
                latest = sent
                if step < steps:
                    arrived[b].append(lax.ppermute(sent, "rows", ring_perm))
                if step >= chips - 1:
                    final[b].append(sent)
                if step == steps:
                    exchange(b, latest)
                    if b == 0:
                        fillers += early_sib[1:]
            row = 2 * step + 1
            if row < 2 * chips:
                count = min(2, 2 * chips - row)
                weights = map_weights(
                    row * piece, count * piece, False, after(slots, latest), bits, rest, left,
                    None, caps[0],
                )
                more = more_shares(after(me, latest), weights, 0, count * piece, bands, parts)
                for k in range(count):
                    share[row + k] = (more, k * piece)
                fillers.append(more)
            if step == chips - 1:
                carried = [pieces[: chips - 1] for pieces in arrived]
                amount = sum_amounts(after(me, latest), amount, bands, carried)
                sel, scale = final_maps(after(me, latest), slots, along, spots, rows_here)
                fillers += [amount, scale]
            b = step - (steps - 2)
            if 0 <= b < len(bands):
                early_mine.append(early_of(0, b, amount, final, after(me, latest)))
                fillers.append(early_mine[-1])
            if step == steps - 1:
                amount_sib = to_sib(after(amount, early_mine[-1]))
                for b in range(len(bands)):
                    exchange(b, early_mine[-1])
                for b in range(len(bands)):
                    early_sib.append(early_of(1, b, amount_sib, final_sib, me))
                fillers.append(early_sib[0])

        out = None
        for b, band in enumerate(bands):
            out = add_last(
                me, (early_mine[b], early_sib[b]), cols + extra_cols, out, sel,
                final[b][early:], final_sib[b][early:], width, band,
            )
        return out[:, :cols] if extra_cols else out

    def per_device(points, targets, coeffs, block_ids, inverses):
        rows_here = points.shape[0]
        total = block_ids.size
        me = lax.axis_index("rows").astype(i32).reshape(1)
        pts_sib = to_sib(points)
        stage_bits = [[stage_bit(s, core) for s in range(bits)] for core in range(2)]
        caps = [stage_cap(total, s) for s in range(bits)]
        fits, *plans = plan(me, block_ids, rows_here, ring, stage_bits, caps)
        out = spread_path(points, targets, coeffs, inverses, pts_sib, me, *plans)

        def general(state):
            return jnp.ones_like(fits), general_path(n, points, targets, coeffs, block_ids, inverses)

        return lax.while_loop(lambda state: state[0][0] == 0, general, (fits, out))[1]

    return jax.shard_map(
        per_device,
        mesh=mesh,
        in_specs=(P("rows", None), P("rows", "labels"), P("rows", "labels"), P(), P()),
        out_specs=P("rows", "labels"),
        check_vma=False,
    )
```

```python
import jax
import jax.numpy as jnp
from jax import lax
from jax.experimental import pallas as pl
from jax.experimental.pallas import tpu as pltpu
from jax.sharding import PartitionSpec as P

ridge_weight = 0.5
bf16 = jnp.bfloat16
f32 = jnp.float32
i32 = jnp.int32
whole = pl.BlockSpec(memory_space=pltpu.VMEM)


def dot_nn(a, b):
    return lax.dot_general(a, b, (((1,), (0,)), ((), ())), preferred_element_type=f32)


def dot_nt(a, b):
    return lax.dot_general(a, b, (((1,), (1,)), ((), ())), preferred_element_type=f32)


def square_sums(pts):
    return jnp.sum(jnp.square(pts.astype(f32)), axis=1, keepdims=True)


def kernel_tile(left, right):
    inner_prod = dot_nt(left, right)
    sq_dist = jnp.maximum(square_sums(left) + square_sums(right).T - 2.0 * inner_prod, 0.0)
    return jnp.exp(-(2.0 / left.shape[1]) * sq_dist).astype(bf16)


def split_bf16(x):
    high = x.astype(bf16)
    return high, (x - high.astype(f32)).astype(bf16)


def both_parts(x):
    high, low = split_bf16(x)
    return jnp.concatenate([high.astype(f32), low.astype(f32)], axis=0).astype(bf16)


def as_row(column):
    n = column.shape[0]
    return jnp.transpose(jnp.broadcast_to(column, (n, 128)))[0:1, :]


def iota(shape, dim):
    return lax.broadcasted_iota(i32, shape, dim)


def one_hot(cond):
    return jnp.where(cond, 1.0, 0.0).astype(bf16)


def after(x, *others):
    return lax.optimization_barrier((x, *others))[0]


def params(megabytes):
    return pltpu.CompilerParams(vmem_limit_bytes=megabytes << 20)


def cost(macs, bytes_accessed):
    return pl.CostEstimate(flops=2 * macs, bytes_accessed=bytes_accessed, transcendentals=0)


def ring_sum(x, n):
    def hop(_, state):
        total, moving = state
        moving = lax.ppermute(moving, "rows", [(i, (i + 1) % n) for i in range(n)])
        return total + moving, moving

    return lax.fori_loop(0, n - 1, hop, (x, x))[0]


def general_path(n, points, targets, coeffs, block_ids, inverses):
    rows_here = points.shape[0]
    first_row = lax.axis_index("rows") * rows_here
    zero_low = jnp.zeros((), bf16)
    current = coeffs
    for blk in range(2):
        local_ids = block_ids[blk] - first_row
        inside = (local_ids >= 0) & (local_ids < rows_here)
        local_rows = jnp.clip(local_ids, 0, rows_here - 1)
        picked = jnp.where(inside[:, None], points[local_rows], zero_low)
        block_pts = ring_sum(picked, n)
        ktile = kernel_tile(points, block_pts)
        c_low = current.astype(bf16)
        sel_targets = jnp.where(inside[:, None], targets[local_rows].astype(f32), 0.0)
        sel_coeffs = jnp.where(inside[:, None], current[local_rows], 0.0)
        local_side = ridge_weight * sel_coeffs - sel_targets
        product = lax.dot_general(
            ktile, c_low, (((0,), (0,)), ((), ())), preferred_element_type=f32
        )
        negated = ring_sum(product + local_side, n)
        update = jnp.dot(
            inverses[blk], -negated, precision=lax.Precision.HIGHEST, preferred_element_type=f32
        )
        where_to = (jnp.arange(rows_here, dtype=i32)[:, None] == local_ids[None, :]).astype(f32)
        current = current + jnp.dot(
            where_to, update, precision=lax.Precision.HIGHEST, preferred_element_type=f32
        )
    return current


def plan(me, block_ids, rows, ring, stage_bits, caps):
    total = block_ids.size
    blk = block_ids.shape[1]
    chips = len(ring)
    place = [ring.index(k) for k in range(chips)]
    piece = total // (2 * chips)
    bits = len(caps)
    n_final = total - (chips - 1) * piece
    step = min(256, total)
    groups = []
    for core in range(2):
        done = 0
        for stage in range(bits):
            members = {}
            for k in range(chips):
                members.setdefault(k & ~done, []).append(k)
            groups += [(m, caps[stage]) for m in members.values()]
            done |= stage_bits[core][stage]

    def body(me_ref, ids_ref, flag_ref, slots_ref, their_ref, spots_ref, shift_ref):
        chip, core = me_ref[0] // 2, me_ref[0] % 2
        ids = jnp.concatenate([ids_ref[0:1, :], ids_ref[1:2, :]], axis=1).astype(f32)
        ids_col = jnp.transpose(jnp.broadcast_to(ids, (128, total)))
        own = jnp.floor((ids + 0.5) * (0.5 / rows))
        index = iota((1, total), 1)
        rank = jnp.zeros((1, total), f32)
        for r in range(0, total, step):
            own_col = jnp.floor((ids_col[r : r + step, 0:1] + 0.5) * (0.5 / rows))
            ahead = (own_col == own) & (r + iota((step, total), 0) < index)
            rank += jnp.sum(jnp.where(ahead, 1.0, 0.0), axis=0, keepdims=True)

        def count(which):
            return jnp.sum(jnp.where(own == which, 1.0, 0.0), axis=1, keepdims=True)

        def slots(listed):
            slot = jnp.full((1, total), -1.0, f32)
            before = jnp.zeros((1, 1), f32)
            for which in listed:
                which = which.astype(f32)
                slot = jnp.where(own == which, before + rank, slot)
                before = before + count(which)
            return slot

        counts = [count(float(k)) for k in range(chips)]
        slack = counts[0] - piece
        for k in range(1, chips):
            slack = jnp.minimum(slack, counts[k] - piece)
        for members, cap in groups:
            slack = jnp.minimum(slack, cap - sum(counts[k] for k in members))
        flag_ref[0] = (jnp.max(slack) >= 0.0).astype(i32)

        slots_ref[...] = jnp.zeros(slots_ref.shape, i32)
        group = [0]
        columns = []
        for stage in range(bits):
            bit = jnp.where(core == 0, stage_bits[0][stage], stage_bits[1][stage])
            mine = slots([chip ^ g for g in group])
            if stage == 0:
                slots_ref[0:1, :] = mine.astype(i32)
                line = iota((caps[0], total), 0).astype(f32)
                wanted = jnp.where(mine == line, ids + 1.0, 0.0)
                wanted = jnp.sum(wanted, axis=1, keepdims=True) - 1.0
            if stage == bits - 1:
                columns += [mine, slots([chip ^ bit ^ g for g in group])]
            else:
                held = sum(count((chip ^ g).astype(f32)) for g in group)
                columns.append(jnp.broadcast_to(held, (1, total)))
            group = group + [g ^ bit for g in group]
        slots_ref[7:8, :] = ids.astype(i32)
        fill = jnp.zeros((127 - len(columns), total), f32)
        columns = jnp.concatenate(columns + [fill, ids], axis=0)
        their_ref[...] = jnp.transpose(columns).astype(i32)
        their_ref[: caps[0], 126:127] = wanted.astype(i32)

        def lookup(which, table):
            out = jnp.int32(table[0])
            for k in range(1, chips):
                out = jnp.where(which == k, table[k], out)
            return out

        here = lookup(chip, place)
        way = jnp.where(core == 0, chips - 1, 1)
        listed = [lookup((here + way * (k + 1)) % chips, ring) for k in range(chips)]
        position = slots(listed)
        slots_ref[bits : bits + 1, :] = position.astype(i32)
        lag = count(listed[0].astype(f32)).astype(i32)
        length = (2 * chips - 1) * piece
        source = iota((piece, length), 0) - lag + length
        shift_ref[...] = one_hot(source == iota((piece, length), 1))
        pos_col = jnp.transpose(jnp.broadcast_to(position, (128, total)))[:, 0:1]
        line = ((chips - 1) * piece + iota((1, n_final), 1)).astype(f32)
        spots = jnp.sum(
            jnp.where(pos_col == line, ids_col[:, 0:1], 0.0), axis=0, keepdims=True
        )
        spots_ref[...] = spots.astype(i32)

    smem = pl.BlockSpec(memory_space=pltpu.SMEM)
    return pl.pallas_call(
        body,
        out_shape=[
            jax.ShapeDtypeStruct((1,), i32),
            jax.ShapeDtypeStruct((8, total), i32),
            jax.ShapeDtypeStruct((total, 128), i32),
            jax.ShapeDtypeStruct((1, n_final), i32),
            jax.ShapeDtypeStruct((piece, total - piece), bf16),
        ],
        in_specs=[smem, whole],
        out_specs=[smem, whole, whole, whole, whole],
        compiler_params=params(16),
        cost_estimate=cost(1 << 20, 1 << 20),
    )(me, block_ids)


def pick_points(me, theirs, points, sib_points, half_f, cap):
    rows = points.shape[0]

    def body(me_ref, their_ref, own_ref, sib_ref, sent_ref):
        cols = pl.ds(pl.multiple_of(me_ref[0] % 2 * half_f, 128), half_f)
        wanted = their_ref[:cap, 126:127]
        local = iota((cap, rows), 1)
        own = one_hot(wanted == local + me_ref[0] * rows)
        sib = one_hot(wanted == local + (me_ref[0] ^ 1) * rows)
        out = dot_nn(own, own_ref[:, cols]) + dot_nn(sib, sib_ref[:, cols])
        sent_ref[...] = out.astype(bf16)

    return pl.pallas_call(
        body,
        out_shape=jax.ShapeDtypeStruct((cap, half_f), bf16),
        in_specs=[pl.BlockSpec(memory_space=pltpu.SMEM)] + [whole] * 3,
        out_specs=whole,
        compiler_params=params(16),
        cost_estimate=cost(2 * cap * rows * half_f, 4 << 20),
    )(me, theirs, points, sib_points)


def append_rows(sent, got, theirs, stage, cap_next):
    cap, half_f = sent.shape

    def body(sent_ref, got_ref, their_ref, out_ref):
        held = their_ref[:cap_next, stage : stage + 1]
        behind = one_hot(iota((cap_next, cap), 0) - held == iota((cap_next, cap), 1))
        out = dot_nn(behind, got_ref[...])
        out_ref[:cap, :] = (out[:cap] + sent_ref[...].astype(f32)).astype(bf16)
        if cap_next > cap:
            out_ref[cap:, :] = out[cap:].astype(bf16)

    return pl.pallas_call(
        body,
        out_shape=jax.ShapeDtypeStruct((cap_next, half_f), bf16),
        in_specs=[whole] * 3,
        out_specs=whole,
        compiler_params=params(16),
        cost_estimate=cost(cap * cap_next * half_f, 4 << 20),
    )(sent, got, theirs)


def place_rows(packed, theirs, column, block=None):
    cap, half_f = packed.shape
    total = theirs.shape[0]

    def body(packed_ref, their_ref, *refs):
        spots = one_hot(their_ref[:, column : column + 1] == iota((total, cap), 1))
        out = dot_nn(spots, packed_ref[...])
        if block is not None:
            out += refs[0][...].astype(f32)
        refs[-1][...] = out.astype(bf16)

    return pl.pallas_call(
        body,
        out_shape=jax.ShapeDtypeStruct((total, half_f), bf16),
        in_specs=[whole] * (2 if block is None else 3),
        out_specs=whole,
        compiler_params=params(16),
        cost_estimate=cost(total * cap * half_f, 4 << 20),
    )(packed, theirs, *([] if block is None else [block]))


def point_norms(points, sib_points):
    rows = points.shape[0]

    def body(own_ref, sib_ref, out_ref):
        for k, ref in enumerate((own_ref, sib_ref)):
            norm = square_sums(ref[...])
            out_ref[k * rows : (k + 1) * rows, :] = jnp.broadcast_to(norm, (rows, 128))

    return pl.pallas_call(
        body,
        out_shape=jax.ShapeDtypeStruct((2 * rows, 128), f32),
        in_specs=[whole] * 2,
        out_specs=whole,
        compiler_params=params(16),
        cost_estimate=cost(4 << 20, 3 << 20),
    )(points, sib_points)


def cut_columns(me, x, width, blk):
    rows = x.shape[0]

    def body(me_ref, mine_ref, other_ref, mine_out, other_out):
        mine_out[...] = mine_ref[...].astype(bf16)
        other_out[...] = other_ref[...].astype(bf16)

    def half(k):
        return pl.BlockSpec(
            (rows, blk), lambda j, me_ref: (0, (me_ref[0] ^ k) % 2 * (width // blk) + j)
        )

    plain = pl.BlockSpec((rows, blk), lambda j, me_ref: (0, j))
    return pl.pallas_call(
        body,
        out_shape=[jax.ShapeDtypeStruct((rows, width), bf16)] * 2,
        grid_spec=pltpu.PrefetchScalarGridSpec(
            num_scalar_prefetch=1,
            grid=(width // blk,),
            in_specs=[half(0), half(1)],
            out_specs=[plain] * 2,
        ),
        compiler_params=params(16),
        cost_estimate=cost(0, rows * width * 8),
    )(me, x, x)


def pack_targets(me, theirs, targets, cap, width, blk):
    rows = targets.shape[0]

    def body(me_ref, their_ref, mine_ref, other_ref, mine_out, other_out):
        local = iota((cap, rows), 1) + me_ref[0] * rows
        pick = one_hot(their_ref[:cap, 126:127] == local)
        mine_out[...] = dot_nn(pick, mine_ref[...]).astype(bf16)
        other_out[...] = dot_nn(pick, other_ref[...]).astype(bf16)

    def half(k):
        return pl.BlockSpec(
            (rows, blk), lambda j, me_ref: (0, (me_ref[0] ^ k) % 2 * (width // blk) + j)
        )

    plain = pl.BlockSpec((cap, blk), lambda j, me_ref: (0, j))
    return pl.pallas_call(
        body,
        out_shape=[jax.ShapeDtypeStruct((cap, width), bf16)] * 2,
        grid_spec=pltpu.PrefetchScalarGridSpec(
            num_scalar_prefetch=1,
            grid=(width // blk,),
            in_specs=[whole, half(0), half(1)],
            out_specs=[plain] * 2,
        ),
        compiler_params=params(16),
        cost_estimate=cost(2 * cap * rows * width, rows * width * 8),
    )(me, theirs, targets, targets)


def build_maps(me, points, sib_points, norms_in, q_half, q_other, inverses, slots, theirs):
    rows, feats = points.shape
    half_f = feats // 2
    total = slots.shape[1]
    blk = total // 2
    step = min(256, rows, blk)
    scale = -(2.0 / feats)

    def body(
        me_ref, own_ref, sib_ref, pn_ref, qh_ref, qo_ref, inv_ref, idr_ref, idc_ref,
        left_ref, rest_ref, rows_ref, along_ref, norm_ref,
    ):
        mine = pl.ds(pl.multiple_of(me_ref[0] % 2 * half_f, 128), half_f)
        other = pl.ds(pl.multiple_of((1 - me_ref[0] % 2) * half_f, 128), half_f)
        for r in range(0, total, step):
            part = square_sums(qh_ref[r : r + step, :]) + square_sums(qo_ref[r : r + step, :])
            norm_ref[r : r + step, :] = jnp.broadcast_to(part, (step, 128))
        norms = jnp.transpose(norm_ref[...])[0:1, :]

        def values(a, b, a_sq, b_sq, same):
            inner = dot_nt(a[0], b[0]) + dot_nt(a[1], b[1])
            sq_dist = jnp.maximum(a_sq + b_sq - 2.0 * inner, 0.0)
            k = jnp.exp(scale * sq_dist).astype(bf16).astype(f32)
            return (k + jnp.where(same, ridge_weight, 0.0)).astype(bf16)

        cross = []
        for r in range(blk, total, step):
            at = slice(r, r + step)
            cross.append(
                values(
                    (qh_ref[at, :], qo_ref[at, :]),
                    (qh_ref[:blk, :], qo_ref[:blk, :]),
                    norm_ref[at, 0:1],
                    norms[:, :blk],
                    idc_ref[at, 127:128] == idr_ref[7:8, :blk],
                )
            )
        cross = jnp.concatenate(cross, axis=0)
        inv0, inv1 = inv_ref[0], inv_ref[1]
        high0, low0 = split_bf16(inv0)
        high1, low1 = split_bf16(inv1)
        high, low = split_bf16(dot_nn(cross, high0) + dot_nn(cross, low0))
        lower = -(dot_nn(high1, high) + dot_nn(high1, low) + dot_nn(low1, high))

        bell = jnp.exp(-scale * (jnp.min(norms) - norms))

        def direction(inv, weights):
            way = jnp.sum(inv * weights, axis=1, keepdims=True)
            return way * lax.rsqrt(jnp.maximum(jnp.sum(way * way), 1e-30))

        way0 = direction(inv0, bell[:, :blk])
        way1 = direction(inv1, bell[:, blk:])
        row00 = jnp.sum(way0 * inv0, axis=0, keepdims=True)
        row10 = jnp.sum(way1 * lower, axis=0, keepdims=True)
        row11 = jnp.sum(way1 * inv1, axis=0, keepdims=True)
        rest_ref[:blk, :blk] = (inv0 - way0 * row00).astype(bf16)
        rest_ref[:blk, blk:] = jnp.zeros((blk, blk), bf16)
        rest_ref[blk:, :blk] = (lower - way1 * row10).astype(bf16)
        rest_ref[blk:, blk:] = (inv1 - way1 * row11).astype(bf16)
        rows_ref[...] = jnp.zeros((8, total), f32)
        rows_ref[0:1, :blk] = row00
        rows_ref[1:2, :blk] = row10
        rows_ref[1:2, blk:] = row11
        along_ref[...] = jnp.zeros((8, total), f32)
        along_ref[0:1, :blk] = as_row(way0)
        along_ref[1:2, blk:] = as_row(way1)

        for which, ref in enumerate((own_ref, sib_ref)):
            for r in range(0, rows, step):
                at = slice(r, r + step)
                a = (ref[at, mine], ref[at, other])
                spot = (me_ref[0] ^ which) * rows + r + iota((step, total), 0)
                left_ref[which * rows + r : which * rows + r + step, :] = -values(
                    a,
                    (qh_ref[...], qo_ref[...]),
                    pn_ref[which * rows + r : which * rows + r + step, 0:1],
                    norms,
                    spot == idr_ref[7:8, :],
                )

    return pl.pallas_call(
        body,
        out_shape=[
            jax.ShapeDtypeStruct((2 * rows, total), bf16),
            jax.ShapeDtypeStruct((total, total), bf16),
            jax.ShapeDtypeStruct((8, total), f32),
            jax.ShapeDtypeStruct((8, total), f32),
        ],
        in_specs=[pl.BlockSpec(memory_space=pltpu.SMEM)] + [whole] * 8,
        out_specs=[whole] * 4,
        scratch_shapes=[pltpu.VMEM((total, 128), f32)],
        compiler_params=params(24),
        cost_estimate=cost(4 * rows * total * feats, 12 << 20),
    )(me, points, sib_points, norms_in, q_half, q_other, inverses, slots, theirs)


def map_weights(lo, count, extra, slots, pos_row, rest, left, rows_along, cap):
    points, total = left.shape

    def fill(slots_ref, rest_ref, left_ref, along_ref, weights):
        sel = one_hot(slots_ref[pos_row : pos_row + 1, :] == lo + iota((count, total), 0))
        moved = dot_nn(sel, rest_ref[...]).astype(bf16)
        if extra:
            moved = jnp.concatenate([moved, both_parts(along_ref[...])], axis=0)
        pack = one_hot(iota((cap, total), 0) == slots_ref[0:1, :])
        for at, other in ((slice(0, points), left_ref[...]), (slice(points, points + cap), pack)):
            mapped = dot_nt(moved, other)
            weights[:count, at] = mapped[:count].astype(bf16)
            if extra:
                both = mapped[count : count + 8] + mapped[count + 8 :]
                weights[count:, at] = both_parts(both)

    if extra:
        return fill

    def body(slots_ref, rest_ref, left_ref, out_ref):
        fill(slots_ref, rest_ref, left_ref, None, out_ref)

    return pl.pallas_call(
        body,
        out_shape=jax.ShapeDtypeStruct((count, points + cap), bf16),
        in_specs=[whole] * 3,
        out_specs=whole,
        compiler_params=params(20),
        cost_estimate=cost(count * (2 * points + cap) * total, 6 << 20),
    )(slots, rest, left)


def strips_of(bands):
    return [(k, min(k + 512, end)) for at, end in bands for k in range(at, end, 512)]


def strip_of(refs, at, end):
    targets = refs[2][:, at:end] + refs[3][:, at:end]
    return jnp.concatenate([refs[0][:, at:end], refs[1][:, at:end], targets], axis=0)


def first_shares(piece, bands, slots, pos_row, rest, left, rows_along, parts):
    width, cap = parts[0].shape[1], parts[-1].shape[0]
    height, depth = piece + 16, left.shape[0] + cap
    fill = map_weights(0, piece, True, slots, pos_row, rest, left, rows_along, cap)

    def body(slots_ref, rest_ref, left_ref, along_ref, *refs):
        part_refs, refs = refs[: len(parts)], refs[len(parts) :]
        amount_ref, band_refs, weights = refs[0], refs[1:-1], refs[-1]
        fill(slots_ref, rest_ref, left_ref, along_ref, weights)
        for at, end in strips_of(bands):
            out = dot_nn(weights[...], strip_of(part_refs, at, end))
            amount_ref[:, at:end] = out[piece : piece + 8] + out[piece + 8 :]
            for band, ref in zip(bands, band_refs):
                if band[0] <= at < band[1]:
                    strip = slice(at - band[0], end - band[0])
                    ref[:piece, strip] = out[:piece].astype(bf16)
                    ref[piece:, strip] = both_parts(out[piece : piece + 8] + out[piece + 8 :])

    out_shape = [jax.ShapeDtypeStruct((8, width), f32)]
    out_shape += [jax.ShapeDtypeStruct((piece + 16, end - at), bf16) for at, end in bands]
    return pl.pallas_call(
        body,
        out_shape=out_shape,
        in_specs=[whole] * (4 + len(parts)),
        out_specs=[whole] * len(out_shape),
        scratch_shapes=[pltpu.VMEM((height, depth), bf16)],
        compiler_params=params(20),
        cost_estimate=cost(height * depth * (width + 1024), 12 << 20),
    )(slots, rest, left, rows_along, *parts)


def more_shares(me, weights, lo, count, bands, parts):
    depth, width = weights.shape[1], parts[0].shape[1]

    def body(me_ref, weights_ref, *refs):
        for at, end in strips_of(bands):
            strip = strip_of(refs, at, end)
            refs[-1][:, at:end] = dot_nn(weights_ref[lo : lo + count, :], strip)

    return pl.pallas_call(
        body,
        out_shape=jax.ShapeDtypeStruct((count, width), f32),
        in_specs=[pl.BlockSpec(memory_space=pltpu.SMEM)] + [whole] * (1 + len(parts)),
        out_specs=whole,
        compiler_params=params(16),
        cost_estimate=cost(count * depth * width, 10 << 20),
    )(me, weights, *parts)


def add_arrived(me, share, row, band, shift, arrived, carry):
    piece, length = shift.shape
    n = len(arrived)

    def body(me_ref, share_ref, shift_ref, *refs):
        out = share_ref[row : row + piece, band[0] : band[1]]
        for k, ref in enumerate(refs[:-1]):
            at = length - (n - k) * piece
            out += dot_nn(shift_ref[:, at : at + piece], ref[:piece, :])
        refs[-1][:piece, :] = out.astype(bf16)
        if carry:
            refs[-1][piece:, :] = refs[-2][piece:, :]

    height = piece + (16 if carry else 0)
    return pl.pallas_call(
        body,
        out_shape=jax.ShapeDtypeStruct((height, band[1] - band[0]), bf16),
        in_specs=[pl.BlockSpec(memory_space=pltpu.SMEM)] + [whole] * (2 + n),
        out_specs=whole,
        compiler_params=params(12),
        cost_estimate=cost(n * piece * piece * (band[1] - band[0]), 6 << 20),
    )(me, share, shift, *arrived)


def sum_amounts(me, amount, bands, arrived):
    piece = arrived[0][0].shape[0] - 16

    def body(me_ref, amount_ref, *refs):
        out_ref, refs = refs[-1], list(refs[:-1])
        for (at, end), pieces in zip(bands, arrived):
            out = amount_ref[:, at:end]
            for _ in pieces:
                both = refs.pop(0)[piece:, :].astype(f32)
                out += both[:8] + both[8:]
            out_ref[:, at:end] = out

    return pl.pallas_call(
        body,
        out_shape=jax.ShapeDtypeStruct(amount.shape, f32),
        in_specs=[pl.BlockSpec(memory_space=pltpu.SMEM)] + [whole] * (1 + sum(map(len, arrived))),
        out_specs=whole,
        compiler_params=params(12),
        cost_estimate=cost(0, 2 << 20),
    )(me, amount, *[ref for pieces in arrived for ref in pieces])


def final_maps(me, slots, along, spots, rows):
    total, n = slots.shape[1], spots.shape[1]

    def body(me_ref, slots_ref, along_ref, spots_ref, sel_ref, scale_ref):
        first = me_ref[0] * rows
        sel_ref[...] = one_hot(first + iota((rows, n), 0) == spots_ref[...])
        same = first + iota((rows, total), 0) == slots_ref[7:8, :]
        scale_ref[...] = jnp.zeros((rows, 128), f32)
        for b in range(2):
            weight = jnp.where(same, along_ref[b : b + 1, :], 0.0)
            scale_ref[:, b : b + 1] = jnp.sum(weight, axis=1, keepdims=True)

    return pl.pallas_call(
        body,
        out_shape=[jax.ShapeDtypeStruct((rows, n), bf16), jax.ShapeDtypeStruct((rows, 128), f32)],
        in_specs=[pl.BlockSpec(memory_space=pltpu.SMEM)] + [whole] * 3,
        out_specs=[whole] * 2,
        compiler_params=params(16),
        cost_estimate=cost(1 << 20, 3 << 20),
    )(me, slots, along, spots)


def strips_in(span):
    return [(k, min(k + 512, span)) for k in range(0, span, 512)]


def add_early(me, coeffs, sel, scale, amount, pieces, width, band):
    rows, span = coeffs.shape[0], band[1] - band[0]
    n, piece = len(pieces), pieces[0].shape[0]
    strips = strips_in(span)

    def body(me_ref, src_ref, sel_ref, scale_ref, amount_ref, *refs):
        out_ref, arrivals = refs[-2:]
        first = me_ref[0] % 2 * width + band[0]
        copies = []
        for i, (at, end) in enumerate(strips):
            cols = pl.ds(pl.multiple_of(first + at, 128), end - at)
            copy = pltpu.make_async_copy(src_ref.at[:, cols], out_ref.at[:, at:end], arrivals.at[i])
            copy.start()
            copies.append(copy)
        for copy, (at, end) in zip(copies, strips):
            strip = jnp.concatenate([ref[:, at:end] for ref in refs[:n]], axis=0)
            out = dot_nn(sel_ref[:, : n * piece], strip)
            for b in range(2):
                row = amount_ref[b : b + 1, band[0] + at : band[0] + end]
                out += scale_ref[:, b : b + 1] * row
            copy.wait()
            out_ref[:, at:end] += out

    return pl.pallas_call(
        body,
        out_shape=jax.ShapeDtypeStruct((rows, span), f32),
        in_specs=[
            pl.BlockSpec(memory_space=pltpu.SMEM),
            pl.BlockSpec(memory_space=pl.ANY),
            *[whole] * (3 + n),
        ],
        out_specs=whole,
        scratch_shapes=[pltpu.SemaphoreType.DMA((len(strips),))],
        compiler_params=params(12),
        cost_estimate=cost(rows * n * piece * span, rows * span * 8),
    )(me, coeffs, sel, scale, amount, *pieces)


def add_last(me, coeffs, early, buffer, sel, scale, amount, mine, sib, width, band):
    rows, cols, span = sel.shape[0], coeffs.shape[1], band[1] - band[0]
    n, piece = len(mine), mine[0].shape[0]
    strips = strips_in(span)

    def body(me_ref, src_ref, sel_ref, scale_ref, amount_ref, early_ref, *refs):
        out_ref, held, arrivals, departures = refs[-4:]

        def cols_of(k, at, end):
            first = (me_ref[0] ^ k) % 2 * width + band[0]
            return pl.ds(pl.multiple_of(first + at, 128), end - at)

        coming, going = [], []
        for i, (at, end) in enumerate(strips):
            copy = pltpu.make_async_copy(
                src_ref.at[:, cols_of(1, at, end)], held.at[1, :, at:end], arrivals.at[i]
            )
            copy.start()
            coming.append(copy)
        for k, parts in enumerate((refs[:n], refs[n : n + len(sib)])):
            chosen = sel_ref[:, sel_ref.shape[1] - len(parts) * piece :]
            for i, (at, end) in enumerate(strips):
                strip = jnp.concatenate([ref[:, at:end] for ref in parts], axis=0)
                out = dot_nn(chosen, strip)
                if k == 0:
                    held[k, :, at:end] = early_ref[:, at:end] + out
                else:
                    for b in range(2):
                        row = amount_ref[b : b + 1, band[0] + at : band[0] + end]
                        out += scale_ref[:, b : b + 1] * row
                    coming[i].wait()
                    held[k, :, at:end] += out
                copy = pltpu.make_async_copy(
                    held.at[k, :, at:end],
                    out_ref.at[:, cols_of(k, at, end)],
                    departures.at[k * len(strips) + i],
                )
                copy.start()
                going.append(copy)
        for copy in going:
            copy.wait()

    operands = [coeffs, sel, scale, amount, early, *mine, *sib]
    in_specs = [pl.BlockSpec(memory_space=pltpu.SMEM), pl.BlockSpec(memory_space=pl.ANY)]
    in_specs += [whole] * (len(operands) - 1)
    aliases = {}
    if buffer is not None:
        aliases = {1 + len(operands): 0}
        operands.append(buffer)
        in_specs.append(pl.BlockSpec(memory_space=pl.ANY))
    return pl.pallas_call(
        body,
        out_shape=pltpu.HBM((rows, cols), f32),
        in_specs=in_specs,
        out_specs=pl.BlockSpec(memory_space=pltpu.HBM),
        scratch_shapes=[
            pltpu.VMEM((2, rows, span), f32),
            pltpu.SemaphoreType.DMA((len(strips),)),
            pltpu.SemaphoreType.DMA((2 * len(strips),)),
        ],
        input_output_aliases=aliases,
        compiler_params=params(12),
        cost_estimate=cost(rows * (n + len(sib)) * piece * span, rows * 2 * span * 8),
    )(me, *operands)


def solution(mesh):
    n = mesh.shape["rows"]
    chips = n // 2
    bits = chips.bit_length() - 1
    ring = [k ^ (k >> 1) for k in range(chips)]
    place = [ring.index(k) for k in range(chips)]

    def core_perm(chip_of):
        return [(i, 2 * chip_of(i // 2, i % 2) + i % 2) for i in range(n)]

    sib_perm = [(i, i ^ 1) for i in range(n)]
    ring_perm = core_perm(
        lambda chip, core: ring[(place[chip] + (1 if core == 0 else chips - 1)) % chips]
    )

    def stage_bit(stage, core):
        return 1 << (stage if core == 0 else bits - 1 - stage)

    def to_sib(x):
        return lax.ppermute(x, "rows", sib_perm)

    def stage_cap(total, stage):
        return min(total, total // 2 + ((1 << stage) - 1) * (total // chips))

    def spread_path(points, targets, coeffs, inverses, pts_sib, me, slots, theirs, spots, shift):
        rows_here, feats = points.shape
        cols = coeffs.shape[1]
        half_f = feats // 2
        extra_cols = -cols % 256
        if extra_cols:
            targets = jnp.pad(targets, ((0, 0), (0, extra_cols)))
            coeffs = jnp.pad(coeffs, ((0, 0), (0, extra_cols)))
        width = (cols + extra_cols) // 2
        blk = 128 * max(d for d in (1, 2, 3, 4) if width // 128 % d == 0)
        total = slots.shape[1]
        piece = total // (2 * chips)
        steps = 2 * chips - 1

        blocks = width // blk
        first = (blocks + 1) // 2 * blk
        bands = [(0, first), (first, width)] if first < width else [(0, width)]

        caps = [stage_cap(total, stage) for stage in range(bits)]
        sent = pick_points(me, theirs, points, pts_sib, half_f, caps[0])
        for stage in range(bits):
            got = lax.ppermute(
                sent, "rows", core_perm(lambda k, c, s=stage: k ^ stage_bit(s, c))
            )
            if stage == 0:
                wide = 128 * max(d for d in range(1, 9) if width // 128 % d == 0)
                t_mine, t_other = pack_targets(
                    after(me, sent), theirs, targets, caps[0], width, wide
                )
                t_sib = to_sib(t_other)
                got = after(got, t_other)
            if stage < bits - 1:
                sent = append_rows(sent, got, theirs, stage, caps[stage + 1])
        c_mine, c_other = cut_columns(after(me, sent), coeffs, width, blk)
        placed = place_rows(sent, theirs, bits - 1)
        norms = point_norms(after(points, placed), pts_sib)
        block_half = place_rows(after(got, norms, c_other), theirs, bits, placed)
        block_other = to_sib(block_half)
        c_sib = to_sib(after(c_other, block_other))
        parts = [c_mine, c_sib, t_mine, t_sib]

        left, rest, rows_along, along = build_maps(
            me, points, pts_sib, norms, block_half, block_other, inverses, slots,
            theirs,
        )

        amount, *first_sent = first_shares(
            piece, bands, slots, bits, rest, left, rows_along, parts
        )
        share = {}
        arrived = [[] for _ in bands]
        final = [[] for _ in bands]
        final_sib = [[] for _ in bands]
        early_mine = []
        early = steps - chips
        fillers = []
        latest = None

        def exchange(b, latest):
            for part in final[b][len(final_sib[b]) :]:
                final_sib[b].append(to_sib(after(part, latest)))

        for step in range(steps + 1):
            for b, band in enumerate(bands):
                if step == 0:
                    sent = first_sent[b]
                else:
                    arrived[b][-1] = after(arrived[b][-1], latest, *fillers)
                    fillers = []
                    sent = add_arrived(
                        me, *share[step], band, shift, arrived[b][-chips:], step < chips - 1
                    )
                latest = sent
                if step < steps:
                    arrived[b].append(lax.ppermute(sent, "rows", ring_perm))
                if step >= chips - 1:
                    final[b].append(sent)
                if step == steps:
                    exchange(b, latest)
                    if b == 0:
                        fillers += [part for parts in final_sib for part in parts[: steps + 1 - chips]]
            row = 2 * step + 1
            if row < 2 * chips:
                count = min(2, 2 * chips - row)
                weights = map_weights(
                    row * piece, count * piece, False, after(slots, latest), bits, rest, left,
                    None, caps[0],
                )
                more = more_shares(after(me, latest), weights, 0, count * piece, bands, parts)
                for k in range(count):
                    share[row + k] = (more, k * piece)
                fillers.append(more)
            if step == chips - 1:
                carried = [pieces[: chips - 1] for pieces in arrived]
                amount = sum_amounts(after(me, latest), amount, bands, carried)
                sel, scale = final_maps(after(me, latest), slots, along, spots, rows_here)
                fillers += [amount, scale]
            b = step - (steps - 2)
            if 0 <= b < len(bands):
                early_mine.append(
                    add_early(
                        after(me, latest), coeffs, sel, scale, amount, final[b][:early], width,
                        bands[b],
                    )
                )
                fillers.append(early_mine[-1])
            if step == steps - 1:
                amount_sib = to_sib(after(amount, early_mine[-1]))
                for b in range(len(bands)):
                    exchange(b, early_mine[-1])

        out = None
        for b, band in enumerate(bands):
            out = add_last(
                me, coeffs, early_mine[b], out, sel, scale, amount_sib, final[b][early:],
                final_sib[b], width, band,
            )
        return out[:, :cols] if extra_cols else out

    def per_device(points, targets, coeffs, block_ids, inverses):
        rows_here = points.shape[0]
        total = block_ids.size
        me = lax.axis_index("rows").astype(i32).reshape(1)
        pts_sib = to_sib(points)
        stage_bits = [[stage_bit(s, core) for s in range(bits)] for core in range(2)]
        caps = [stage_cap(total, s) for s in range(bits)]
        fits, *plans = plan(me, block_ids, rows_here, ring, stage_bits, caps)
        out = spread_path(points, targets, coeffs, inverses, pts_sib, me, *plans)

        def general(state):
            return jnp.ones_like(fits), general_path(n, points, targets, coeffs, block_ids, inverses)

        return lax.while_loop(lambda state: state[0][0] == 0, general, (fits, out))[1]

    return jax.shard_map(
        per_device,
        mesh=mesh,
        in_specs=(P("rows", None), P("rows", "labels"), P("rows", "labels"), P(), P()),
        out_specs=P("rows", "labels"),
        check_vma=False,
    )
```

```python
import jax
import jax.numpy as jnp
from jax import lax
from jax.experimental import pallas as pl
from jax.experimental.pallas import tpu as pltpu
from jax.sharding import PartitionSpec as P

ridge_weight = 0.5
bf16 = jnp.bfloat16
f32 = jnp.float32
i32 = jnp.int32
whole = pl.BlockSpec(memory_space=pltpu.VMEM)


def dot_nn(a, b):
    return lax.dot_general(a, b, (((1,), (0,)), ((), ())), preferred_element_type=f32)


def dot_nt(a, b):
    return lax.dot_general(a, b, (((1,), (1,)), ((), ())), preferred_element_type=f32)


def square_sums(pts):
    return jnp.sum(jnp.square(pts.astype(f32)), axis=1, keepdims=True)


def kernel_tile(left, right):
    inner_prod = dot_nt(left, right)
    sq_dist = jnp.maximum(square_sums(left) + square_sums(right).T - 2.0 * inner_prod, 0.0)
    return jnp.exp(-(2.0 / left.shape[1]) * sq_dist).astype(bf16)


def split_bf16(x):
    high = x.astype(bf16)
    return high, (x - high.astype(f32)).astype(bf16)


def both_parts(x):
    high, low = split_bf16(x)
    return jnp.concatenate([high.astype(f32), low.astype(f32)], axis=0).astype(bf16)


def as_row(column):
    n = column.shape[0]
    return jnp.transpose(jnp.broadcast_to(column, (n, 128)))[0:1, :]


def iota(shape, dim):
    return lax.broadcasted_iota(i32, shape, dim)


def one_hot(cond):
    return jnp.where(cond, 1.0, 0.0).astype(bf16)


def after(x, *others):
    return lax.optimization_barrier((x, *others))[0]


def params(megabytes):
    return pltpu.CompilerParams(vmem_limit_bytes=megabytes << 20)


def cost(macs, bytes_accessed):
    return pl.CostEstimate(flops=2 * macs, bytes_accessed=bytes_accessed, transcendentals=0)


def ring_sum(x, n):
    def hop(_, state):
        total, moving = state
        moving = lax.ppermute(moving, "rows", [(i, (i + 1) % n) for i in range(n)])
        return total + moving, moving

    return lax.fori_loop(0, n - 1, hop, (x, x))[0]


def general_path(n, points, targets, coeffs, block_ids, inverses):
    rows_here = points.shape[0]
    first_row = lax.axis_index("rows") * rows_here
    zero_low = jnp.zeros((), bf16)
    current = coeffs
    for blk in range(2):
        local_ids = block_ids[blk] - first_row
        inside = (local_ids >= 0) & (local_ids < rows_here)
        local_rows = jnp.clip(local_ids, 0, rows_here - 1)
        picked = jnp.where(inside[:, None], points[local_rows], zero_low)
        block_pts = ring_sum(picked, n)
        ktile = kernel_tile(points, block_pts)
        c_low = current.astype(bf16)
        sel_targets = jnp.where(inside[:, None], targets[local_rows].astype(f32), 0.0)
        sel_coeffs = jnp.where(inside[:, None], current[local_rows], 0.0)
        local_side = ridge_weight * sel_coeffs - sel_targets
        product = lax.dot_general(
            ktile, c_low, (((0,), (0,)), ((), ())), preferred_element_type=f32
        )
        negated = ring_sum(product + local_side, n)
        update = jnp.dot(
            inverses[blk], -negated, precision=lax.Precision.HIGHEST, preferred_element_type=f32
        )
        where_to = (jnp.arange(rows_here, dtype=i32)[:, None] == local_ids[None, :]).astype(f32)
        current = current + jnp.dot(
            where_to, update, precision=lax.Precision.HIGHEST, preferred_element_type=f32
        )
    return current


def plan(me, block_ids, rows, ring, stage_bits, caps):
    total = block_ids.size
    blk = block_ids.shape[1]
    chips = len(ring)
    place = [ring.index(k) for k in range(chips)]
    piece = total // (2 * chips)
    bits = len(caps)
    n_final = total - (chips - 1) * piece
    step = min(256, total)
    groups = []
    for core in range(2):
        done = 0
        for stage in range(bits):
            members = {}
            for k in range(chips):
                members.setdefault(k & ~done, []).append(k)
            groups += [(m, caps[stage]) for m in members.values()]
            done |= stage_bits[core][stage]

    def body(me_ref, ids_ref, flag_ref, slots_ref, their_ref, spots_ref, shift_ref):
        chip, core = me_ref[0] // 2, me_ref[0] % 2
        ids = jnp.concatenate([ids_ref[0:1, :], ids_ref[1:2, :]], axis=1).astype(f32)
        ids_col = jnp.transpose(jnp.broadcast_to(ids, (128, total)))
        own = jnp.floor((ids + 0.5) * (0.5 / rows))
        index = iota((1, total), 1)
        rank = jnp.zeros((1, total), f32)
        for r in range(0, total, step):
            own_col = jnp.floor((ids_col[r : r + step, 0:1] + 0.5) * (0.5 / rows))
            ahead = (own_col == own) & (r + iota((step, total), 0) < index)
            rank += jnp.sum(jnp.where(ahead, 1.0, 0.0), axis=0, keepdims=True)

        def count(which):
            return jnp.sum(jnp.where(own == which, 1.0, 0.0), axis=1, keepdims=True)

        def slots(listed):
            slot = jnp.full((1, total), -1.0, f32)
            before = jnp.zeros((1, 1), f32)
            for which in listed:
                which = which.astype(f32)
                slot = jnp.where(own == which, before + rank, slot)
                before = before + count(which)
            return slot

        counts = [count(float(k)) for k in range(chips)]
        slack = counts[0] - piece
        for k in range(1, chips):
            slack = jnp.minimum(slack, counts[k] - piece)
        for members, cap in groups:
            slack = jnp.minimum(slack, cap - sum(counts[k] for k in members))
        flag_ref[0] = (jnp.max(slack) >= 0.0).astype(i32)

        slots_ref[...] = jnp.zeros(slots_ref.shape, i32)
        group = [0]
        columns = []
        for stage in range(bits):
            bit = jnp.where(core == 0, stage_bits[0][stage], stage_bits[1][stage])
            mine = slots([chip ^ g for g in group])
            if stage == 0:
                slots_ref[0:1, :] = mine.astype(i32)
                line = iota((caps[0], total), 0).astype(f32)
                wanted = jnp.where(mine == line, ids + 1.0, 0.0)
                wanted = jnp.sum(wanted, axis=1, keepdims=True) - 1.0
            if stage == bits - 1:
                columns += [mine, slots([chip ^ bit ^ g for g in group])]
            else:
                held = sum(count((chip ^ g).astype(f32)) for g in group)
                columns.append(jnp.broadcast_to(held, (1, total)))
            group = group + [g ^ bit for g in group]
        slots_ref[7:8, :] = ids.astype(i32)
        fill = jnp.zeros((127 - len(columns), total), f32)
        columns = jnp.concatenate(columns + [fill, ids], axis=0)
        their_ref[...] = jnp.transpose(columns).astype(i32)
        their_ref[: caps[0], 126:127] = wanted.astype(i32)

        def lookup(which, table):
            out = jnp.int32(table[0])
            for k in range(1, chips):
                out = jnp.where(which == k, table[k], out)
            return out

        here = lookup(chip, place)
        way = jnp.where(core == 0, chips - 1, 1)
        listed = [lookup((here + way * (k + 1)) % chips, ring) for k in range(chips)]
        position = slots(listed)
        slots_ref[bits : bits + 1, :] = position.astype(i32)
        lag = count(listed[0].astype(f32)).astype(i32)
        length = (2 * chips - 1) * piece
        source = iota((piece, length), 0) - lag + length
        shift_ref[...] = one_hot(source == iota((piece, length), 1))
        pos_col = jnp.transpose(jnp.broadcast_to(position, (128, total)))[:, 0:1]
        line = ((chips - 1) * piece + iota((1, n_final), 1)).astype(f32)
        spots = jnp.sum(
            jnp.where(pos_col == line, ids_col[:, 0:1], 0.0), axis=0, keepdims=True
        )
        spots_ref[...] = spots.astype(i32)

    smem = pl.BlockSpec(memory_space=pltpu.SMEM)
    return pl.pallas_call(
        body,
        out_shape=[
            jax.ShapeDtypeStruct((1,), i32),
            jax.ShapeDtypeStruct((8, total), i32),
            jax.ShapeDtypeStruct((total, 128), i32),
            jax.ShapeDtypeStruct((1, n_final), i32),
            jax.ShapeDtypeStruct((piece, total - piece), bf16),
        ],
        in_specs=[smem, whole],
        out_specs=[smem, whole, whole, whole, whole],
        compiler_params=params(16),
        cost_estimate=cost(1 << 20, 1 << 20),
    )(me, block_ids)


def pick_points(me, theirs, points, sib_points, half_f, cap):
    rows = points.shape[0]

    def body(me_ref, their_ref, own_ref, sib_ref, sent_ref):
        cols = pl.ds(pl.multiple_of(me_ref[0] % 2 * half_f, 128), half_f)
        wanted = their_ref[:cap, 126:127]
        local = iota((cap, rows), 1)
        own = one_hot(wanted == local + me_ref[0] * rows)
        sib = one_hot(wanted == local + (me_ref[0] ^ 1) * rows)
        out = dot_nn(own, own_ref[:, cols]) + dot_nn(sib, sib_ref[:, cols])
        sent_ref[...] = out.astype(bf16)

    return pl.pallas_call(
        body,
        out_shape=jax.ShapeDtypeStruct((cap, half_f), bf16),
        in_specs=[pl.BlockSpec(memory_space=pltpu.SMEM)] + [whole] * 3,
        out_specs=whole,
        compiler_params=params(16),
        cost_estimate=cost(2 * cap * rows * half_f, 4 << 20),
    )(me, theirs, points, sib_points)


def append_rows(sent, got, theirs, stage, cap_next):
    cap, half_f = sent.shape

    def body(sent_ref, got_ref, their_ref, out_ref):
        held = their_ref[:cap_next, stage : stage + 1]
        behind = one_hot(iota((cap_next, cap), 0) - held == iota((cap_next, cap), 1))
        out = dot_nn(behind, got_ref[...])
        out_ref[:cap, :] = (out[:cap] + sent_ref[...].astype(f32)).astype(bf16)
        if cap_next > cap:
            out_ref[cap:, :] = out[cap:].astype(bf16)

    return pl.pallas_call(
        body,
        out_shape=jax.ShapeDtypeStruct((cap_next, half_f), bf16),
        in_specs=[whole] * 3,
        out_specs=whole,
        compiler_params=params(16),
        cost_estimate=cost(cap * cap_next * half_f, 4 << 20),
    )(sent, got, theirs)


def place_rows(packed, theirs, column, block=None):
    cap, half_f = packed.shape
    total = theirs.shape[0]

    def body(packed_ref, their_ref, *refs):
        spots = one_hot(their_ref[:, column : column + 1] == iota((total, cap), 1))
        out = dot_nn(spots, packed_ref[...])
        if block is not None:
            out += refs[0][...].astype(f32)
        refs[-1][...] = out.astype(bf16)

    return pl.pallas_call(
        body,
        out_shape=jax.ShapeDtypeStruct((total, half_f), bf16),
        in_specs=[whole] * (2 if block is None else 3),
        out_specs=whole,
        compiler_params=params(16),
        cost_estimate=cost(total * cap * half_f, 4 << 20),
    )(packed, theirs, *([] if block is None else [block]))


def point_norms(points, sib_points):
    rows = points.shape[0]

    def body(own_ref, sib_ref, out_ref):
        for k, ref in enumerate((own_ref, sib_ref)):
            norm = square_sums(ref[...])
            out_ref[k * rows : (k + 1) * rows, :] = jnp.broadcast_to(norm, (rows, 128))

    return pl.pallas_call(
        body,
        out_shape=jax.ShapeDtypeStruct((2 * rows, 128), f32),
        in_specs=[whole] * 2,
        out_specs=whole,
        compiler_params=params(16),
        cost_estimate=cost(4 << 20, 3 << 20),
    )(points, sib_points)


def cut_columns(me, x, width, blk):
    rows = x.shape[0]

    def body(me_ref, mine_ref, other_ref, mine_out, other_out):
        mine_out[...] = mine_ref[...].astype(bf16)
        other_out[...] = other_ref[...].astype(bf16)

    def half(k):
        return pl.BlockSpec(
            (rows, blk), lambda j, me_ref: (0, (me_ref[0] ^ k) % 2 * (width // blk) + j)
        )

    plain = pl.BlockSpec((rows, blk), lambda j, me_ref: (0, j))
    return pl.pallas_call(
        body,
        out_shape=[jax.ShapeDtypeStruct((rows, width), bf16)] * 2,
        grid_spec=pltpu.PrefetchScalarGridSpec(
            num_scalar_prefetch=1,
            grid=(width // blk,),
            in_specs=[half(0), half(1)],
            out_specs=[plain] * 2,
        ),
        compiler_params=params(16),
        cost_estimate=cost(0, rows * width * 8),
    )(me, x, x)


def pack_targets(me, theirs, targets, cap, width, blk):
    rows = targets.shape[0]

    def body(me_ref, their_ref, mine_ref, other_ref, mine_out, other_out):
        local = iota((cap, rows), 1) + me_ref[0] * rows
        pick = one_hot(their_ref[:cap, 126:127] == local)
        mine_out[...] = dot_nn(pick, mine_ref[...]).astype(bf16)
        other_out[...] = dot_nn(pick, other_ref[...]).astype(bf16)

    def half(k):
        return pl.BlockSpec(
            (rows, blk), lambda j, me_ref: (0, (me_ref[0] ^ k) % 2 * (width // blk) + j)
        )

    plain = pl.BlockSpec((cap, blk), lambda j, me_ref: (0, j))
    return pl.pallas_call(
        body,
        out_shape=[jax.ShapeDtypeStruct((cap, width), bf16)] * 2,
        grid_spec=pltpu.PrefetchScalarGridSpec(
            num_scalar_prefetch=1,
            grid=(width // blk,),
            in_specs=[whole, half(0), half(1)],
            out_specs=[plain] * 2,
        ),
        compiler_params=params(16),
        cost_estimate=cost(2 * cap * rows * width, rows * width * 8),
    )(me, theirs, targets, targets)


def build_maps(me, points, sib_points, norms_in, q_half, q_other, inverses, slots, theirs):
    rows, feats = points.shape
    half_f = feats // 2
    total = slots.shape[1]
    blk = total // 2
    step = min(256, rows, blk)
    scale = -(2.0 / feats)

    def body(
        me_ref, own_ref, sib_ref, pn_ref, qh_ref, qo_ref, inv_ref, idr_ref, idc_ref,
        left_ref, rest_ref, rows_ref, along_ref, norm_ref,
    ):
        mine = pl.ds(pl.multiple_of(me_ref[0] % 2 * half_f, 128), half_f)
        other = pl.ds(pl.multiple_of((1 - me_ref[0] % 2) * half_f, 128), half_f)
        for r in range(0, total, step):
            part = square_sums(qh_ref[r : r + step, :]) + square_sums(qo_ref[r : r + step, :])
            norm_ref[r : r + step, :] = jnp.broadcast_to(part, (step, 128))
        norms = jnp.transpose(norm_ref[...])[0:1, :]

        def values(a, b, a_sq, b_sq, same):
            inner = dot_nt(a[0], b[0]) + dot_nt(a[1], b[1])
            sq_dist = jnp.maximum(a_sq + b_sq - 2.0 * inner, 0.0)
            k = jnp.exp(scale * sq_dist).astype(bf16).astype(f32)
            return (k + jnp.where(same, ridge_weight, 0.0)).astype(bf16)

        cross = []
        for r in range(blk, total, step):
            at = slice(r, r + step)
            cross.append(
                values(
                    (qh_ref[at, :], qo_ref[at, :]),
                    (qh_ref[:blk, :], qo_ref[:blk, :]),
                    norm_ref[at, 0:1],
                    norms[:, :blk],
                    idc_ref[at, 127:128] == idr_ref[7:8, :blk],
                )
            )
        cross = jnp.concatenate(cross, axis=0)
        inv0, inv1 = inv_ref[0], inv_ref[1]
        high0, low0 = split_bf16(inv0)
        high1, low1 = split_bf16(inv1)
        high, low = split_bf16(dot_nn(cross, high0) + dot_nn(cross, low0))
        lower = -(dot_nn(high1, high) + dot_nn(high1, low) + dot_nn(low1, high))

        bell = jnp.exp(-scale * (jnp.min(norms) - norms))

        def direction(inv, weights):
            way = jnp.sum(inv * weights, axis=1, keepdims=True)
            return way * lax.rsqrt(jnp.maximum(jnp.sum(way * way), 1e-30))

        way0 = direction(inv0, bell[:, :blk])
        way1 = direction(inv1, bell[:, blk:])
        row00 = jnp.sum(way0 * inv0, axis=0, keepdims=True)
        row10 = jnp.sum(way1 * lower, axis=0, keepdims=True)
        row11 = jnp.sum(way1 * inv1, axis=0, keepdims=True)
        rest_ref[:blk, :blk] = (inv0 - way0 * row00).astype(bf16)
        rest_ref[:blk, blk:] = jnp.zeros((blk, blk), bf16)
        rest_ref[blk:, :blk] = (lower - way1 * row10).astype(bf16)
        rest_ref[blk:, blk:] = (inv1 - way1 * row11).astype(bf16)
        rows_ref[...] = jnp.zeros((8, total), f32)
        rows_ref[0:1, :blk] = row00
        rows_ref[1:2, :blk] = row10
        rows_ref[1:2, blk:] = row11
        along_ref[...] = jnp.zeros((8, total), f32)
        along_ref[0:1, :blk] = as_row(way0)
        along_ref[1:2, blk:] = as_row(way1)

        for which, ref in enumerate((own_ref, sib_ref)):
            for r in range(0, rows, step):
                at = slice(r, r + step)
                a = (ref[at, mine], ref[at, other])
                spot = (me_ref[0] ^ which) * rows + r + iota((step, total), 0)
                left_ref[which * rows + r : which * rows + r + step, :] = -values(
                    a,
                    (qh_ref[...], qo_ref[...]),
                    pn_ref[which * rows + r : which * rows + r + step, 0:1],
                    norms,
                    spot == idr_ref[7:8, :],
                )

    return pl.pallas_call(
        body,
        out_shape=[
            jax.ShapeDtypeStruct((2 * rows, total), bf16),
            jax.ShapeDtypeStruct((total, total), bf16),
            jax.ShapeDtypeStruct((8, total), f32),
            jax.ShapeDtypeStruct((8, total), f32),
        ],
        in_specs=[pl.BlockSpec(memory_space=pltpu.SMEM)] + [whole] * 8,
        out_specs=[whole] * 4,
        scratch_shapes=[pltpu.VMEM((total, 128), f32)],
        compiler_params=params(24),
        cost_estimate=cost(4 * rows * total * feats, 12 << 20),
    )(me, points, sib_points, norms_in, q_half, q_other, inverses, slots, theirs)


def map_weights(lo, count, extra, slots, pos_row, rest, left, rows_along, cap):
    points, total = left.shape

    def fill(slots_ref, rest_ref, left_ref, along_ref, weights):
        sel = one_hot(slots_ref[pos_row : pos_row + 1, :] == lo + iota((count, total), 0))
        moved = dot_nn(sel, rest_ref[...]).astype(bf16)
        if extra:
            moved = jnp.concatenate([moved, both_parts(along_ref[...])], axis=0)
        pack = one_hot(iota((cap, total), 0) == slots_ref[0:1, :])
        for at, other in ((slice(0, points), left_ref[...]), (slice(points, points + cap), pack)):
            mapped = dot_nt(moved, other)
            weights[:count, at] = mapped[:count].astype(bf16)
            if extra:
                both = mapped[count : count + 8] + mapped[count + 8 :]
                weights[count:, at] = both_parts(both)

    if extra:
        return fill

    def body(slots_ref, rest_ref, left_ref, out_ref):
        fill(slots_ref, rest_ref, left_ref, None, out_ref)

    return pl.pallas_call(
        body,
        out_shape=jax.ShapeDtypeStruct((count, points + cap), bf16),
        in_specs=[whole] * 3,
        out_specs=whole,
        compiler_params=params(20),
        cost_estimate=cost(count * (2 * points + cap) * total, 6 << 20),
    )(slots, rest, left)


def strips_of(bands):
    return [(k, min(k + 512, end)) for at, end in bands for k in range(at, end, 512)]


def strip_of(refs, at, end):
    targets = refs[2][:, at:end] + refs[3][:, at:end]
    return jnp.concatenate([refs[0][:, at:end], refs[1][:, at:end], targets], axis=0)


def first_shares(piece, bands, slots, pos_row, rest, left, rows_along, parts):
    width, cap = parts[0].shape[1], parts[-1].shape[0]
    height, depth = piece + 16, left.shape[0] + cap
    fill = map_weights(0, piece, True, slots, pos_row, rest, left, rows_along, cap)

    def body(slots_ref, rest_ref, left_ref, along_ref, *refs):
        part_refs, refs = refs[: len(parts)], refs[len(parts) :]
        amount_ref, band_refs, weights = refs[0], refs[1:-1], refs[-1]
        fill(slots_ref, rest_ref, left_ref, along_ref, weights)
        for at, end in strips_of(bands):
            out = dot_nn(weights[...], strip_of(part_refs, at, end))
            amount_ref[:, at:end] = out[piece : piece + 8] + out[piece + 8 :]
            for band, ref in zip(bands, band_refs):
                if band[0] <= at < band[1]:
                    strip = slice(at - band[0], end - band[0])
                    ref[:piece, strip] = out[:piece].astype(bf16)
                    ref[piece:, strip] = both_parts(out[piece : piece + 8] + out[piece + 8 :])

    out_shape = [jax.ShapeDtypeStruct((8, width), f32)]
    out_shape += [jax.ShapeDtypeStruct((piece + 16, end - at), bf16) for at, end in bands]
    return pl.pallas_call(
        body,
        out_shape=out_shape,
        in_specs=[whole] * (4 + len(parts)),
        out_specs=[whole] * len(out_shape),
        scratch_shapes=[pltpu.VMEM((height, depth), bf16)],
        compiler_params=params(20),
        cost_estimate=cost(height * depth * (width + 1024), 12 << 20),
    )(slots, rest, left, rows_along, *parts)


def more_shares(me, weights, lo, count, bands, parts):
    depth, width = weights.shape[1], parts[0].shape[1]

    def body(me_ref, weights_ref, *refs):
        for at, end in strips_of(bands):
            strip = strip_of(refs, at, end)
            refs[-1][:, at:end] = dot_nn(weights_ref[lo : lo + count, :], strip)

    return pl.pallas_call(
        body,
        out_shape=jax.ShapeDtypeStruct((count, width), f32),
        in_specs=[pl.BlockSpec(memory_space=pltpu.SMEM)] + [whole] * (1 + len(parts)),
        out_specs=whole,
        compiler_params=params(16),
        cost_estimate=cost(count * depth * width, 10 << 20),
    )(me, weights, *parts)


def add_arrived(me, share, row, band, shift, arrived, carry):
    piece, length = shift.shape
    n = len(arrived)

    def body(me_ref, share_ref, shift_ref, *refs):
        out = share_ref[row : row + piece, band[0] : band[1]]
        for k, ref in enumerate(refs[:-1]):
            at = length - (n - k) * piece
            out += dot_nn(shift_ref[:, at : at + piece], ref[:piece, :])
        refs[-1][:piece, :] = out.astype(bf16)
        if carry:
            refs[-1][piece:, :] = refs[-2][piece:, :]

    height = piece + (16 if carry else 0)
    return pl.pallas_call(
        body,
        out_shape=jax.ShapeDtypeStruct((height, band[1] - band[0]), bf16),
        in_specs=[pl.BlockSpec(memory_space=pltpu.SMEM)] + [whole] * (2 + n),
        out_specs=whole,
        compiler_params=params(12),
        cost_estimate=cost(n * piece * piece * (band[1] - band[0]), 6 << 20),
    )(me, share, shift, *arrived)


def sum_amounts(me, amount, bands, arrived):
    piece = arrived[0][0].shape[0] - 16

    def body(me_ref, amount_ref, *refs):
        out_ref, refs = refs[-1], list(refs[:-1])
        for (at, end), pieces in zip(bands, arrived):
            out = amount_ref[:, at:end]
            for _ in pieces:
                both = refs.pop(0)[piece:, :].astype(f32)
                out += both[:8] + both[8:]
            out_ref[:, at:end] = out

    return pl.pallas_call(
        body,
        out_shape=jax.ShapeDtypeStruct(amount.shape, f32),
        in_specs=[pl.BlockSpec(memory_space=pltpu.SMEM)] + [whole] * (1 + sum(map(len, arrived))),
        out_specs=whole,
        compiler_params=params(12),
        cost_estimate=cost(0, 2 << 20),
    )(me, amount, *[ref for pieces in arrived for ref in pieces])


def final_maps(me, slots, along, spots, rows):
    total, n = slots.shape[1], spots.shape[1]

    def body(me_ref, slots_ref, along_ref, spots_ref, sel_ref, scale_ref):
        first = me_ref[0] * rows
        sel_ref[...] = one_hot(first + iota((rows, n), 0) == spots_ref[...])
        same = first + iota((rows, total), 0) == slots_ref[7:8, :]
        scale_ref[...] = jnp.zeros((rows, 128), f32)
        for b in range(2):
            weight = jnp.where(same, along_ref[b : b + 1, :], 0.0)
            scale_ref[:, b : b + 1] = jnp.sum(weight, axis=1, keepdims=True)

    return pl.pallas_call(
        body,
        out_shape=[jax.ShapeDtypeStruct((rows, n), bf16), jax.ShapeDtypeStruct((rows, 128), f32)],
        in_specs=[pl.BlockSpec(memory_space=pltpu.SMEM)] + [whole] * 3,
        out_specs=[whole] * 2,
        compiler_params=params(16),
        cost_estimate=cost(1 << 20, 3 << 20),
    )(me, slots, along, spots)


def strips_in(span):
    return [(k, min(k + 512, span)) for k in range(0, span, 512)]


def add_early(me, other, coeffs, sel, scale, amount, pieces, width, band):
    rows, span = coeffs.shape[0], band[1] - band[0]
    n, piece = len(pieces), pieces[0].shape[0]
    strips = strips_in(span)

    def body(me_ref, src_ref, sel_ref, scale_ref, amount_ref, *refs):
        out_ref, arrivals = refs[-2:]
        first = (me_ref[0] ^ other) % 2 * width + band[0]
        copies = []
        for i, (at, end) in enumerate(strips):
            cols = pl.ds(pl.multiple_of(first + at, 128), end - at)
            copy = pltpu.make_async_copy(src_ref.at[:, cols], out_ref.at[:, at:end], arrivals.at[i])
            copy.start()
            copies.append(copy)
        for copy, (at, end) in zip(copies, strips):
            strip = jnp.concatenate([ref[:, at:end] for ref in refs[:n]], axis=0)
            out = dot_nn(sel_ref[:, : n * piece], strip)
            for b in range(2):
                row = amount_ref[b : b + 1, band[0] + at : band[0] + end]
                out += scale_ref[:, b : b + 1] * row
            copy.wait()
            out_ref[:, at:end] += out

    return pl.pallas_call(
        body,
        out_shape=jax.ShapeDtypeStruct((rows, span), f32),
        in_specs=[
            pl.BlockSpec(memory_space=pltpu.SMEM),
            pl.BlockSpec(memory_space=pl.ANY),
            *[whole] * (3 + n),
        ],
        out_specs=whole,
        scratch_shapes=[pltpu.SemaphoreType.DMA((len(strips),))],
        compiler_params=params(12),
        cost_estimate=cost(rows * n * piece * span, rows * span * 8),
    )(me, coeffs, sel, scale, amount, *pieces)


def add_last(me, early, cols, buffer, sel, mine, sib, width, band):
    rows, span = sel.shape[0], band[1] - band[0]
    n, piece = len(mine), mine[0].shape[0]
    strips = strips_in(span)

    def body(me_ref, sel_ref, early_mine, early_sib, *refs):
        out_ref, held, departures = refs[-3:]
        chosen = sel_ref[:, sel_ref.shape[1] - n * piece :]
        copies = []
        for k, early_ref in enumerate((early_mine, early_sib)):
            first = (me_ref[0] ^ k) % 2 * width + band[0]
            for i, (at, end) in enumerate(strips):
                strip = jnp.concatenate([ref[:, at:end] for ref in refs[k * n : k * n + n]], axis=0)
                held[k, :, at:end] = early_ref[:, at:end] + dot_nn(chosen, strip)
                cut = pl.ds(pl.multiple_of(first + at, 128), end - at)
                copy = pltpu.make_async_copy(
                    held.at[k, :, at:end], out_ref.at[:, cut], departures.at[k * len(strips) + i]
                )
                copy.start()
                copies.append(copy)
        for copy in copies:
            copy.wait()

    operands = [sel, *early, *mine, *sib]
    in_specs = [pl.BlockSpec(memory_space=pltpu.SMEM)] + [whole] * len(operands)
    aliases = {}
    if buffer is not None:
        aliases = {1 + len(operands): 0}
        operands.append(buffer)
        in_specs.append(pl.BlockSpec(memory_space=pl.ANY))
    return pl.pallas_call(
        body,
        out_shape=pltpu.HBM((rows, cols), f32),
        in_specs=in_specs,
        out_specs=pl.BlockSpec(memory_space=pltpu.HBM),
        scratch_shapes=[
            pltpu.VMEM((2, rows, span), f32),
            pltpu.SemaphoreType.DMA((2 * len(strips),)),
        ],
        input_output_aliases=aliases,
        compiler_params=params(12),
        cost_estimate=cost(rows * n * piece * 2 * span, rows * 2 * span * 8),
    )(me, *operands)


def solution(mesh):
    n = mesh.shape["rows"]
    chips = n // 2
    bits = chips.bit_length() - 1
    ring = [k ^ (k >> 1) for k in range(chips)]
    place = [ring.index(k) for k in range(chips)]

    def core_perm(chip_of):
        return [(i, 2 * chip_of(i // 2, i % 2) + i % 2) for i in range(n)]

    sib_perm = [(i, i ^ 1) for i in range(n)]
    ring_perm = core_perm(
        lambda chip, core: ring[(place[chip] + (1 if core == 0 else chips - 1)) % chips]
    )

    def stage_bit(stage, core):
        return 1 << (stage if core == 0 else bits - 1 - stage)

    def to_sib(x):
        return lax.ppermute(x, "rows", sib_perm)

    def stage_cap(total, stage):
        return min(total, total // 2 + ((1 << stage) - 1) * (total // chips))

    def spread_path(points, targets, coeffs, inverses, pts_sib, me, slots, theirs, spots, shift):
        rows_here, feats = points.shape
        cols = coeffs.shape[1]
        half_f = feats // 2
        extra_cols = -cols % 256
        if extra_cols:
            targets = jnp.pad(targets, ((0, 0), (0, extra_cols)))
            coeffs = jnp.pad(coeffs, ((0, 0), (0, extra_cols)))
        width = (cols + extra_cols) // 2
        blk = 128 * max(d for d in (1, 2, 3, 4) if width // 128 % d == 0)
        total = slots.shape[1]
        piece = total // (2 * chips)
        steps = 2 * chips - 1

        blocks = width // blk
        first = (blocks + 1) // 2 * blk
        bands = [(0, first), (first, width)] if first < width else [(0, width)]

        caps = [stage_cap(total, stage) for stage in range(bits)]
        sent = pick_points(me, theirs, points, pts_sib, half_f, caps[0])
        for stage in range(bits):
            got = lax.ppermute(
                sent, "rows", core_perm(lambda k, c, s=stage: k ^ stage_bit(s, c))
            )
            if stage == 0:
                wide = 128 * max(d for d in range(1, 9) if width // 128 % d == 0)
                t_mine, t_other = pack_targets(
                    after(me, sent), theirs, targets, caps[0], width, wide
                )
                t_sib = to_sib(t_other)
                got = after(got, t_other)
            if stage < bits - 1:
                sent = append_rows(sent, got, theirs, stage, caps[stage + 1])
        c_mine, c_other = cut_columns(after(me, sent), coeffs, width, blk)
        placed = place_rows(sent, theirs, bits - 1)
        norms = point_norms(after(points, placed), pts_sib)
        block_half = place_rows(after(got, norms, c_other), theirs, bits, placed)
        block_other = to_sib(block_half)
        c_sib = to_sib(after(c_other, block_other))
        parts = [c_mine, c_sib, t_mine, t_sib]

        left, rest, rows_along, along = build_maps(
            me, points, pts_sib, norms, block_half, block_other, inverses, slots,
            theirs,
        )

        amount, *first_sent = first_shares(
            piece, bands, slots, bits, rest, left, rows_along, parts
        )
        share = {}
        arrived = [[] for _ in bands]
        final = [[] for _ in bands]
        final_sib = [[] for _ in bands]
        early_mine, early_sib = [], []
        early = steps - chips
        fillers = []
        latest = None

        def exchange(b, latest):
            for part in final[b][len(final_sib[b]) :]:
                final_sib[b].append(to_sib(after(part, latest)))

        def early_of(other, b, amounts, pieces, me_then):
            return add_early(
                me_then, other, coeffs, sel, scale, amounts, pieces[b][:early], width, bands[b]
            )

        for step in range(steps + 1):
            for b, band in enumerate(bands):
                if step == 0:
                    sent = first_sent[b]
                else:
                    arrived[b][-1] = after(arrived[b][-1], latest, *fillers)
                    fillers = []
                    sent = add_arrived(
                        me, *share[step], band, shift, arrived[b][-chips:], step < chips - 1
                    )
                latest = sent
                if step < steps:
                    arrived[b].append(lax.ppermute(sent, "rows", ring_perm))
                if step >= chips - 1:
                    final[b].append(sent)
                if step == steps - 1 and b + 1 < len(bands):
                    early_mine.append(early_of(0, b + 1, amount, final, after(me, latest)))
                    fillers.append(early_mine[-1])
                if step == steps:
                    exchange(b, latest)
                    if b == 0:
                        fillers += early_sib[1:]
            row = 2 * step + 1
            if row < 2 * chips:
                count = min(2, 2 * chips - row)
                weights = map_weights(
                    row * piece, count * piece, False, after(slots, latest), bits, rest, left,
                    None, caps[0],
                )
                more = more_shares(after(me, latest), weights, 0, count * piece, bands, parts)
                for k in range(count):
                    share[row + k] = (more, k * piece)
                fillers.append(more)
            if step == chips - 1:
                carried = [pieces[: chips - 1] for pieces in arrived]
                amount = sum_amounts(after(me, latest), amount, bands, carried)
                sel, scale = final_maps(after(me, latest), slots, along, spots, rows_here)
                fillers += [amount, scale]
            if step == steps - 2:
                early_mine.append(early_of(0, 0, amount, final, after(me, latest)))
                amount_sib = to_sib(after(amount, latest))
                fillers += [early_mine[0], amount_sib]
            if step == steps - 1:
                for b in range(len(bands)):
                    exchange(b, latest)
                for b in range(len(bands)):
                    early_sib.append(early_of(1, b, amount_sib, final_sib, me))
                fillers.append(early_sib[0])

        out = None
        for b, band in enumerate(bands):
            out = add_last(
                me, (early_mine[b], early_sib[b]), cols + extra_cols, out, sel,
                final[b][early:], final_sib[b][early:], width, band,
            )
        return out[:, :cols] if extra_cols else out

    def per_device(points, targets, coeffs, block_ids, inverses):
        rows_here = points.shape[0]
        total = block_ids.size
        me = lax.axis_index("rows").astype(i32).reshape(1)
        pts_sib = to_sib(points)
        stage_bits = [[stage_bit(s, core) for s in range(bits)] for core in range(2)]
        caps = [stage_cap(total, s) for s in range(bits)]
        fits, *plans = plan(me, block_ids, rows_here, ring, stage_bits, caps)
        out = spread_path(points, targets, coeffs, inverses, pts_sib, me, *plans)

        def general(state):
            return jnp.ones_like(fits), general_path(n, points, targets, coeffs, block_ids, inverses)

        return lax.while_loop(lambda state: state[0][0] == 0, general, (fits, out))[1]

    return jax.shard_map(
        per_device,
        mesh=mesh,
        in_specs=(P("rows", None), P("rows", "labels"), P("rows", "labels"), P(), P()),
        out_specs=P("rows", "labels"),
        check_vma=False,
    )
```

```python
import jax
import jax.numpy as jnp
from jax import lax
from jax.experimental import pallas as pl
from jax.experimental.pallas import tpu as pltpu
from jax.sharding import PartitionSpec as P

ridge_weight = 0.5
bf16 = jnp.bfloat16
f32 = jnp.float32
i32 = jnp.int32
whole = pl.BlockSpec(memory_space=pltpu.VMEM)


def dot_nn(a, b):
    return lax.dot_general(a, b, (((1,), (0,)), ((), ())), preferred_element_type=f32)


def dot_nt(a, b):
    return lax.dot_general(a, b, (((1,), (1,)), ((), ())), preferred_element_type=f32)


def square_sums(pts):
    return jnp.sum(jnp.square(pts.astype(f32)), axis=1, keepdims=True)


def kernel_tile(left, right):
    inner_prod = dot_nt(left, right)
    sq_dist = jnp.maximum(square_sums(left) + square_sums(right).T - 2.0 * inner_prod, 0.0)
    return jnp.exp(-(2.0 / left.shape[1]) * sq_dist).astype(bf16)


def split_bf16(x):
    high = x.astype(bf16)
    return high, (x - high.astype(f32)).astype(bf16)


def both_parts(x):
    high, low = split_bf16(x)
    return jnp.concatenate([high.astype(f32), low.astype(f32)], axis=0).astype(bf16)


def as_row(column):
    n = column.shape[0]
    return jnp.transpose(jnp.broadcast_to(column, (n, 128)))[0:1, :]


def iota(shape, dim):
    return lax.broadcasted_iota(i32, shape, dim)


def one_hot(cond):
    return jnp.where(cond, 1.0, 0.0).astype(bf16)


def after(x, *others):
    return lax.optimization_barrier((x, *others))[0]


def params(megabytes):
    return pltpu.CompilerParams(vmem_limit_bytes=megabytes << 20)


def cost(macs, bytes_accessed):
    return pl.CostEstimate(flops=2 * macs, bytes_accessed=bytes_accessed, transcendentals=0)


def ring_sum(x, n):
    def hop(_, state):
        total, moving = state
        moving = lax.ppermute(moving, "rows", [(i, (i + 1) % n) for i in range(n)])
        return total + moving, moving

    return lax.fori_loop(0, n - 1, hop, (x, x))[0]


def general_path(n, points, targets, coeffs, block_ids, inverses):
    rows_here = points.shape[0]
    first_row = lax.axis_index("rows") * rows_here
    zero_low = jnp.zeros((), bf16)
    current = coeffs
    for blk in range(2):
        local_ids = block_ids[blk] - first_row
        inside = (local_ids >= 0) & (local_ids < rows_here)
        local_rows = jnp.clip(local_ids, 0, rows_here - 1)
        picked = jnp.where(inside[:, None], points[local_rows], zero_low)
        block_pts = ring_sum(picked, n)
        ktile = kernel_tile(points, block_pts)
        c_low = current.astype(bf16)
        sel_targets = jnp.where(inside[:, None], targets[local_rows].astype(f32), 0.0)
        sel_coeffs = jnp.where(inside[:, None], current[local_rows], 0.0)
        local_side = ridge_weight * sel_coeffs - sel_targets
        product = lax.dot_general(
            ktile, c_low, (((0,), (0,)), ((), ())), preferred_element_type=f32
        )
        negated = ring_sum(product + local_side, n)
        update = jnp.dot(
            inverses[blk], -negated, precision=lax.Precision.HIGHEST, preferred_element_type=f32
        )
        where_to = (jnp.arange(rows_here, dtype=i32)[:, None] == local_ids[None, :]).astype(f32)
        current = current + jnp.dot(
            where_to, update, precision=lax.Precision.HIGHEST, preferred_element_type=f32
        )
    return current


def plan(me, block_ids, rows, ring, stage_bits, caps):
    total = block_ids.size
    blk = block_ids.shape[1]
    chips = len(ring)
    place = [ring.index(k) for k in range(chips)]
    piece = total // (2 * chips)
    bits = len(caps)
    n_final = total - (chips - 1) * piece
    step = min(256, total)
    groups = []
    for core in range(2):
        done = 0
        for stage in range(bits):
            members = {}
            for k in range(chips):
                members.setdefault(k & ~done, []).append(k)
            groups += [(m, caps[stage]) for m in members.values()]
            done |= stage_bits[core][stage]

    def body(me_ref, ids_ref, flag_ref, slots_ref, their_ref, spots_ref, shift_ref):
        chip, core = me_ref[0] // 2, me_ref[0] % 2
        ids = jnp.concatenate([ids_ref[0:1, :], ids_ref[1:2, :]], axis=1).astype(f32)
        ids_col = jnp.transpose(jnp.broadcast_to(ids, (128, total)))
        own = jnp.floor((ids + 0.5) * (0.5 / rows))
        index = iota((1, total), 1)
        rank = jnp.zeros((1, total), f32)
        for r in range(0, total, step):
            own_col = jnp.floor((ids_col[r : r + step, 0:1] + 0.5) * (0.5 / rows))
            ahead = (own_col == own) & (r + iota((step, total), 0) < index)
            rank += jnp.sum(jnp.where(ahead, 1.0, 0.0), axis=0, keepdims=True)

        def count(which):
            return jnp.sum(jnp.where(own == which, 1.0, 0.0), axis=1, keepdims=True)

        def slots(listed):
            slot = jnp.full((1, total), -1.0, f32)
            before = jnp.zeros((1, 1), f32)
            for which in listed:
                which = which.astype(f32)
                slot = jnp.where(own == which, before + rank, slot)
                before = before + count(which)
            return slot

        counts = [count(float(k)) for k in range(chips)]
        slack = counts[0] - piece
        for k in range(1, chips):
            slack = jnp.minimum(slack, counts[k] - piece)
        for members, cap in groups:
            slack = jnp.minimum(slack, cap - sum(counts[k] for k in members))
        flag_ref[0] = (jnp.max(slack) >= 0.0).astype(i32)

        slots_ref[...] = jnp.zeros(slots_ref.shape, i32)
        group = [0]
        columns = []
        for stage in range(bits):
            bit = jnp.where(core == 0, stage_bits[0][stage], stage_bits[1][stage])
            mine = slots([chip ^ g for g in group])
            if stage == 0:
                slots_ref[0:1, :] = mine.astype(i32)
                line = iota((caps[0], total), 0).astype(f32)
                wanted = jnp.where(mine == line, ids + 1.0, 0.0)
                wanted = jnp.sum(wanted, axis=1, keepdims=True) - 1.0
            if stage == bits - 1:
                columns += [mine, slots([chip ^ bit ^ g for g in group])]
            else:
                held = sum(count((chip ^ g).astype(f32)) for g in group)
                columns.append(jnp.broadcast_to(held, (1, total)))
            group = group + [g ^ bit for g in group]
        slots_ref[7:8, :] = ids.astype(i32)
        fill = jnp.zeros((127 - len(columns), total), f32)
        columns = jnp.concatenate(columns + [fill, ids], axis=0)
        their_ref[...] = jnp.transpose(columns).astype(i32)
        their_ref[: caps[0], 126:127] = wanted.astype(i32)

        def lookup(which, table):
            out = jnp.int32(table[0])
            for k in range(1, chips):
                out = jnp.where(which == k, table[k], out)
            return out

        here = lookup(chip, place)
        way = jnp.where(core == 0, chips - 1, 1)
        listed = [lookup((here + way * (k + 1)) % chips, ring) for k in range(chips)]
        position = slots(listed)
        slots_ref[bits : bits + 1, :] = position.astype(i32)
        lag = count(listed[0].astype(f32)).astype(i32)
        length = (2 * chips - 1) * piece
        source = iota((piece, length), 0) - lag + length
        shift_ref[...] = one_hot(source == iota((piece, length), 1))
        pos_col = jnp.transpose(jnp.broadcast_to(position, (128, total)))[:, 0:1]
        line = ((chips - 1) * piece + iota((1, n_final), 1)).astype(f32)
        spots = jnp.sum(
            jnp.where(pos_col == line, ids_col[:, 0:1], 0.0), axis=0, keepdims=True
        )
        spots_ref[...] = spots.astype(i32)

    smem = pl.BlockSpec(memory_space=pltpu.SMEM)
    return pl.pallas_call(
        body,
        out_shape=[
            jax.ShapeDtypeStruct((1,), i32),
            jax.ShapeDtypeStruct((8, total), i32),
            jax.ShapeDtypeStruct((total, 128), i32),
            jax.ShapeDtypeStruct((1, n_final), i32),
            jax.ShapeDtypeStruct((piece, total - piece), bf16),
        ],
        in_specs=[smem, whole],
        out_specs=[smem, whole, whole, whole, whole],
        compiler_params=params(16),
        cost_estimate=cost(1 << 20, 1 << 20),
    )(me, block_ids)


def pick_points(me, theirs, points, sib_points, half_f, cap):
    rows = points.shape[0]

    def body(me_ref, their_ref, own_ref, sib_ref, sent_ref):
        cols = pl.ds(pl.multiple_of(me_ref[0] % 2 * half_f, 128), half_f)
        wanted = their_ref[:cap, 126:127]
        local = iota((cap, rows), 1)
        own = one_hot(wanted == local + me_ref[0] * rows)
        sib = one_hot(wanted == local + (me_ref[0] ^ 1) * rows)
        out = dot_nn(own, own_ref[:, cols]) + dot_nn(sib, sib_ref[:, cols])
        sent_ref[...] = out.astype(bf16)

    return pl.pallas_call(
        body,
        out_shape=jax.ShapeDtypeStruct((cap, half_f), bf16),
        in_specs=[pl.BlockSpec(memory_space=pltpu.SMEM)] + [whole] * 3,
        out_specs=whole,
        compiler_params=params(16),
        cost_estimate=cost(2 * cap * rows * half_f, 4 << 20),
    )(me, theirs, points, sib_points)


def append_rows(sent, got, theirs, stage, cap_next):
    cap, half_f = sent.shape

    def body(sent_ref, got_ref, their_ref, out_ref):
        held = their_ref[:cap_next, stage : stage + 1]
        behind = one_hot(iota((cap_next, cap), 0) - held == iota((cap_next, cap), 1))
        out = dot_nn(behind, got_ref[...])
        out_ref[:cap, :] = (out[:cap] + sent_ref[...].astype(f32)).astype(bf16)
        if cap_next > cap:
            out_ref[cap:, :] = out[cap:].astype(bf16)

    return pl.pallas_call(
        body,
        out_shape=jax.ShapeDtypeStruct((cap_next, half_f), bf16),
        in_specs=[whole] * 3,
        out_specs=whole,
        compiler_params=params(16),
        cost_estimate=cost(cap * cap_next * half_f, 4 << 20),
    )(sent, got, theirs)


def place_rows(packed, theirs, column, block=None):
    cap, half_f = packed.shape
    total = theirs.shape[0]

    def body(packed_ref, their_ref, *refs):
        spots = one_hot(their_ref[:, column : column + 1] == iota((total, cap), 1))
        out = dot_nn(spots, packed_ref[...])
        if block is not None:
            out += refs[0][...].astype(f32)
        refs[-1][...] = out.astype(bf16)

    return pl.pallas_call(
        body,
        out_shape=jax.ShapeDtypeStruct((total, half_f), bf16),
        in_specs=[whole] * (2 if block is None else 3),
        out_specs=whole,
        compiler_params=params(16),
        cost_estimate=cost(total * cap * half_f, 4 << 20),
    )(packed, theirs, *([] if block is None else [block]))


def point_norms(points, sib_points):
    rows = points.shape[0]

    def body(own_ref, sib_ref, out_ref):
        for k, ref in enumerate((own_ref, sib_ref)):
            norm = square_sums(ref[...])
            out_ref[k * rows : (k + 1) * rows, :] = jnp.broadcast_to(norm, (rows, 128))

    return pl.pallas_call(
        body,
        out_shape=jax.ShapeDtypeStruct((2 * rows, 128), f32),
        in_specs=[whole] * 2,
        out_specs=whole,
        compiler_params=params(16),
        cost_estimate=cost(4 << 20, 3 << 20),
    )(points, sib_points)


def cut_columns(me, x, width, blk):
    rows = x.shape[0]

    def body(me_ref, mine_ref, other_ref, mine_out, other_out):
        mine_out[...] = mine_ref[...].astype(bf16)
        other_out[...] = other_ref[...].astype(bf16)

    def half(k):
        return pl.BlockSpec(
            (rows, blk), lambda j, me_ref: (0, (me_ref[0] ^ k) % 2 * (width // blk) + j)
        )

    plain = pl.BlockSpec((rows, blk), lambda j, me_ref: (0, j))
    return pl.pallas_call(
        body,
        out_shape=[jax.ShapeDtypeStruct((rows, width), bf16)] * 2,
        grid_spec=pltpu.PrefetchScalarGridSpec(
            num_scalar_prefetch=1,
            grid=(width // blk,),
            in_specs=[half(0), half(1)],
            out_specs=[plain] * 2,
        ),
        compiler_params=params(16),
        cost_estimate=cost(0, rows * width * 8),
    )(me, x, x)


def pack_targets(me, theirs, targets, cap, width, blk):
    rows = targets.shape[0]

    def body(me_ref, their_ref, mine_ref, other_ref, mine_out, other_out):
        local = iota((cap, rows), 1) + me_ref[0] * rows
        pick = one_hot(their_ref[:cap, 126:127] == local)
        mine_out[...] = dot_nn(pick, mine_ref[...]).astype(bf16)
        other_out[...] = dot_nn(pick, other_ref[...]).astype(bf16)

    def half(k):
        return pl.BlockSpec(
            (rows, blk), lambda j, me_ref: (0, (me_ref[0] ^ k) % 2 * (width // blk) + j)
        )

    plain = pl.BlockSpec((cap, blk), lambda j, me_ref: (0, j))
    return pl.pallas_call(
        body,
        out_shape=[jax.ShapeDtypeStruct((cap, width), bf16)] * 2,
        grid_spec=pltpu.PrefetchScalarGridSpec(
            num_scalar_prefetch=1,
            grid=(width // blk,),
            in_specs=[whole, half(0), half(1)],
            out_specs=[plain] * 2,
        ),
        compiler_params=params(16),
        cost_estimate=cost(2 * cap * rows * width, rows * width * 8),
    )(me, theirs, targets, targets)


def build_maps(me, points, sib_points, norms_in, q_half, q_other, inverses, slots, theirs):
    rows, feats = points.shape
    half_f = feats // 2
    total = slots.shape[1]
    blk = total // 2
    step = min(256, rows, blk)
    scale = -(2.0 / feats)

    def body(
        me_ref, own_ref, sib_ref, pn_ref, qh_ref, qo_ref, inv_ref, idr_ref, idc_ref,
        left_ref, rest_ref, rows_ref, along_ref, norm_ref,
    ):
        mine = pl.ds(pl.multiple_of(me_ref[0] % 2 * half_f, 128), half_f)
        other = pl.ds(pl.multiple_of((1 - me_ref[0] % 2) * half_f, 128), half_f)
        for r in range(0, total, step):
            part = square_sums(qh_ref[r : r + step, :]) + square_sums(qo_ref[r : r + step, :])
            norm_ref[r : r + step, :] = jnp.broadcast_to(part, (step, 128))
        norms = jnp.transpose(norm_ref[...])[0:1, :]

        def values(a, b, a_sq, b_sq, same):
            inner = dot_nt(a[0], b[0]) + dot_nt(a[1], b[1])
            sq_dist = jnp.maximum(a_sq + b_sq - 2.0 * inner, 0.0)
            k = jnp.exp(scale * sq_dist).astype(bf16).astype(f32)
            return (k + jnp.where(same, ridge_weight, 0.0)).astype(bf16)

        cross = []
        for r in range(blk, total, step):
            at = slice(r, r + step)
            cross.append(
                values(
                    (qh_ref[at, :], qo_ref[at, :]),
                    (qh_ref[:blk, :], qo_ref[:blk, :]),
                    norm_ref[at, 0:1],
                    norms[:, :blk],
                    idc_ref[at, 127:128] == idr_ref[7:8, :blk],
                )
            )
        cross = jnp.concatenate(cross, axis=0)
        inv0, inv1 = inv_ref[0], inv_ref[1]
        high0, low0 = split_bf16(inv0)
        high1, low1 = split_bf16(inv1)
        high, low = split_bf16(dot_nn(cross, high0) + dot_nn(cross, low0))
        lower = -(dot_nn(high1, high) + dot_nn(high1, low) + dot_nn(low1, high))

        bell = jnp.exp(-scale * (jnp.min(norms) - norms))

        def direction(inv, weights):
            way = jnp.sum(inv * weights, axis=1, keepdims=True)
            return way * lax.rsqrt(jnp.maximum(jnp.sum(way * way), 1e-30))

        way0 = direction(inv0, bell[:, :blk])
        way1 = direction(inv1, bell[:, blk:])
        row00 = jnp.sum(way0 * inv0, axis=0, keepdims=True)
        row10 = jnp.sum(way1 * lower, axis=0, keepdims=True)
        row11 = jnp.sum(way1 * inv1, axis=0, keepdims=True)
        rest_ref[:blk, :blk] = (inv0 - way0 * row00).astype(bf16)
        rest_ref[:blk, blk:] = jnp.zeros((blk, blk), bf16)
        rest_ref[blk:, :blk] = (lower - way1 * row10).astype(bf16)
        rest_ref[blk:, blk:] = (inv1 - way1 * row11).astype(bf16)
        rows_ref[...] = jnp.zeros((8, total), f32)
        rows_ref[0:1, :blk] = row00
        rows_ref[1:2, :blk] = row10
        rows_ref[1:2, blk:] = row11
        along_ref[...] = jnp.zeros((8, total), f32)
        along_ref[0:1, :blk] = as_row(way0)
        along_ref[1:2, blk:] = as_row(way1)

        for which, ref in enumerate((own_ref, sib_ref)):
            for r in range(0, rows, step):
                at = slice(r, r + step)
                a = (ref[at, mine], ref[at, other])
                spot = (me_ref[0] ^ which) * rows + r + iota((step, total), 0)
                left_ref[which * rows + r : which * rows + r + step, :] = -values(
                    a,
                    (qh_ref[...], qo_ref[...]),
                    pn_ref[which * rows + r : which * rows + r + step, 0:1],
                    norms,
                    spot == idr_ref[7:8, :],
                )

    return pl.pallas_call(
        body,
        out_shape=[
            jax.ShapeDtypeStruct((2 * rows, total), bf16),
            jax.ShapeDtypeStruct((total, total), bf16),
            jax.ShapeDtypeStruct((8, total), f32),
            jax.ShapeDtypeStruct((8, total), f32),
        ],
        in_specs=[pl.BlockSpec(memory_space=pltpu.SMEM)] + [whole] * 8,
        out_specs=[whole] * 4,
        scratch_shapes=[pltpu.VMEM((total, 128), f32)],
        compiler_params=params(24),
        cost_estimate=cost(4 * rows * total * feats, 12 << 20),
    )(me, points, sib_points, norms_in, q_half, q_other, inverses, slots, theirs)


def map_weights(lo, count, extra, slots, pos_row, rest, left, rows_along, cap):
    points, total = left.shape

    def fill(slots_ref, rest_ref, left_ref, along_ref, weights):
        sel = one_hot(slots_ref[pos_row : pos_row + 1, :] == lo + iota((count, total), 0))
        moved = dot_nn(sel, rest_ref[...]).astype(bf16)
        if extra:
            moved = jnp.concatenate([moved, both_parts(along_ref[...])], axis=0)
        pack = one_hot(iota((cap, total), 0) == slots_ref[0:1, :])
        for at, other in ((slice(0, points), left_ref[...]), (slice(points, points + cap), pack)):
            mapped = dot_nt(moved, other)
            weights[:count, at] = mapped[:count].astype(bf16)
            if extra:
                both = mapped[count : count + 8] + mapped[count + 8 :]
                weights[count:, at] = both_parts(both)

    if extra:
        return fill

    def body(slots_ref, rest_ref, left_ref, out_ref):
        fill(slots_ref, rest_ref, left_ref, None, out_ref)

    return pl.pallas_call(
        body,
        out_shape=jax.ShapeDtypeStruct((count, points + cap), bf16),
        in_specs=[whole] * 3,
        out_specs=whole,
        compiler_params=params(20),
        cost_estimate=cost(count * (2 * points + cap) * total, 6 << 20),
    )(slots, rest, left)


def strips_of(bands):
    return [(k, min(k + 512, end)) for at, end in bands for k in range(at, end, 512)]


def strip_of(refs, at, end):
    targets = refs[2][:, at:end] + refs[3][:, at:end]
    return jnp.concatenate([refs[0][:, at:end], refs[1][:, at:end], targets], axis=0)


def first_shares(piece, bands, slots, pos_row, rest, left, rows_along, parts):
    width, cap = parts[0].shape[1], parts[-1].shape[0]
    height, depth = piece + 16, left.shape[0] + cap
    fill = map_weights(0, piece, True, slots, pos_row, rest, left, rows_along, cap)

    def body(slots_ref, rest_ref, left_ref, along_ref, *refs):
        part_refs, refs = refs[: len(parts)], refs[len(parts) :]
        amount_ref, band_refs, weights = refs[0], refs[1:-1], refs[-1]
        fill(slots_ref, rest_ref, left_ref, along_ref, weights)
        for at, end in strips_of(bands):
            out = dot_nn(weights[...], strip_of(part_refs, at, end))
            amount_ref[:, at:end] = out[piece : piece + 8] + out[piece + 8 :]
            for band, ref in zip(bands, band_refs):
                if band[0] <= at < band[1]:
                    strip = slice(at - band[0], end - band[0])
                    ref[:piece, strip] = out[:piece].astype(bf16)
                    ref[piece:, strip] = both_parts(out[piece : piece + 8] + out[piece + 8 :])

    out_shape = [jax.ShapeDtypeStruct((8, width), f32)]
    out_shape += [jax.ShapeDtypeStruct((piece + 16, end - at), bf16) for at, end in bands]
    return pl.pallas_call(
        body,
        out_shape=out_shape,
        in_specs=[whole] * (4 + len(parts)),
        out_specs=[whole] * len(out_shape),
        scratch_shapes=[pltpu.VMEM((height, depth), bf16)],
        compiler_params=params(20),
        cost_estimate=cost(height * depth * (width + 1024), 12 << 20),
    )(slots, rest, left, rows_along, *parts)


def more_shares(me, weights, lo, count, bands, parts):
    depth, width = weights.shape[1], parts[0].shape[1]

    def body(me_ref, weights_ref, *refs):
        for at, end in strips_of(bands):
            strip = strip_of(refs, at, end)
            refs[-1][:, at:end] = dot_nn(weights_ref[lo : lo + count, :], strip)

    return pl.pallas_call(
        body,
        out_shape=jax.ShapeDtypeStruct((count, width), f32),
        in_specs=[pl.BlockSpec(memory_space=pltpu.SMEM)] + [whole] * (1 + len(parts)),
        out_specs=whole,
        compiler_params=params(16),
        cost_estimate=cost(count * depth * width, 10 << 20),
    )(me, weights, *parts)


def add_arrived(me, share, row, band, shift, arrived, carry):
    piece, length = shift.shape
    n = len(arrived)

    def body(me_ref, share_ref, shift_ref, *refs):
        out = share_ref[row : row + piece, band[0] : band[1]]
        for k, ref in enumerate(refs[:-1]):
            at = length - (n - k) * piece
            out += dot_nn(shift_ref[:, at : at + piece], ref[:piece, :])
        refs[-1][:piece, :] = out.astype(bf16)
        if carry:
            refs[-1][piece:, :] = refs[-2][piece:, :]

    height = piece + (16 if carry else 0)
    return pl.pallas_call(
        body,
        out_shape=jax.ShapeDtypeStruct((height, band[1] - band[0]), bf16),
        in_specs=[pl.BlockSpec(memory_space=pltpu.SMEM)] + [whole] * (2 + n),
        out_specs=whole,
        compiler_params=params(12),
        cost_estimate=cost(n * piece * piece * (band[1] - band[0]), 6 << 20),
    )(me, share, shift, *arrived)


def sum_amounts(me, amount, bands, arrived):
    piece = arrived[0][0].shape[0] - 16

    def body(me_ref, amount_ref, *refs):
        out_ref, refs = refs[-1], list(refs[:-1])
        for (at, end), pieces in zip(bands, arrived):
            out = amount_ref[:, at:end]
            for _ in pieces:
                both = refs.pop(0)[piece:, :].astype(f32)
                out += both[:8] + both[8:]
            out_ref[:, at:end] = out

    return pl.pallas_call(
        body,
        out_shape=jax.ShapeDtypeStruct(amount.shape, f32),
        in_specs=[pl.BlockSpec(memory_space=pltpu.SMEM)] + [whole] * (1 + sum(map(len, arrived))),
        out_specs=whole,
        compiler_params=params(12),
        cost_estimate=cost(0, 2 << 20),
    )(me, amount, *[ref for pieces in arrived for ref in pieces])


def final_maps(me, slots, along, spots, rows):
    total, n = slots.shape[1], spots.shape[1]

    def body(me_ref, slots_ref, along_ref, spots_ref, sel_ref, scale_ref):
        first = me_ref[0] * rows
        sel_ref[...] = one_hot(first + iota((rows, n), 0) == spots_ref[...])
        same = first + iota((rows, total), 0) == slots_ref[7:8, :]
        scale_ref[...] = jnp.zeros((rows, 128), f32)
        for b in range(2):
            weight = jnp.where(same, along_ref[b : b + 1, :], 0.0)
            scale_ref[:, b : b + 1] = jnp.sum(weight, axis=1, keepdims=True)

    return pl.pallas_call(
        body,
        out_shape=[jax.ShapeDtypeStruct((rows, n), bf16), jax.ShapeDtypeStruct((rows, 128), f32)],
        in_specs=[pl.BlockSpec(memory_space=pltpu.SMEM)] + [whole] * 3,
        out_specs=[whole] * 2,
        compiler_params=params(16),
        cost_estimate=cost(1 << 20, 3 << 20),
    )(me, slots, along, spots)


def strips_in(span):
    return [(k, min(k + 512, span)) for k in range(0, span, 512)]


def add_early(me, other, coeffs, sel, scale, amount, pieces, width, band):
    rows, span = coeffs.shape[0], band[1] - band[0]
    n, piece = len(pieces), pieces[0].shape[0]
    strips = strips_in(span)

    def body(me_ref, src_ref, sel_ref, scale_ref, amount_ref, *refs):
        out_ref, arrivals = refs[-2:]
        first = (me_ref[0] ^ other) % 2 * width + band[0]
        copies = []
        for i, (at, end) in enumerate(strips):
            cols = pl.ds(pl.multiple_of(first + at, 128), end - at)
            copy = pltpu.make_async_copy(src_ref.at[:, cols], out_ref.at[:, at:end], arrivals.at[i])
            copy.start()
            copies.append(copy)
        for copy, (at, end) in zip(copies, strips):
            strip = jnp.concatenate([ref[:, at:end] for ref in refs[:n]], axis=0)
            out = dot_nn(sel_ref[:, : n * piece], strip)
            for b in range(2):
                row = amount_ref[b : b + 1, band[0] + at : band[0] + end]
                out += scale_ref[:, b : b + 1] * row
            copy.wait()
            out_ref[:, at:end] += out

    return pl.pallas_call(
        body,
        out_shape=jax.ShapeDtypeStruct((rows, span), f32),
        in_specs=[
            pl.BlockSpec(memory_space=pltpu.SMEM),
            pl.BlockSpec(memory_space=pl.ANY),
            *[whole] * (3 + n),
        ],
        out_specs=whole,
        scratch_shapes=[pltpu.SemaphoreType.DMA((len(strips),))],
        compiler_params=params(12),
        cost_estimate=cost(rows * n * piece * span, rows * span * 8),
    )(me, coeffs, sel, scale, amount, *pieces)


def add_last(me, early, cols, buffer, sel, mine, sib, width, band):
    rows, span = sel.shape[0], band[1] - band[0]
    n, piece = len(mine), mine[0].shape[0]
    strips = strips_in(span)

    def body(me_ref, sel_ref, early_mine, early_sib, *refs):
        out_ref, held, departures = refs[-3:]
        chosen = sel_ref[:, sel_ref.shape[1] - n * piece :]
        copies = []
        for k, early_ref in enumerate((early_mine, early_sib)):
            first = (me_ref[0] ^ k) % 2 * width + band[0]
            for i, (at, end) in enumerate(strips):
                strip = jnp.concatenate([ref[:, at:end] for ref in refs[k * n : k * n + n]], axis=0)
                held[k, :, at:end] = early_ref[:, at:end] + dot_nn(chosen, strip)
                cut = pl.ds(pl.multiple_of(first + at, 128), end - at)
                copy = pltpu.make_async_copy(
                    held.at[k, :, at:end], out_ref.at[:, cut], departures.at[k * len(strips) + i]
                )
                copy.start()
                copies.append(copy)
        for copy in copies:
            copy.wait()

    operands = [sel, *early, *mine, *sib]
    in_specs = [pl.BlockSpec(memory_space=pltpu.SMEM)] + [whole] * len(operands)
    aliases = {}
    if buffer is not None:
        aliases = {1 + len(operands): 0}
        operands.append(buffer)
        in_specs.append(pl.BlockSpec(memory_space=pl.ANY))
    return pl.pallas_call(
        body,
        out_shape=pltpu.HBM((rows, cols), f32),
        in_specs=in_specs,
        out_specs=pl.BlockSpec(memory_space=pltpu.HBM),
        scratch_shapes=[
            pltpu.VMEM((2, rows, span), f32),
            pltpu.SemaphoreType.DMA((2 * len(strips),)),
        ],
        input_output_aliases=aliases,
        compiler_params=params(12),
        cost_estimate=cost(rows * n * piece * 2 * span, rows * 2 * span * 8),
    )(me, *operands)


def solution(mesh):
    n = mesh.shape["rows"]
    chips = n // 2
    bits = chips.bit_length() - 1
    ring = [k ^ (k >> 1) for k in range(chips)]
    place = [ring.index(k) for k in range(chips)]

    def core_perm(chip_of):
        return [(i, 2 * chip_of(i // 2, i % 2) + i % 2) for i in range(n)]

    sib_perm = [(i, i ^ 1) for i in range(n)]
    ring_perm = core_perm(
        lambda chip, core: ring[(place[chip] + (1 if core == 0 else chips - 1)) % chips]
    )

    def stage_bit(stage, core):
        return 1 << (stage if core == 0 else bits - 1 - stage)

    def to_sib(x):
        return lax.ppermute(x, "rows", sib_perm)

    def stage_cap(total, stage):
        return min(total, total // 2 + ((1 << stage) - 1) * (total // chips))

    def spread_path(points, targets, coeffs, inverses, pts_sib, me, slots, theirs, spots, shift):
        rows_here, feats = points.shape
        cols = coeffs.shape[1]
        half_f = feats // 2
        extra_cols = -cols % 256
        if extra_cols:
            targets = jnp.pad(targets, ((0, 0), (0, extra_cols)))
            coeffs = jnp.pad(coeffs, ((0, 0), (0, extra_cols)))
        width = (cols + extra_cols) // 2
        blk = 128 * max(d for d in (1, 2, 3, 4) if width // 128 % d == 0)
        total = slots.shape[1]
        piece = total // (2 * chips)
        steps = 2 * chips - 1

        blocks = width // blk
        first = (blocks + 1) // 2 * blk
        bands = [(0, first), (first, width)] if first < width else [(0, width)]

        caps = [stage_cap(total, stage) for stage in range(bits)]
        sent = pick_points(me, theirs, points, pts_sib, half_f, caps[0])
        for stage in range(bits):
            got = lax.ppermute(
                sent, "rows", core_perm(lambda k, c, s=stage: k ^ stage_bit(s, c))
            )
            if stage == 0:
                wide = 128 * max(d for d in range(1, 9) if width // 128 % d == 0)
                t_mine, t_other = pack_targets(
                    after(me, sent), theirs, targets, caps[0], width, wide
                )
                t_sib = to_sib(t_other)
                got = after(got, t_other)
            if stage < bits - 1:
                sent = append_rows(sent, got, theirs, stage, caps[stage + 1])
        c_mine, c_other = cut_columns(after(me, sent), coeffs, width, blk)
        placed = place_rows(sent, theirs, bits - 1)
        norms = point_norms(after(points, placed), pts_sib)
        block_half = place_rows(after(got, norms, c_other), theirs, bits, placed)
        block_other = to_sib(block_half)
        c_sib = to_sib(after(c_other, block_other))
        parts = [c_mine, c_sib, t_mine, t_sib]

        left, rest, rows_along, along = build_maps(
            me, points, pts_sib, norms, block_half, block_other, inverses, slots,
            theirs,
        )

        amount, *first_sent = first_shares(
            piece, bands, slots, bits, rest, left, rows_along, parts
        )
        share = {}
        arrived = [[] for _ in bands]
        final = [[] for _ in bands]
        final_sib = [[] for _ in bands]
        early_mine, early_sib = [], []
        early = steps - chips
        fillers = []
        latest = None

        def exchange(b, latest):
            for part in final[b][len(final_sib[b]) :]:
                final_sib[b].append(to_sib(after(part, latest)))

        def early_of(other, b, amounts, pieces, me_then):
            return add_early(
                me_then, other, coeffs, sel, scale, amounts, pieces[b][:early], width, bands[b]
            )

        for step in range(steps + 1):
            for b, band in enumerate(bands):
                if step == 0:
                    sent = first_sent[b]
                else:
                    arrived[b][-1] = after(arrived[b][-1], latest, *fillers)
                    fillers = []
                    sent = add_arrived(
                        me, *share[step], band, shift, arrived[b][-chips:], step < chips - 1
                    )
                latest = sent
                if step < steps:
                    arrived[b].append(lax.ppermute(sent, "rows", ring_perm))
                if step >= chips - 1:
                    final[b].append(sent)
                if step == steps - 1 and b + 1 < len(bands):
                    early_mine.append(early_of(0, b + 1, amount, final, after(me, latest)))
                    fillers.append(early_mine[-1])
                if step == steps:
                    exchange(b, latest)
            row = 2 * step + 1
            if row < 2 * chips:
                count = min(2, 2 * chips - row)
                weights = map_weights(
                    row * piece, count * piece, False, after(slots, latest), bits, rest, left,
                    None, caps[0],
                )
                more = more_shares(after(me, latest), weights, 0, count * piece, bands, parts)
                for k in range(count):
                    share[row + k] = (more, k * piece)
                fillers.append(more)
            if step == chips - 1:
                carried = [pieces[: chips - 1] for pieces in arrived]
                amount = sum_amounts(after(me, latest), amount, bands, carried)
                sel, scale = final_maps(after(me, latest), slots, along, spots, rows_here)
                fillers += [amount, scale]
            if step == steps - 2:
                early_mine.append(early_of(0, 0, amount, final, after(me, latest)))
                amount_sib = to_sib(after(amount, latest))
                fillers += [early_mine[0], amount_sib]
            if step == steps - 1:
                for b in range(len(bands)):
                    exchange(b, latest)
                for b in range(len(bands)):
                    early_sib.append(early_of(1, b, amount_sib, final_sib, me))
                fillers += early_sib

        out = None
        for b, band in enumerate(bands):
            out = add_last(
                me, (early_mine[b], early_sib[b]), cols + extra_cols, out, sel,
                final[b][early:], final_sib[b][early:], width, band,
            )
        return out[:, :cols] if extra_cols else out

    def per_device(points, targets, coeffs, block_ids, inverses):
        rows_here = points.shape[0]
        total = block_ids.size
        me = lax.axis_index("rows").astype(i32).reshape(1)
        pts_sib = to_sib(points)
        stage_bits = [[stage_bit(s, core) for s in range(bits)] for core in range(2)]
        caps = [stage_cap(total, s) for s in range(bits)]
        fits, *plans = plan(me, block_ids, rows_here, ring, stage_bits, caps)
        out = spread_path(points, targets, coeffs, inverses, pts_sib, me, *plans)

        def general(state):
            return jnp.ones_like(fits), general_path(n, points, targets, coeffs, block_ids, inverses)

        return lax.while_loop(lambda state: state[0][0] == 0, general, (fits, out))[1]

    return jax.shard_map(
        per_device,
        mesh=mesh,
        in_specs=(P("rows", None), P("rows", "labels"), P("rows", "labels"), P(), P()),
        out_specs=P("rows", "labels"),
        check_vma=False,
    )
```
